32 devices in a mesh: ctx: 8 (over y, x, core), fsdp: 4 (over z).
Axes of the slice: x: 2, y: 2, z: 4, core: 2. Of those that a mesh axis runs over, the one named last changes fastest.
Arguments:
- layer_input: bfloat16 [4, 1024, 2048], P('fsdp', 'ctx'), may hold values from -6 to 6
- pairing: int32 [4, 8], P('fsdp'), may hold values from 0 to 7, each once within a row
- query_weight: bfloat16 [2048, 2048], P(('ctx', 'fsdp')), may hold values from -0.125 to 0.125
- key_weight: bfloat16 [2048, 2048], P(('ctx', 'fsdp')), may hold values from -0.125 to 0.125
- value_weight: bfloat16 [2048, 2048], P(('ctx', 'fsdp')), may hold values from -0.125 to 0.125
- merge_weight: bfloat16 [2048, 2048], P(('ctx', 'fsdp')), may hold values from -3 to 3
- gate_weight: bfloat16 [2048, 8192], P(('ctx', 'fsdp')), may hold values from -0.125 to 0.125
- up_weight: bfloat16 [2048, 8192], P(('ctx', 'fsdp')), may hold values from -0.125 to 0.125
- down_weight: bfloat16 [8192, 2048], P(('ctx', 'fsdp')), may hold values from -0.0625 to 0.0625
- norm_first: bfloat16 [2048], P(('ctx', 'fsdp')), may hold values from 0.5 to 1.5
- norm_second: bfloat16 [2048], P(('ctx', 'fsdp')), may hold values from 0.5 to 1.5
- output_cotangent: bfloat16 [4, 1024, 2048], P('fsdp', 'ctx'), may hold values from -6 to 6
Outputs:
- layer_output: bfloat16 [4, 1024, 2048], P('fsdp', 'ctx')
- input_grad: bfloat16 [4, 1024, 2048], P('fsdp', 'ctx')
- query_grad: float32 [2048, 2048], P(('ctx', 'fsdp'))
- key_grad: float32 [2048, 2048], P(('ctx', 'fsdp'))
- value_grad: float32 [2048, 2048], P(('ctx', 'fsdp'))
- merge_grad: float32 [2048, 2048], P(('ctx', 'fsdp'))
- gate_grad: float32 [2048, 8192], P(('ctx', 'fsdp'))
- up_grad: float32 [2048, 8192], P(('ctx', 'fsdp'))
- down_grad: float32 [8192, 2048], P(('ctx', 'fsdp'))
- first_grad: float32 [2048], P(('ctx', 'fsdp'))
- second_grad: float32 [2048], P(('ctx', 'fsdp'))
The draws below stay inside these ranges and needn't reach their ends.
Inputs may be any that keep to these rules, and one draw needn't show every extreme that they name: Each row is a permutation of the ctx indices: index c holds causal blocks pairing[s, c] and 15 - pairing[s, c] of sequence s, each of 64 tokens.
All inputs are finite; a program needn't handle non-finite values.
Results may differ from the reference program's by a relative error of at most 0.018.
Values may be sent and summed in bfloat16 or wider, within the bound.
No kernel may reach another device: no remote copies, remote signals or barrier semaphores. Data moves between devices by JAX's collectives and lax.ppermute only.
A program may use at most 320 MiB of HBM per device.

```python
import jax
import jax.numpy as jnp
from jax import lax

D = 2048
HEADS = 32
HEAD_DIM = 64
FF = 8192
BLK = 64
SEQS = 4
LEN = 1024
N_CTX = 8


def level_of(stream_key, extent, pieces, low, high):
    def one(axis_at, parts):
        draws = jax.random.uniform(jax.random.fold_in(jax.random.fold_in(stream_key, 6), axis_at), (parts,), jnp.float32, low / len(pieces), high / len(pieces))
        return jnp.repeat(jnp.exp(draws), extent[axis_at] // parts).reshape((-1,) + (1,) * (len(extent) - axis_at - 1))

    factor_of = one(*pieces[0])
    for cut in pieces[1:]:
        factor_of = factor_of * one(*cut)
    return factor_of


def normal_values(key, dims, deviation, reach, cuts=(), kind=jnp.bfloat16):
    values = jax.random.normal(key, dims, jnp.float32) * deviation
    if len(cuts) > 0:
        values = level_of(key, dims, cuts, -0.22, 0.18) * values
    return jnp.clip(values, min=-reach, max=reach).astype(kind)


def setup_inputs(seed: int = 0) -> dict:
    keys = jax.random.split(jax.random.key(seed), 13)
    return {
        "layer_input": normal_values(keys[0], (SEQS, LEN, D), 1.0, 6.0, ((0, 4), (1, 8))),
        "pairing": jax.vmap(lambda own: jax.random.permutation(own, N_CTX))(jax.random.split(keys[1], SEQS)).reshape((SEQS, N_CTX)).astype(jnp.int32),
        "query_weight": normal_values(keys[2], (D, D), D ** -0.5, 0.125, ((0, 32),)),
        "key_weight": normal_values(keys[3], (D, D), D ** -0.5, 0.125, ((0, 32),)),
        "value_weight": normal_values(keys[4], (D, D), D ** -0.5, 0.125, ((0, 32),)),
        "merge_weight": normal_values(keys[5], (D, D), (max(D // (N_CTX * BLK), 1)) ** -0.5, 3.0, ((0, 32),)),
        "gate_weight": normal_values(keys[6], (D, FF), D ** -0.5, 0.125, ((0, 32),)),
        "up_weight": normal_values(keys[7], (D, FF), D ** -0.5, 0.125, ((0, 32),)),
        "down_weight": normal_values(keys[8], (FF, D), FF ** -0.5, 0.0625, ((0, 32),)),
        "norm_first": jnp.clip(1.0 + 0.1 * jax.random.normal(keys[9], (D,), jnp.float32), 0.5, 1.5).astype(jnp.bfloat16),
        "norm_second": jnp.clip(1.0 + 0.1 * jax.random.normal(keys[10], (D,), jnp.float32), 0.5, 1.5).astype(jnp.bfloat16),
        "output_cotangent": normal_values(keys[11], (SEQS, LEN, D), 1.0, 6.0, ((0, 4), (1, 8))),
    }


@jax.custom_vjp
def low(v):
    return lax.optimization_barrier(v.astype(jnp.bfloat16)).astype(jnp.float32)

@jax.custom_vjp
def low_back(v):
    return v

def low_keep(v):
    return (low(v), None)

def low_pass(kept, grad):
    return (grad,)

def back_keep(v):
    return (v, None)

def back_low(kept, grad):
    return (low(grad),)
low.defvjp(low_keep, low_pass)
low_back.defvjp(back_keep, back_low)
THETA = 130000.0
EPS = 1e-05

def matmul(left, right):
    return jnp.dot(left, right, precision=lax.Precision.HIGHEST, preferred_element_type=jnp.float32)

def block_positions(pair_cols, length_block, n_ctx):
    lower = pair_cols * length_block
    upper = (2 * n_ctx - 1 - pair_cols) * length_block
    starts = jnp.stack([lower, upper], axis=-1)
    offsets = jnp.arange(length_block, dtype=jnp.int32)
    return (starts[..., None] + offsets).reshape(pair_cols.shape[0], -1).astype(jnp.int32)

def rotary(values, position, sign):
    shape = values.shape
    heads_view = values.reshape(shape[:-1] + (shape[-1] // HEAD_DIM, HEAD_DIM))
    half = HEAD_DIM // 2
    freq = THETA ** (-2.0 * jnp.arange(half, dtype=jnp.float32) / HEAD_DIM)
    angle = position[..., None].astype(jnp.float32) * freq
    cosine = jnp.cos(angle)[..., None, :]
    sine = sign * jnp.sin(angle)[..., None, :]
    first = heads_view[..., :half]
    second = heads_view[..., half:]
    turned = jnp.concatenate([first * cosine - second * sine, second * cosine + first * sine], axis=-1)
    return turned.reshape(shape)

def rms_norm(values, gain):
    return values * lax.rsqrt(lax.optimization_barrier(jnp.mean(values * values, axis=-1, keepdims=True)) + EPS) * gain

def attend_head(position, scale):

    def attend(operands):
        query, key, value = operands
        scores = low_back(matmul(query, key.T) * scale)
        visible = position[None, :] <= position[:, None]
        scores = jnp.where(visible, scores, -1e+30)
        peak = lax.optimization_barrier(jnp.max(scores, axis=-1, keepdims=True))
        weights = jnp.exp(scores - peak)
        probs = weights / lax.optimization_barrier(jnp.sum(weights, axis=-1, keepdims=True))
        return matmul(low(probs), value)
    return jax.checkpoint(attend)

def split_heads(values):
    return values.reshape(values.shape[0], HEADS, HEAD_DIM).transpose(1, 0, 2)

def sequence_layer(weights, operands):
    query_weight, key_weight, value_weight, merge_weight, gate_weight, up_weight, down_weight, norm_first, norm_second = weights
    tokens, position = operands
    scale = HEAD_DIM ** (-0.5)
    normed = low(rms_norm(tokens, norm_first))
    queries = low_back(low(rotary(low_back(matmul(normed, query_weight)), position, 1.0)))
    keys_rot = low_back(low(rotary(low_back(matmul(normed, key_weight)), position, 1.0)))
    values = low_back(low(matmul(normed, value_weight)))
    attended = lax.map(attend_head(position, scale), (split_heads(queries), split_heads(keys_rot), split_heads(values)))
    attended = low_back(low(attended.transpose(1, 0, 2).reshape(tokens.shape)))
    mixed = tokens + low_back(matmul(attended, merge_weight))
    normed_two = low(rms_norm(mixed, norm_second))
    gate = low_back(matmul(normed_two, gate_weight))
    up = low_back(matmul(normed_two, up_weight))
    hidden = low(jax.nn.silu(gate) * up)
    return mixed + matmul(hidden, down_weight)

def reference(layer_input, pairing, query_weight, key_weight, value_weight, merge_weight, gate_weight, up_weight, down_weight, norm_first, norm_second, output_cotangent):
    position = block_positions(pairing, BLK, N_CTX)
    weights = tuple((w.astype(jnp.float32) for w in (query_weight, key_weight, value_weight, merge_weight, gate_weight, up_weight, down_weight, norm_first, norm_second)))
    tokens = layer_input.astype(jnp.float32)
    layer_step = jax.checkpoint(sequence_layer)

    def forward(tokens, *weights):
        return lax.map(lambda operands: layer_step(weights, operands), (tokens, position))
    result, pull = jax.vjp(forward, tokens, *weights)
    grads = pull(output_cotangent.astype(jnp.float32))
    return (result.astype(jnp.bfloat16), grads[0].astype(jnp.bfloat16), grads[1], grads[2], grads[3], grads[4], grads[5], grads[6], grads[7], grads[8], grads[9])
```

```python
import functools

import jax
import jax.numpy as jnp
from jax import lax
from jax.experimental import pallas as pl
from jax.experimental.pallas import tpu as pltpu
from jax.sharding import Mesh, PartitionSpec as P

HEAD_DIM = 64
THETA = 130000.0
EPS = 1e-05
SCALE = HEAD_DIM**-0.5
NEG = -1e30
BF = jnp.bfloat16
F32 = jnp.float32
CTX = ("plane", "core")
TOK = ("core", "fsdp")
VMEM_LIMIT = 56 * 1024 * 1024


def mm(left, right):
    return jnp.dot(left, right, preferred_element_type=F32)


def mm_t(left, right):
    return lax.dot_general(left, right, (((1,), (1,)), ((), ())), preferred_element_type=F32)


def t_mm(left, right):
    return lax.dot_general(left, right, (((0,), (0,)), ((), ())), preferred_element_type=F32)


def rope_tables(length, cols):
    half = HEAD_DIM // 2
    freq = THETA ** (-2.0 * jnp.arange(half, dtype=F32) / HEAD_DIM)
    angle = jnp.arange(length, dtype=jnp.int32).astype(F32)[:, None] * freq
    cosine, sine = jnp.cos(angle), jnp.sin(angle)
    heads = cols // HEAD_DIM
    return (
        jnp.tile(jnp.concatenate([cosine, cosine], axis=1), (1, heads)),
        jnp.tile(jnp.concatenate([-sine, sine], axis=1), (1, heads)),
    )


def swap_halves(values):
    cols = values.shape[1]
    half = HEAD_DIM // 2
    lane = lax.broadcasted_iota(jnp.int32, values.shape, 1)
    up = pltpu.roll(values, half, 1)
    down = pltpu.roll(values, cols - half, 1)
    return jnp.where(lane % HEAD_DIM < half, down, up)


def slot_block(pair_ref, slot, n_ctx):
    low = pair_ref[0, slot // 2]
    return low if slot % 2 == 0 else 2 * n_ctx - 1 - low


def head_mask(shape, head):
    lane = lax.broadcasted_iota(jnp.int32, shape, 1)
    return lane // HEAD_DIM == head


def forward_kernel(n_ctx, qblk, pair_ref, qkv_ref, cos_ref, sin_ref, q_ref, k_ref, v_ref, o_ref, acc_ref):
    length, cols = q_ref.shape
    blk = length // (2 * n_ctx)
    heads = cols // HEAD_DIM
    for slot in range(2 * n_ctx):
        at = pl.multiple_of(slot_block(pair_ref, slot, n_ctx) * blk, blk)
        rows = pl.ds(slot * blk, blk)
        to = pl.ds(at, blk)
        cosine, sine = cos_ref[to, :], sin_ref[to, :]
        query = qkv_ref[rows, :cols]
        key = qkv_ref[rows, cols : 2 * cols]
        q_ref[to, :] = (query * cosine + swap_halves(query) * sine).astype(BF)
        k_ref[to, :] = (key * cosine + swap_halves(key) * sine).astype(BF)
        v_ref[to, :] = qkv_ref[rows, 2 * cols :].astype(BF)
    acc_ref[...] = jnp.zeros_like(acc_ref)

    def one_head(head, carry):
        for i in range(length // qblk):
            have = (i + 1) * qblk
            rows = pl.ds(i * qblk, qblk)
            mask = head_mask((qblk, cols), head)
            query = jnp.where(mask, q_ref[rows, :], jnp.zeros((), BF))
            scores = mm_t(query, k_ref[:have, :]) * SCALE
            row = lax.broadcasted_iota(jnp.int32, scores.shape, 0) + i * qblk
            col = lax.broadcasted_iota(jnp.int32, scores.shape, 1)
            scores = jnp.where(col <= row, scores, NEG)
            peak = jnp.max(scores, axis=1, keepdims=True)
            weights = jnp.exp(scores - peak)
            total = jnp.sum(weights, axis=1, keepdims=True)
            probs = (weights * (1.0 / total)).astype(BF)
            out = mm(probs, v_ref[:have, :])
            acc_ref[rows, :] = jnp.where(mask, out, acc_ref[rows, :])
        return carry

    lax.fori_loop(0, heads, one_head, 0)
    for slot in range(2 * n_ctx):
        at = pl.multiple_of(slot_block(pair_ref, slot, n_ctx) * blk, blk)
        o_ref[pl.ds(slot * blk, blk), :] = acc_ref[pl.ds(at, blk), :].astype(BF)


def attention_forward(pair, qkv, cosine, sine, n_ctx):
    length, cols = cosine.shape
    vm = pl.BlockSpec(memory_space=pltpu.VMEM)
    return pl.pallas_call(
        functools.partial(forward_kernel, n_ctx, 256),
        out_shape=[jax.ShapeDtypeStruct((length, cols), BF)] * 4,
        in_specs=[pl.BlockSpec(memory_space=pltpu.SMEM), vm, vm, vm],
        out_specs=[vm] * 4,
        scratch_shapes=[pltpu.VMEM((length, cols), F32)],
        compiler_params=pltpu.CompilerParams(vmem_limit_bytes=VMEM_LIMIT),
        name="attention_forward",
    )(pair, qkv, cosine, sine)


def backward_kernel(
    n_ctx, qblk, pair_ref, q_ref, k_ref, v_ref, do_ref, r_ref, cos_ref, sin_ref,
    g_ref, gr_ref, go_ref, dq_ref, dk_ref, dv_ref,
):
    length, cols = q_ref.shape
    blk = length // (2 * n_ctx)
    heads = cols // HEAD_DIM
    for slot in range(2 * n_ctx):
        at = pl.multiple_of(slot_block(pair_ref, slot, n_ctx) * blk, blk)
        go_ref[pl.ds(at, blk), :] = do_ref[pl.ds(slot * blk, blk), :]
    dq_ref[...] = jnp.zeros_like(dq_ref)
    dk_ref[...] = jnp.zeros_like(dk_ref)
    dv_ref[...] = jnp.zeros_like(dv_ref)

    def one_head(head, carry):
        for i in range(length // qblk):
            have = (i + 1) * qblk
            rows = pl.ds(i * qblk, qblk)
            mask = head_mask((qblk, cols), head)
            query = jnp.where(mask, q_ref[rows, :], jnp.zeros((), BF))
            grad = jnp.where(mask, go_ref[rows, :], jnp.zeros((), BF))
            scores = mm_t(k_ref[:have, :], query) * SCALE
            key_at = lax.broadcasted_iota(jnp.int32, scores.shape, 0)
            query_at = lax.broadcasted_iota(jnp.int32, scores.shape, 1) + i * qblk
            scores = jnp.where(key_at <= query_at, scores, NEG)
            peak = jnp.max(scores, axis=0, keepdims=True)
            weights = jnp.exp(scores - peak)
            total = jnp.sum(weights, axis=0, keepdims=True)
            probs = weights * (1.0 / total)
            grad_probs = mm_t(v_ref[:have, :], grad)
            centre = jnp.sum(probs * grad_probs, axis=0, keepdims=True)
            grad_scores = (probs * (grad_probs - centre)).astype(BF)
            dk_ref[:have, :] += mm(grad_scores, query)
            dv_ref[:have, :] += mm(probs.astype(BF), grad)
            out = t_mm(grad_scores, k_ref[:have, :])
            dq_ref[rows, :] = jnp.where(mask, out, dq_ref[rows, :])
        return carry

    lax.fori_loop(0, heads, one_head, 0)
    for slot in range(2 * n_ctx):
        at = pl.multiple_of(slot_block(pair_ref, slot, n_ctx) * blk, blk)
        rows = pl.ds(slot * blk, blk)
        to = pl.ds(at, blk)
        cosine, sine = cos_ref[to, :], sin_ref[to, :]
        scale = r_ref[rows, :]
        query = (dq_ref[to, :] * SCALE).astype(BF).astype(F32)
        key = (dk_ref[to, :] * SCALE).astype(BF).astype(F32)
        value = dv_ref[to, :].astype(BF).astype(F32)
        query = query * cosine - swap_halves(query) * sine
        key = key * cosine - swap_halves(key) * sine
        for at_col, part in enumerate((query, key, value)):
            span = pl.ds(at_col * cols, cols)
            g_ref[rows, span] = part.astype(BF)
            gr_ref[rows, span] = (part * scale).astype(BF)


def attention_backward(pair, q, k, v, grad, scale, cosine, sine, n_ctx):
    length, cols = cosine.shape
    vm = pl.BlockSpec(memory_space=pltpu.VMEM)
    return pl.pallas_call(
        functools.partial(backward_kernel, n_ctx, 256),
        out_shape=[jax.ShapeDtypeStruct((length, 3 * cols), BF)] * 2,
        in_specs=[pl.BlockSpec(memory_space=pltpu.SMEM)] + [vm] * 7,
        out_specs=[vm] * 2,
        scratch_shapes=[pltpu.VMEM((length, cols), BF)] + [pltpu.VMEM((length, cols), F32)] * 3,
        compiler_params=pltpu.CompilerParams(vmem_limit_bytes=VMEM_LIMIT),
        name="attention_backward",
    )(pair, q, k, v, grad, scale, cosine, sine)


def gather(value, axes, axis=0):
    return lax.all_gather(value, axes, axis=axis, tiled=True)


def scatter(value, axes):
    return lax.psum_scatter(value, axes, scatter_dimension=0, tiled=True)


def exchange(value, axes):
    return lax.all_to_all(value, axes, split_axis=0, concat_axis=0, tiled=True)


def on_device(
    layer_input, pairing, query_weight, key_weight, value_weight, merge_weight,
    gate_weight, up_weight, down_weight, norm_first, norm_second, output_cotangent,
):
    n_plane = lax.axis_size("plane")
    n_core = lax.axis_size("core")
    n_fsdp = lax.axis_size("fsdp")
    n_ctx = n_plane * n_core
    n_tok = n_core * n_fsdp
    _, rows, width = layer_input.shape
    length = rows * n_ctx
    cols = width // n_ctx
    dev_rows = gate_weight.shape[0]
    hidden_total = gate_weight.shape[1]
    piece = hidden_total // (n_ctx * n_fsdp)
    hid = piece * n_plane
    tokens = layer_input.reshape(rows, width)
    cotangent = output_cotangent.reshape(rows, width)
    gain_first = norm_first.astype(F32)[:, None]
    gain_second = norm_second.astype(F32)[:, None]

    own = jnp.stack(
        [(w.astype(F32) * gain_first).astype(BF).reshape(dev_rows, n_ctx, cols) for w in (query_weight, key_weight, value_weight)],
        axis=2,
    )
    own = own.transpose(1, 0, 2, 3).reshape(n_ctx, dev_rows, 3 * cols)
    own = exchange(own, CTX)
    qkv_weight = gather(own[:, None], "fsdp", axis=1).reshape(width, 3 * cols)
    merge_rows = gather(merge_weight, "fsdp")
    x_all = gather(tokens, CTX)

    both = jnp.stack(
        [(w.astype(F32) * gain_second).astype(BF).reshape(dev_rows, n_plane, n_tok, piece) for w in (gate_weight, up_weight)],
        axis=1,
    )
    both = both.transpose(3, 0, 1, 2, 4).reshape(n_tok, dev_rows, 2 * hid)
    both = exchange(both, TOK).reshape(n_tok * dev_rows, 2 * hid)
    gate_up = gather(both, "plane")
    down_rows = gather(down_weight, "plane")
    cot_all = gather(cotangent, TOK)

    x_f = x_all.astype(F32)
    scale_all = lax.rsqrt(jnp.mean(x_f * x_f, axis=-1, keepdims=True) + EPS)
    qkv = mm(x_all, qkv_weight) * scale_all
    cosine, sine = rope_tables(length, cols)
    q, k, v, attended = attention_forward(pairing, qkv, cosine, sine, n_ctx)
    own_f = tokens.astype(F32)
    mixed = own_f + scatter(mm(attended, merge_rows).astype(BF), CTX).astype(F32)

    scale_second = lax.rsqrt(jnp.mean(mixed * mixed, axis=-1, keepdims=True) + EPS)
    unit_second = mixed * scale_second
    normed_all = gather(unit_second.astype(BF), TOK)
    gu = mm(normed_all, gate_up)
    gate, up = gu[:, :hid], gu[:, hid:]
    sig = jax.nn.sigmoid(gate)
    active = gate * sig
    hidden = (active * up).astype(BF)
    branch = scatter(mm(hidden, down_rows).astype(BF), TOK).astype(F32)
    layer_output = (mixed + branch).astype(BF)
    grad_hidden = mm_t(cot_all, down_rows)
    grad_gate = (grad_hidden * up * sig * (1.0 + gate * (1.0 - sig))).astype(BF)
    grad_up = (grad_hidden * active).astype(BF)
    grad_gu = jnp.concatenate([grad_gate, grad_up], axis=1)
    e_two = scatter(mm_t(grad_gu, gate_up).astype(BF), TOK).astype(F32)
    grad_mixed = cotangent.astype(F32) + scale_second * (
        e_two - unit_second * jnp.mean(e_two * unit_second, axis=-1, keepdims=True)
    )
    branch_all = gather(grad_mixed.astype(BF), CTX)

    gu_sum = scatter(t_mm(normed_all, grad_gu).astype(BF), "plane")
    gu_sum = exchange(gu_sum.reshape(n_tok, dev_rows, 2 * hid), TOK)
    gu_sum = gu_sum.reshape(n_tok, dev_rows, 2, n_plane, piece).transpose(1, 2, 3, 0, 4)
    gu_sum = gu_sum.reshape(dev_rows, 2, hidden_total).astype(F32)
    gate_grad = gu_sum[:, 0] * gain_second
    up_grad = gu_sum[:, 1] * gain_second
    second_grad = jnp.sum(
        gu_sum[:, 0] * gate_weight.astype(F32) + gu_sum[:, 1] * up_weight.astype(F32), axis=1
    )
    down_grad = scatter(t_mm(hidden, cot_all).astype(BF), "plane").astype(F32)

    merge_grad = scatter(t_mm(attended, branch_all).astype(BF), "fsdp").astype(F32)
    grad_attended = mm_t(branch_all, merge_rows).astype(BF)
    grad_qkv, grad_scaled = attention_backward(
        pairing, q, k, v, grad_attended, scale_all, cosine, sine, n_ctx
    )
    e_one = scatter(mm_t(grad_qkv, qkv_weight).astype(BF), CTX).astype(F32)
    scale_first = lax.rsqrt(jnp.mean(own_f * own_f, axis=-1, keepdims=True) + EPS)
    unit_first = own_f * scale_first
    input_grad = (
        grad_mixed
        + scale_first * (e_one - unit_first * jnp.mean(e_one * unit_first, axis=-1, keepdims=True))
    ).astype(BF)
    sums = t_mm(x_all, grad_scaled).astype(BF).reshape(n_ctx, n_fsdp, dev_rows, 3 * cols)
    sums = scatter(sums.transpose(1, 0, 2, 3).reshape(width, 3 * cols), "fsdp")
    sums = exchange(sums.reshape(n_ctx, dev_rows, 3 * cols), CTX)
    sums = sums.reshape(n_ctx, dev_rows, 3, cols).transpose(1, 2, 0, 3)
    sums = sums.reshape(dev_rows, 3, width).astype(F32)
    first_grad = jnp.sum(
        sums[:, 0] * query_weight.astype(F32)
        + sums[:, 1] * key_weight.astype(F32)
        + sums[:, 2] * value_weight.astype(F32),
        axis=1,
    )
    return (
        layer_output.reshape(1, rows, width),
        input_grad.reshape(1, rows, width),
        sums[:, 0] * gain_first,
        sums[:, 1] * gain_first,
        sums[:, 2] * gain_first,
        merge_grad,
        gate_grad,
        up_grad,
        down_grad,
        first_grad,
        second_grad,
    )


def solution(mesh):
    n_ctx, n_fsdp = mesh.shape["ctx"], mesh.shape["fsdp"]
    inner = Mesh(mesh.devices.reshape(n_ctx // 2, 2, n_fsdp), ("plane", "core", "fsdp"))
    token = P("fsdp", CTX, None)
    weight = P(("plane", "core", "fsdp"), None)
    gain = P(("plane", "core", "fsdp"))
    return jax.shard_map(
        on_device,
        mesh=inner,
        in_specs=(token, P("fsdp", None)) + (weight,) * 7 + (gain, gain, token),
        out_specs=(token, token) + (weight,) * 7 + (gain, gain),
        check_vma=False,
    )
```

```python
import functools

import jax
import jax.numpy as jnp
from jax import lax
from jax.experimental import pallas as pl
from jax.experimental.pallas import tpu as pltpu
from jax.sharding import Mesh, PartitionSpec as P

HEAD_DIM = 64
THETA = 130000.0
EPS = 1e-05
SCALE = HEAD_DIM**-0.5
NEG = -1e30
BF = jnp.bfloat16
F32 = jnp.float32
CTX = ("plane", "core")
TOK = ("core", "fsdp")
VMEM_LIMIT = 56 * 1024 * 1024


def mm(left, right):
    return jnp.dot(left, right, preferred_element_type=F32)


def mm_t(left, right):
    return lax.dot_general(left, right, (((1,), (1,)), ((), ())), preferred_element_type=F32)


def t_mm(left, right):
    return lax.dot_general(left, right, (((0,), (0,)), ((), ())), preferred_element_type=F32)


def rope_tables(length, cols):
    half = HEAD_DIM // 2
    freq = THETA ** (-2.0 * jnp.arange(half, dtype=F32) / HEAD_DIM)
    angle = jnp.arange(length, dtype=jnp.int32).astype(F32)[:, None] * freq
    cosine, sine = jnp.cos(angle), jnp.sin(angle)
    heads = cols // HEAD_DIM
    return (
        jnp.tile(jnp.concatenate([cosine, cosine], axis=1), (1, heads)),
        jnp.tile(jnp.concatenate([-sine, sine], axis=1), (1, heads)),
    )


def swap_halves(values):
    cols = values.shape[1]
    half = HEAD_DIM // 2
    lane = lax.broadcasted_iota(jnp.int32, values.shape, 1)
    up = pltpu.roll(values, half, 1)
    down = pltpu.roll(values, cols - half, 1)
    return jnp.where(lane % HEAD_DIM < half, down, up)


def relative(n_plane):
    bits = n_plane.bit_length() - 1
    steps = [[1 << ((s + c) % bits) for s in range(bits)] for c in range(2)]
    order = []
    for masks in steps:
        found = [0]
        for mask in masks:
            found += [m ^ mask for m in found]
        order.append(found)
    return steps, order


def slot_block(pair_ref, me_ref, slot, n_ctx):
    _, order = relative(n_ctx // 2)
    at, half = slot // 2, n_ctx // 2
    plane, core = me_ref[0], me_ref[1]
    if at < half:
        holder = jnp.bitwise_xor(plane, jnp.where(core == 0, order[0][at], order[1][at])) * 2 + core
    else:
        at -= half
        holder = jnp.bitwise_xor(plane, jnp.where(core == 0, order[1][at], order[0][at])) * 2 + 1 - core
    low = pair_ref[0, holder]
    return low if slot % 2 == 0 else 2 * n_ctx - 1 - low


def head_mask(shape, head):
    lane = lax.broadcasted_iota(jnp.int32, shape, 1)
    return lane // HEAD_DIM == head


def params():
    return pltpu.CompilerParams(vmem_limit_bytes=VMEM_LIMIT)


def cost(flops, moved):
    return pl.CostEstimate(flops=int(flops), bytes_accessed=int(moved), transcendentals=0)


def in_vmem(n):
    return [pl.BlockSpec(memory_space=pltpu.VMEM)] * n


def in_smem(n):
    return [pl.BlockSpec(memory_space=pltpu.SMEM)] * n


def forward_kernel(n_ctx, qblk, pair_ref, me_ref, *refs):
    x_refs = refs[:n_ctx]
    w_ref, cos_ref, sin_ref, q_ref, k_ref, v_ref, r_ref, o_ref, acc_ref = refs[n_ctx:]
    length, cols = q_ref.shape
    blk = length // (2 * n_ctx)
    heads = cols // HEAD_DIM
    for at, x_ref in enumerate(x_refs):
        x = x_ref[...]
        x_f = x.astype(F32)
        scale = lax.rsqrt(jnp.mean(x_f * x_f, axis=1, keepdims=True) + EPS)
        r_ref[pl.ds(at * 2 * blk, 2 * blk), :] = scale
        qkv = mm(x, w_ref[...]) * scale
        for second in range(2):
            to = pl.ds(pl.multiple_of(slot_block(pair_ref, me_ref, 2 * at + second, n_ctx) * blk, blk), blk)
            cosine, sine = cos_ref[to, :], sin_ref[to, :]
            query = qkv[second * blk : (second + 1) * blk, :cols]
            key = qkv[second * blk : (second + 1) * blk, cols : 2 * cols]
            q_ref[to, :] = (query * cosine + swap_halves(query) * sine).astype(BF)
            k_ref[to, :] = (key * cosine + swap_halves(key) * sine).astype(BF)
            v_ref[to, :] = qkv[second * blk : (second + 1) * blk, 2 * cols :].astype(BF)
    acc_ref[...] = jnp.zeros_like(acc_ref)

    def one_head(head, carry):
        for i in range(length // qblk):
            have = (i + 1) * qblk
            rows = pl.ds(i * qblk, qblk)
            mask = head_mask((qblk, cols), head)
            query = jnp.where(mask, q_ref[rows, :], jnp.zeros((), BF))
            scores = mm_t(query, k_ref[:have, :]) * SCALE
            row = lax.broadcasted_iota(jnp.int32, scores.shape, 0) + i * qblk
            col = lax.broadcasted_iota(jnp.int32, scores.shape, 1)
            scores = jnp.where(col <= row, scores, NEG)
            peak = jnp.max(scores, axis=1, keepdims=True)
            weights = jnp.exp(scores - peak)
            total = jnp.sum(weights, axis=1, keepdims=True)
            probs = (weights * (1.0 / total)).astype(BF)
            out = mm(probs, v_ref[:have, :])
            acc_ref[rows, :] = jnp.where(mask, out, acc_ref[rows, :])
        return carry

    lax.fori_loop(0, heads, one_head, 0)
    for slot in range(2 * n_ctx):
        at = pl.multiple_of(slot_block(pair_ref, me_ref, slot, n_ctx) * blk, blk)
        o_ref[pl.ds(slot * blk, blk), :] = acc_ref[pl.ds(at, blk), :].astype(BF)


def attention_forward(pair, me, pieces, weight, cosine, sine):
    length, cols = cosine.shape
    width = weight.shape[0]
    n_ctx = len(pieces)
    return pl.pallas_call(
        functools.partial(forward_kernel, n_ctx, 256),
        out_shape=[jax.ShapeDtypeStruct((length, cols), BF)] * 3
        + [jax.ShapeDtypeStruct((length, 1), F32), jax.ShapeDtypeStruct((length, cols), BF)],
        in_specs=in_smem(2) + in_vmem(n_ctx + 3),
        out_specs=in_vmem(5),
        scratch_shapes=[pltpu.VMEM((length, cols), F32)],
        compiler_params=params(),
        cost_estimate=cost(6 * length * width * cols + 16 * length * length * cols, 12 * width * length),
        name="attention_forward",
    )(pair, me, *pieces, weight, cosine, sine)


def backward_kernel(n_ctx, qblk, pair_ref, me_ref, *refs):
    b_refs = refs[:n_ctx]
    (
        m_ref, q_ref, k_ref, v_ref, r_ref, cos_ref, sin_ref,
        g_ref, gr_ref, go_ref, dq_ref, dk_ref, dv_ref,
    ) = refs[n_ctx:]
    length, cols = q_ref.shape
    blk = length // (2 * n_ctx)
    heads = cols // HEAD_DIM
    for at, b_ref in enumerate(b_refs):
        grad = mm_t(b_ref[...], m_ref[...]).astype(BF)
        for second in range(2):
            to = pl.ds(pl.multiple_of(slot_block(pair_ref, me_ref, 2 * at + second, n_ctx) * blk, blk), blk)
            go_ref[to, :] = grad[second * blk : (second + 1) * blk, :]
    dq_ref[...] = jnp.zeros_like(dq_ref)
    dk_ref[...] = jnp.zeros_like(dk_ref)
    dv_ref[...] = jnp.zeros_like(dv_ref)

    def one_head(head, carry):
        for i in range(length // qblk):
            have = (i + 1) * qblk
            rows = pl.ds(i * qblk, qblk)
            mask = head_mask((qblk, cols), head)
            query = jnp.where(mask, q_ref[rows, :], jnp.zeros((), BF))
            grad = jnp.where(mask, go_ref[rows, :], jnp.zeros((), BF))
            scores = mm_t(k_ref[:have, :], query) * SCALE
            key_at = lax.broadcasted_iota(jnp.int32, scores.shape, 0)
            query_at = lax.broadcasted_iota(jnp.int32, scores.shape, 1) + i * qblk
            scores = jnp.where(key_at <= query_at, scores, NEG)
            peak = jnp.max(scores, axis=0, keepdims=True)
            weights = jnp.exp(scores - peak)
            total = jnp.sum(weights, axis=0, keepdims=True)
            probs = weights * (1.0 / total)
            grad_probs = mm_t(v_ref[:have, :], grad)
            centre = jnp.sum(probs * grad_probs, axis=0, keepdims=True)
            grad_scores = (probs * (grad_probs - centre)).astype(BF)
            dk_ref[:have, :] += mm(grad_scores, query)
            dv_ref[:have, :] += mm(probs.astype(BF), grad)
            out = t_mm(grad_scores, k_ref[:have, :])
            dq_ref[rows, :] = jnp.where(mask, out, dq_ref[rows, :])
        return carry

    lax.fori_loop(0, heads, one_head, 0)
    for slot in range(2 * n_ctx):
        at = pl.multiple_of(slot_block(pair_ref, me_ref, slot, n_ctx) * blk, blk)
        rows = pl.ds(slot * blk, blk)
        to = pl.ds(at, blk)
        cosine, sine = cos_ref[to, :], sin_ref[to, :]
        scale = r_ref[rows, :]
        query = (dq_ref[to, :] * SCALE).astype(BF).astype(F32)
        key = (dk_ref[to, :] * SCALE).astype(BF).astype(F32)
        value = dv_ref[to, :].astype(BF).astype(F32)
        query = query * cosine - swap_halves(query) * sine
        key = key * cosine - swap_halves(key) * sine
        for at_col, part in enumerate((query, key, value)):
            span = pl.ds(at_col * cols, cols)
            g_ref[rows, span] = part.astype(BF)
            gr_ref[rows, span] = (part * scale).astype(BF)


def attention_backward(pair, me, pieces, merge_rows, q, k, v, scale, cosine, sine):
    length, cols = cosine.shape
    width = merge_rows.shape[1]
    n_ctx = len(pieces)
    return pl.pallas_call(
        functools.partial(backward_kernel, n_ctx, 256),
        out_shape=[jax.ShapeDtypeStruct((length, 3 * cols), BF)] * 2,
        in_specs=in_smem(2) + in_vmem(n_ctx + 7),
        out_specs=in_vmem(2),
        scratch_shapes=[pltpu.VMEM((length, cols), BF)] + [pltpu.VMEM((length, cols), F32)] * 3,
        compiler_params=params(),
        cost_estimate=cost(2 * length * width * cols + 40 * length * length * cols, 8 * width * length),
        name="attention_backward",
    )(pair, me, *pieces, merge_rows, q, k, v, scale, cosine, sine)


def fold_heads_kernel(q_ref, k_ref, v_ref, gain_ref, out_ref):
    n_ctx, _, cols = out_ref.shape
    cols //= 3
    gain = gain_ref[...]
    for at, ref in enumerate((q_ref, k_ref, v_ref)):
        for to in range(n_ctx):
            part = ref[:, to * cols : (to + 1) * cols].astype(F32) * gain
            out_ref[to, :, at * cols : (at + 1) * cols] = part.astype(BF)


def fold_heads(weights, gain, n_ctx):
    rows, width = weights[0].shape
    return pl.pallas_call(
        fold_heads_kernel,
        out_shape=jax.ShapeDtypeStruct((n_ctx, rows, 3 * (width // n_ctx)), BF),
        in_specs=in_vmem(4),
        out_specs=pl.BlockSpec(memory_space=pltpu.VMEM),
        compiler_params=params(),
        cost_estimate=cost(3 * rows * width, 12 * rows * width),
        name="fold_heads",
    )(*weights, gain)


def unfold_heads_kernel(s_ref, q_ref, k_ref, v_ref, gain_ref, dq_ref, dk_ref, dv_ref, first_ref):
    n_ctx, rows, cols = s_ref.shape
    cols //= 3
    gain = gain_ref[...]
    total = jnp.zeros((rows, cols), F32)
    for at, (ref, out) in enumerate(((q_ref, dq_ref), (k_ref, dk_ref), (v_ref, dv_ref))):
        for to in range(n_ctx):
            span = slice(to * cols, (to + 1) * cols)
            part = s_ref[to, :, at * cols : (at + 1) * cols].astype(F32)
            total += part * ref[:, span].astype(F32)
            out[:, span] = part * gain
    first_ref[...] = jnp.sum(total, axis=1, keepdims=True)


def unfold_heads(sums, weights, gain):
    rows, width = weights[0].shape
    return pl.pallas_call(
        unfold_heads_kernel,
        out_shape=[jax.ShapeDtypeStruct((rows, width), F32)] * 3 + [jax.ShapeDtypeStruct((rows, 1), F32)],
        in_specs=in_vmem(5),
        out_specs=in_vmem(4),
        compiler_params=params(),
        cost_estimate=cost(12 * rows * width, 24 * rows * width),
        name="unfold_heads",
    )(sums, *weights, gain)


def fold_hidden_kernel(piece, w_ref, gain_ref, out_ref):
    n_core, n_fsdp, _, hid = out_ref.shape
    gain = gain_ref[...]
    for plane in range(hid // piece):
        for core in range(n_core):
            for line in range(n_fsdp):
                at = ((plane * n_core + core) * n_fsdp + line) * piece
                part = w_ref[:, at : at + piece].astype(F32) * gain
                out_ref[core, line, :, plane * piece : (plane + 1) * piece] = part.astype(BF)


def fold_hidden(weight, gain, n_plane, n_core, n_fsdp):
    rows, total = weight.shape
    piece = total // (n_plane * n_core * n_fsdp)
    if piece % 128:
        folded = (weight.astype(F32) * gain).astype(BF).reshape(rows, n_plane, n_core, n_fsdp, piece)
        return folded.transpose(2, 3, 0, 1, 4).reshape(n_core, n_fsdp, rows, n_plane * piece)
    return pl.pallas_call(
        functools.partial(fold_hidden_kernel, piece),
        out_shape=jax.ShapeDtypeStruct((n_core, n_fsdp, rows, n_plane * piece), BF),
        in_specs=in_vmem(2),
        out_specs=pl.BlockSpec(memory_space=pltpu.VMEM),
        compiler_params=params(),
        cost_estimate=cost(rows * total, 4 * rows * total),
        name="fold_hidden",
    )(weight, gain)


def unfold_hidden_kernel(piece, at_ref, *refs):
    *s_refs, w_ref, gain_ref, out_ref, second_ref = refs
    n_fsdp = len(s_refs)
    n_core, rows, hid = s_refs[0].shape
    gain = gain_ref[...]
    total = jnp.zeros((rows, piece), F32)
    for mask, ref in enumerate(s_refs):
        line = jnp.bitwise_xor(at_ref[1], mask)
        for other in range(n_core):
            core = jnp.bitwise_xor(at_ref[0], other)
            for plane in range(hid // piece):
                at = ((plane * n_core + core) * n_fsdp + line) * piece
                span = pl.ds(pl.multiple_of(at, piece), piece)
                part = ref[other, :, plane * piece : (plane + 1) * piece].astype(F32)
                total += part * w_ref[:, span].astype(F32)
                out_ref[:, span] = part * gain
    second_ref[...] = jnp.sum(total, axis=1, keepdims=True)


def unfold_hidden(pieces, weight, gain, n_plane):
    rows, total = weight.shape
    n_core, _, hid = pieces[0].shape
    n_fsdp = len(pieces)
    piece = hid // n_plane
    core, line = lax.axis_index("core"), lax.axis_index("fsdp")
    if piece % 128:
        out = jnp.zeros((rows, n_plane, n_core, n_fsdp, piece), BF)
        for mask, block in enumerate(pieces):
            for other in range(n_core):
                part = block[other].reshape(rows, n_plane, 1, 1, piece)
                out = lax.dynamic_update_slice(out, part, (0, 0, core ^ other, line ^ mask, 0))
        out = out.reshape(rows, total).astype(F32)
        return out * gain, jnp.sum(out * weight.astype(F32), axis=1, keepdims=True)
    return pl.pallas_call(
        functools.partial(unfold_hidden_kernel, piece),
        out_shape=[jax.ShapeDtypeStruct((rows, total), F32), jax.ShapeDtypeStruct((rows, 1), F32)],
        in_specs=in_smem(1) + in_vmem(n_fsdp + 2),
        out_specs=in_vmem(2),
        compiler_params=params(),
        cost_estimate=cost(4 * rows * total, 8 * rows * total),
        name="unfold_hidden",
    )(jnp.stack([core, line]).astype(jnp.int32), *pieces, weight, gain)


def place_kernel(at_ref, *refs):
    *p_refs, out_ref = refs
    for i, ref in enumerate(p_refs):
        out_ref[at_ref[i]] = ref[...]


def place(pieces, index):
    n = len(pieces)
    moved = 2 * n * pieces[0].size * pieces[0].dtype.itemsize
    return pl.pallas_call(
        place_kernel,
        out_shape=jax.ShapeDtypeStruct((n,) + pieces[0].shape, pieces[0].dtype),
        in_specs=in_smem(1) + in_vmem(n),
        out_specs=pl.BlockSpec(memory_space=pltpu.VMEM),
        compiler_params=params(),
        cost_estimate=cost(0, moved),
        name="place",
    )(jnp.stack(index).astype(jnp.int32), *pieces)


def gather(value, axes, axis=0):
    return lax.all_gather(value, axes, axis=axis, tiled=True)


def scatter(value, axes):
    return lax.psum_scatter(value, axes, scatter_dimension=0, tiled=True)


def exchange(value, axes):
    return lax.all_to_all(value, axes, split_axis=0, concat_axis=0, tiled=True)


def after(value, *earlier):
    return lax.optimization_barrier((value, earlier))[0]


def alone(value):
    return lax.optimization_barrier(value)


def core_swap(value):
    n = lax.axis_size("plane") * 2
    return lax.ppermute(value, CTX, [(i, i ^ 1) for i in range(n)])


def plane_step(value, step):
    steps, _ = relative(lax.axis_size("plane"))
    n = lax.axis_size("plane") * 2
    return lax.ppermute(value, CTX, [(i, i ^ (2 * steps[i % 2][step])) for i in range(n)])


def line_swap(value, mask):
    n = lax.axis_size("fsdp")
    return lax.ppermute(value, "fsdp", [(i, i ^ mask) for i in range(n)])


def plane_gather(value):
    pieces = [value]
    for j in range(1, lax.axis_size("plane")):
        step = j.bit_length() - 1
        pieces.append(plane_step(pieces[j - (1 << step)], step))
    return pieces


def plane_scatter(chunks):
    total = list(chunks)
    for j in reversed(range(1, len(total))):
        step = j.bit_length() - 1
        to = j - (1 << step)
        total[to] = total[to].astype(F32) + plane_step(total[j].astype(BF), step).astype(F32)
    return total[0]


def plane_index():
    _, order = relative(lax.axis_size("plane"))
    core = lax.axis_index("core")
    plane = lax.axis_index("plane")
    return [plane ^ jnp.where(core == 0, a, b) for a, b in zip(*order)]


def part(value, at, size, axis):
    return lax.dynamic_slice_in_dim(value, at * size, size, axis)


def ctx_gather(value):
    mine = plane_gather(value)
    return mine + [core_swap(piece) for piece in mine]


def ctx_scatter(theirs, mine, n_plane):
    total = (mine.astype(F32) + core_swap(theirs).astype(F32)).astype(BF)
    rows = total.shape[0] // n_plane
    return plane_scatter([total[i * rows : (i + 1) * rows] for i in range(n_plane)])


def token_scatter(left, product):
    core = lax.axis_index("core")
    rows = left.shape[0] // 2
    theirs = core_swap(alone(product(part(left, 1 - core, rows, 0)).astype(BF)))
    mine = alone(product(part(left, core, rows, 0)).astype(BF))
    return (mine.astype(F32) + theirs.astype(F32)).astype(BF)


def line_exchange(value):
    core, line = lax.axis_index("core"), lax.axis_index("fsdp")
    kept = lax.dynamic_index_in_dim(value, core, 0, keepdims=False)
    came = core_swap(lax.dynamic_index_in_dim(value, 1 - core, 0, keepdims=False))
    pieces = []
    for mask in range(lax.axis_size("fsdp")):
        to = line ^ mask
        pair = jnp.stack(
            [lax.dynamic_index_in_dim(v, to, 0, keepdims=False) for v in (kept, came)]
        )
        pieces.append(pair if mask == 0 else line_swap(pair, mask))
    return pieces


def line_rows(pieces):
    core, line = lax.axis_index("core"), lax.axis_index("fsdp")
    n_fsdp = len(pieces)
    blocks = [(piece[other], (core ^ other) * n_fsdp + (line ^ mask)) for mask, piece in enumerate(pieces) for other in range(2)]
    return place([b for b, _ in blocks], [i for _, i in blocks])


def on_device(
    layer_input, pairing, query_weight, key_weight, value_weight, merge_weight,
    gate_weight, up_weight, down_weight, norm_first, norm_second, output_cotangent,
):
    n_plane = lax.axis_size("plane")
    n_core = lax.axis_size("core")
    n_fsdp = lax.axis_size("fsdp")
    n_ctx = n_plane * n_core
    n_tok = n_core * n_fsdp
    me = jnp.stack([lax.axis_index("plane"), lax.axis_index("core")]).astype(jnp.int32)
    index = plane_index()
    _, rows, width = layer_input.shape
    length = rows * n_ctx
    half = length // 2
    cols = width // n_ctx
    dev_rows = gate_weight.shape[0]
    piece = gate_weight.shape[1] // (n_ctx * n_fsdp)
    hid = piece * n_plane
    d_rows = n_tok * dev_rows
    tokens = layer_input.reshape(rows, width)
    cotangent = output_cotangent.reshape(rows, width)
    gain_first = norm_first.astype(F32)[:, None]
    gain_second = norm_second.astype(F32)[:, None]
    projections = (query_weight, key_weight, value_weight)

    gate_moved = line_exchange(fold_hidden(gate_weight, gain_second, n_plane, n_core, n_fsdp))
    own = exchange(fold_heads(projections, gain_first, n_ctx), CTX)
    own = after(own, gate_moved)
    qkv_weight = gather(own[:, None], "fsdp", axis=1).reshape(width, 3 * cols)
    x_pieces = ctx_gather(tokens)
    gate_pieces = plane_gather(line_rows(gate_moved).reshape(d_rows, hid))
    up_own = after(fold_hidden(up_weight, gain_second, n_plane, n_core, n_fsdp), qkv_weight)
    up_moved = line_exchange(up_own)
    merge_rows = gather(after(merge_weight, qkv_weight), "fsdp")
    cot_all = gather(after(cotangent, merge_rows), TOK)
    down_pieces = plane_gather(after(down_weight, x_pieces, gate_pieces))

    cosine, sine = rope_tables(length, cols)
    x_pieces, gate_pieces = lax.optimization_barrier((x_pieces, gate_pieces))
    q, k, v, scale_all, attended = attention_forward(pairing, me, x_pieces, qkv_weight, cosine, sine)
    x_all = jnp.concatenate(x_pieces, axis=0)
    own_f = tokens.astype(F32)
    theirs = alone(mm(attended[half:], merge_rows).astype(BF))
    mine = alone(mm(attended[:half], merge_rows).astype(BF))
    mixed = own_f + ctx_scatter(theirs, mine, n_plane)
    up_pieces = plane_gather(line_rows(up_moved).reshape(d_rows, hid))

    scale_second = lax.rsqrt(jnp.mean(mixed * mixed, axis=-1, keepdims=True) + EPS)
    unit_second = mixed * scale_second
    normed = after(unit_second.astype(BF), down_pieces)
    normed_all = gather(normed, TOK)
    gate_rows = place(gate_pieces, index).reshape(width, hid)
    up_rows = place(up_pieces, index).reshape(width, hid)
    down_rows = place(down_pieces, index).reshape(hid, width)
    gate = mm(normed_all, gate_rows)
    up = mm(normed_all, up_rows)
    sig = jax.nn.sigmoid(gate)
    active = gate * sig
    hidden = (active * up).astype(BF)
    grad_hidden = mm_t(cot_all, down_rows)
    grad_gate = (grad_hidden * up * sig * (1.0 + gate * (1.0 - sig))).astype(BF)
    grad_up = (grad_hidden * active).astype(BF)
    hidden, grad_gate, grad_up = lax.optimization_barrier((hidden, grad_gate, grad_up))
    grad_gu = jnp.concatenate([grad_gate, grad_up], axis=1)
    e_two = token_scatter(
        grad_gu, lambda v: mm_t(v[:, :hid], gate_rows) + mm_t(v[:, hid:], up_rows)
    )

    hidden_w, gate_w, up_w = after((hidden, grad_gate, grad_up), e_two)
    normed_w = [part(normed_all, at, d_rows, 1) for at in index]
    down_chunks = [t_mm(part(hidden_w, at, piece, 1), cot_all).astype(BF) for at in index]
    gate_chunks = [t_mm(rows_of, gate_w).astype(BF) for rows_of in normed_w]
    up_chunks = [t_mm(rows_of, up_w).astype(BF) for rows_of in normed_w]
    branch = token_scatter(hidden_w, lambda v: mm(v, down_rows))
    down_chunks, gate_chunks, up_chunks, branch = lax.optimization_barrier(
        (down_chunks, gate_chunks, up_chunks, branch)
    )
    e_two = scatter(e_two, "fsdp")
    branch_sum = scatter(after(branch, e_two), "fsdp").astype(F32)
    layer_output = (mixed + branch_sum).astype(BF)
    gate_sum = plane_scatter(gate_chunks).astype(BF).reshape(n_core, n_fsdp, dev_rows, hid)
    gate_back = line_exchange(gate_sum)
    up_sum = plane_scatter(up_chunks).astype(BF).reshape(n_core, n_fsdp, dev_rows, hid)
    up_back = line_exchange(up_sum)
    down_grad = plane_scatter(down_chunks).astype(F32)
    gate_grad, second_gate = unfold_hidden(gate_back, gate_weight, gain_second, n_plane)
    up_grad, second_up = unfold_hidden(up_back, up_weight, gain_second, n_plane)
    second_grad = (second_gate + second_up)[:, 0]

    e_two = after(e_two, gate_chunks, up_chunks, down_chunks, branch).astype(F32)
    grad_mixed = cotangent.astype(F32) + scale_second * (
        e_two - unit_second * jnp.mean(e_two * unit_second, axis=-1, keepdims=True)
    )
    branch_pieces = ctx_gather(grad_mixed.astype(BF))
    grad_qkv, grad_scaled = attention_backward(
        pairing, me, branch_pieces, merge_rows, q, k, v, scale_all, cosine, sine
    )
    sums = t_mm(x_all, grad_scaled).astype(BF).reshape(n_ctx, n_fsdp, dev_rows, 3 * cols)
    sums = scatter(sums.transpose(1, 0, 2, 3).reshape(width, 3 * cols), "fsdp")
    branch_all = jnp.concatenate(branch_pieces, axis=0)
    merge_grad = t_mm(attended, branch_all).astype(BF)
    merge_grad = scatter(after(merge_grad, sums), "fsdp").astype(F32)
    theirs = alone(mm_t(grad_qkv[half:], qkv_weight).astype(BF))
    mine = alone(mm_t(grad_qkv[:half], qkv_weight).astype(BF))
    e_one = ctx_scatter(theirs, mine, n_plane)
    scale_first = lax.rsqrt(jnp.mean(own_f * own_f, axis=-1, keepdims=True) + EPS)
    unit_first = own_f * scale_first
    input_grad = (
        grad_mixed
        + scale_first * (e_one - unit_first * jnp.mean(e_one * unit_first, axis=-1, keepdims=True))
    ).astype(BF)
    sums = exchange(sums.reshape(n_ctx, dev_rows, 3 * cols), CTX)
    query_grad, key_grad, value_grad, first_grad = unfold_heads(sums, projections, gain_first)
    return (
        layer_output.reshape(1, rows, width),
        input_grad.reshape(1, rows, width),
        query_grad,
        key_grad,
        value_grad,
        merge_grad,
        gate_grad,
        up_grad,
        down_grad,
        first_grad[:, 0],
        second_grad,
    )


def solution(mesh):
    n_ctx, n_fsdp = mesh.shape["ctx"], mesh.shape["fsdp"]
    inner = Mesh(mesh.devices.reshape(n_ctx // 2, 2, n_fsdp), ("plane", "core", "fsdp"))
    token = P("fsdp", CTX, None)
    weight = P(("plane", "core", "fsdp"), None)
    gain = P(("plane", "core", "fsdp"))
    return jax.shard_map(
        on_device,
        mesh=inner,
        in_specs=(token, P("fsdp", None)) + (weight,) * 7 + (gain, gain, token),
        out_specs=(token, token) + (weight,) * 7 + (gain, gain),
        check_vma=False,
    )
```

```python
import functools

import jax
import jax.numpy as jnp
from jax import lax
from jax.experimental import pallas as pl
from jax.experimental.pallas import tpu as pltpu
from jax.sharding import Mesh, PartitionSpec as P

HEAD_DIM = 64
THETA = 130000.0
EPS = 1e-05
SCALE = HEAD_DIM**-0.5
NEG = -1e30
BF = jnp.bfloat16
F32 = jnp.float32
CTX = ("plane", "core")
TOK = ("core", "fsdp")
VMEM_LIMIT = 56 * 1024 * 1024
LIGHT = pl.CostEstimate(flops=1024, bytes_accessed=1024, transcendentals=0)


def mm(left, right):
    return jnp.dot(left, right, preferred_element_type=F32)


def mm_t(left, right):
    return lax.dot_general(left, right, (((1,), (1,)), ((), ())), preferred_element_type=F32)


def t_mm(left, right):
    return lax.dot_general(left, right, (((0,), (0,)), ((), ())), preferred_element_type=F32)


def rope_tables(length, cols):
    half = HEAD_DIM // 2
    freq = THETA ** (-2.0 * jnp.arange(half, dtype=F32) / HEAD_DIM)
    angle = jnp.arange(length, dtype=jnp.int32).astype(F32)[:, None] * freq
    cosine, sine = jnp.cos(angle), jnp.sin(angle)
    heads = cols // HEAD_DIM
    return (
        jnp.tile(jnp.concatenate([cosine, cosine], axis=1), (1, heads)),
        jnp.tile(jnp.concatenate([-sine, sine], axis=1), (1, heads)),
    )


def swap_halves(values):
    cols = values.shape[1]
    half = HEAD_DIM // 2
    lane = lax.broadcasted_iota(jnp.int32, values.shape, 1)
    up = pltpu.roll(values, half, 1)
    down = pltpu.roll(values, cols - half, 1)
    return jnp.where(lane % HEAD_DIM < half, down, up)


def relative(n_plane):
    bits = n_plane.bit_length() - 1
    steps = [[1 << ((s + c) % bits) for s in range(bits)] for c in range(2)]
    order = []
    for masks in steps:
        found = [0]
        for mask in masks:
            found += [m ^ mask for m in found]
        order.append(found)
    return steps, order


def slot_block(pair_ref, me_ref, slot, n_ctx):
    _, order = relative(n_ctx // 2)
    at, half = slot // 2, n_ctx // 2
    plane, core = me_ref[0], me_ref[1]
    if at < half:
        holder = jnp.bitwise_xor(plane, jnp.where(core == 0, order[0][at], order[1][at])) * 2 + core
    else:
        at -= half
        holder = jnp.bitwise_xor(plane, jnp.where(core == 0, order[1][at], order[0][at])) * 2 + 1 - core
    low = pair_ref[0, holder]
    return low if slot % 2 == 0 else 2 * n_ctx - 1 - low


def head_mask(shape, head):
    lane = lax.broadcasted_iota(jnp.int32, shape, 1)
    return lane // HEAD_DIM == head


def params():
    return pltpu.CompilerParams(vmem_limit_bytes=VMEM_LIMIT)


def in_vmem(n):
    return [pl.BlockSpec(memory_space=pltpu.VMEM)] * n


def in_smem(n):
    return [pl.BlockSpec(memory_space=pltpu.SMEM)] * n


def forward_kernel(
    n_ctx, qblk, pair_ref, me_ref, x_ref, w_ref, cos_ref, sin_ref, q_ref, k_ref, v_ref, r_ref, o_ref, lse_ref, acc_ref
):
    length, cols = q_ref.shape
    blk = length // (2 * n_ctx)
    heads = cols // HEAD_DIM
    for at in range(n_ctx):
        x = x_ref[pl.ds(at * 2 * blk, 2 * blk), :]
        x_f = x.astype(F32)
        scale = lax.rsqrt(jnp.mean(x_f * x_f, axis=1, keepdims=True) + EPS)
        r_ref[pl.ds(at * 2 * blk, 2 * blk), :] = scale
        qkv = mm(x, w_ref[...]) * scale
        for second in range(2):
            to = pl.ds(pl.multiple_of(slot_block(pair_ref, me_ref, 2 * at + second, n_ctx) * blk, blk), blk)
            cosine, sine = cos_ref[to, :], sin_ref[to, :]
            query = qkv[second * blk : (second + 1) * blk, :cols]
            key = qkv[second * blk : (second + 1) * blk, cols : 2 * cols]
            q_ref[to, :] = (query * cosine + swap_halves(query) * sine).astype(BF)
            k_ref[to, :] = (key * cosine + swap_halves(key) * sine).astype(BF)
            v_ref[to, :] = qkv[second * blk : (second + 1) * blk, 2 * cols :].astype(BF)
    acc_ref[...] = jnp.zeros_like(acc_ref)
    lse_ref[...] = jnp.zeros_like(lse_ref)

    def one_head(head, carry):
        mask = head_mask((qblk, cols), head)
        here = lax.broadcasted_iota(jnp.int32, (qblk, lse_ref.shape[1]), 1) == head
        below = lax.broadcasted_iota(jnp.int32, (qblk, qblk), 1) <= lax.broadcasted_iota(jnp.int32, (qblk, qblk), 0)
        for i in range(length // qblk):
            rows = pl.ds(i * qblk, qblk)
            query = jnp.where(mask, q_ref[rows, :], jnp.zeros((), BF))
            last = jnp.where(below, mm_t(query, k_ref[rows, :]), NEG)
            peak = jnp.max(last, axis=1, keepdims=True)
            if i:
                before = mm_t(query, k_ref[: i * qblk, :])
                peak = jnp.maximum(peak, jnp.max(before, axis=1, keepdims=True))
            shift = peak * SCALE
            last = jnp.exp(last * SCALE - shift)
            total = jnp.sum(last, axis=1, keepdims=True)
            out = mm(last.astype(BF), v_ref[rows, :])
            if i:
                before = jnp.exp(before * SCALE - shift)
                total += jnp.sum(before, axis=1, keepdims=True)
                out += mm(before.astype(BF), v_ref[: i * qblk, :])
            acc_ref[rows, :] = jnp.where(mask, out * (1.0 / total), acc_ref[rows, :])
            lse_ref[rows, :] = jnp.where(here, shift + jnp.log(total), lse_ref[rows, :])
        return carry

    lax.fori_loop(0, heads, one_head, 0)
    for slot in range(2 * n_ctx):
        at = pl.multiple_of(slot_block(pair_ref, me_ref, slot, n_ctx) * blk, blk)
        o_ref[pl.ds(slot * blk, blk), :] = acc_ref[pl.ds(at, blk), :].astype(BF)


def attention_forward(pair, me, tokens, weight, cosine, sine):
    length, cols = cosine.shape
    width = weight.shape[0]
    n_ctx = width // cols
    return pl.pallas_call(
        functools.partial(forward_kernel, n_ctx, 256),
        out_shape=[jax.ShapeDtypeStruct((length, cols), BF)] * 3
        + [
            jax.ShapeDtypeStruct((length, 1), F32),
            jax.ShapeDtypeStruct((length, cols), BF),
            jax.ShapeDtypeStruct((length, 128), F32),
        ],
        in_specs=in_smem(2) + in_vmem(4),
        out_specs=in_vmem(6),
        scratch_shapes=[pltpu.VMEM((length, cols), F32)],
        compiler_params=params(),
        cost_estimate=LIGHT,
        name="attention_forward",
    )(pair, me, tokens, weight, cosine, sine)


def backward_kernel(n_ctx, qblk, pair_ref, me_ref, *refs):
    b_refs = refs[:n_ctx]
    (
        m_ref, q_ref, k_ref, v_ref, r_ref, o_ref, lse_ref, cos_ref, sin_ref,
        g_ref, gr_ref, go_ref, dq_ref, dk_ref, dv_ref, do_ref, centre_ref,
    ) = refs[n_ctx:]
    length, cols = q_ref.shape
    blk = length // (2 * n_ctx)
    heads = cols // HEAD_DIM
    for at, b_ref in enumerate(b_refs):
        grad = mm_t(b_ref[...], m_ref[...]).astype(BF)
        for second in range(2):
            to = pl.ds(pl.multiple_of(slot_block(pair_ref, me_ref, 2 * at + second, n_ctx) * blk, blk), blk)
            go_ref[to, :] = grad[second * blk : (second + 1) * blk, :]
            do_ref[to, :] = o_ref[pl.ds((2 * at + second) * blk, blk), :]
    dq_ref[...] = jnp.zeros_like(dq_ref)
    dk_ref[...] = jnp.zeros_like(dk_ref)
    dv_ref[...] = jnp.zeros_like(dv_ref)

    pick = head_mask((8, cols), lax.broadcasted_iota(jnp.int32, (8, cols), 0)).astype(F32)
    centre_ref[...] = lax.dot_general(
        pick,
        go_ref[...].astype(F32) * do_ref[...].astype(F32),
        (((1,), (1,)), ((), ())),
        precision=lax.Precision.HIGHEST,
        preferred_element_type=F32,
    )

    def one_head(head, carry):
        mask = head_mask((qblk, cols), head)
        below = lax.broadcasted_iota(jnp.int32, (qblk, qblk), 0) <= lax.broadcasted_iota(jnp.int32, (qblk, qblk), 1)
        for i in range(length // qblk):
            rows = pl.ds(i * qblk, qblk)
            query = jnp.where(mask, q_ref[rows, :], jnp.zeros((), BF))
            grad = jnp.where(mask, go_ref[rows, :], jnp.zeros((), BF))
            lse = lse_ref[pl.ds(head, 1), rows]
            centre = centre_ref[pl.ds(head, 1), rows]
            out = None
            for at, size in ((i * qblk, qblk), (0, i * qblk)):
                if not size:
                    continue
                keys = pl.ds(at, size)
                probs = jnp.exp(mm_t(k_ref[keys, :], query) * SCALE - lse)
                if at or not i:
                    probs = jnp.where(below, probs, 0.0)
                grad_probs = mm_t(v_ref[keys, :], grad)
                grad_scores = (probs * (grad_probs - centre)).astype(BF)
                dk_ref[keys, :] += mm(grad_scores, query)
                dv_ref[keys, :] += mm(probs.astype(BF), grad)
                term = t_mm(grad_scores, k_ref[keys, :])
                out = term if out is None else out + term
            dq_ref[rows, :] = jnp.where(mask, out, dq_ref[rows, :])
        return carry

    lax.fori_loop(0, heads, one_head, 0)
    for slot in range(2 * n_ctx):
        at = pl.multiple_of(slot_block(pair_ref, me_ref, slot, n_ctx) * blk, blk)
        rows = pl.ds(slot * blk, blk)
        to = pl.ds(at, blk)
        cosine, sine = cos_ref[to, :], sin_ref[to, :]
        scale = r_ref[rows, :]
        query = (dq_ref[to, :] * SCALE).astype(BF).astype(F32)
        key = (dk_ref[to, :] * SCALE).astype(BF).astype(F32)
        value = dv_ref[to, :].astype(BF).astype(F32)
        query = query * cosine - swap_halves(query) * sine
        key = key * cosine - swap_halves(key) * sine
        for at_col, part in enumerate((query, key, value)):
            span = pl.ds(at_col * cols, cols)
            g_ref[rows, span] = part.astype(BF)
            gr_ref[rows, span] = (part * scale).astype(BF)


def attention_backward(pair, me, pieces, merge_rows, q, k, v, scale, attended, lse, cosine, sine):
    length, cols = cosine.shape
    width = merge_rows.shape[1]
    n_ctx = len(pieces)
    return pl.pallas_call(
        functools.partial(backward_kernel, n_ctx, 256),
        out_shape=[jax.ShapeDtypeStruct((length, 3 * cols), BF)] * 2,
        in_specs=in_smem(2) + in_vmem(n_ctx + 9),
        out_specs=in_vmem(2),
        scratch_shapes=[pltpu.VMEM((length, cols), BF)]
        + [pltpu.VMEM((length, cols), F32)] * 3
        + [pltpu.VMEM((length, cols), BF), pltpu.VMEM((8, length), F32)],
        compiler_params=params(),
        cost_estimate=LIGHT,
        name="attention_backward",
    )(pair, me, *pieces, merge_rows, q, k, v, scale, attended, lse, cosine, sine)


def feed_forward_kernel(
    core_ref, n_ref, c_ref, g_ref, u_ref, d_ref, h_ref, dg_ref, du_ref, theirs_ref, mine_ref
):
    rows, cot = n_ref[...], c_ref[...]
    hid, tile = g_ref.shape[1], 256
    for at in range(0, hid, tile):
        span = slice(at, at + tile)
        gate = mm(rows, g_ref[:, span])
        up = mm(rows, u_ref[:, span])
        grad = mm_t(cot, d_ref[span, :])
        sig = 1.0 / (1.0 + jnp.exp(-gate))
        active = gate * sig
        h_ref[:, span] = (active * up).astype(BF)
        dg_ref[:, span] = (grad * up * sig * (1.0 + gate * (1.0 - sig))).astype(BF)
        du_ref[:, span] = (grad * active).astype(BF)
    back = (mm_t(dg_ref[...], g_ref[...]) + mm_t(du_ref[...], u_ref[...])).astype(BF)
    first = pl.program_id(0) < pl.num_programs(0) // 2

    @pl.when(first)
    def _():
        theirs_ref[...] = back

    @pl.when(jnp.logical_not(first))
    def _():
        mine_ref[...] = back


def feed_forward(normed, cotangent, gate_w, up_w, down_w):
    count, width = normed.shape
    hid = gate_w.shape[1]
    tile = 256
    half = count // tile // 2

    def rows_of(r, core):
        return (jnp.where(r < half, (1 - core[0]) * half + r, core[0] * half + r - half), 0)

    def fixed(r, core):
        return (0, 0)

    once = pl.Buffered(1)
    return pl.pallas_call(
        feed_forward_kernel,
        grid_spec=pltpu.PrefetchScalarGridSpec(
            num_scalar_prefetch=1,
            grid=(2 * half,),
            in_specs=[
                pl.BlockSpec((tile, width), rows_of),
                pl.BlockSpec((tile, width), rows_of),
                pl.BlockSpec((width, hid), fixed, pipeline_mode=once),
                pl.BlockSpec((width, hid), fixed, pipeline_mode=once),
                pl.BlockSpec((hid, width), fixed, pipeline_mode=once),
            ],
            out_specs=[pl.BlockSpec((tile, hid), rows_of)] * 3
            + [
                pl.BlockSpec((tile, width), lambda r, core: (jnp.minimum(r, half - 1), 0)),
                pl.BlockSpec((tile, width), lambda r, core: (jnp.maximum(r - half, 0), 0)),
            ],
        ),
        out_shape=[jax.ShapeDtypeStruct((count, hid), BF)] * 3
        + [jax.ShapeDtypeStruct((count // 2, width), BF)] * 2,
        compiler_params=params(),
        cost_estimate=LIGHT,
        name="feed_forward",
    )(lax.axis_index("core").astype(jnp.int32)[None], normed, cotangent, gate_w, up_w, down_w)


def branch_kernel(core_ref, h_ref, d_ref, theirs_ref, mine_ref):
    out = mm(h_ref[...], d_ref[...]).astype(BF)
    first = pl.program_id(0) < pl.num_programs(0) // 2

    @pl.when(first)
    def _():
        theirs_ref[...] = out

    @pl.when(jnp.logical_not(first))
    def _():
        mine_ref[...] = out


def branch_rows(hidden, down_w):
    count, hid = hidden.shape
    width = down_w.shape[1]
    tile = 256
    half = count // tile // 2
    return pl.pallas_call(
        branch_kernel,
        grid_spec=pltpu.PrefetchScalarGridSpec(
            num_scalar_prefetch=1,
            grid=(2 * half,),
            in_specs=[
                pl.BlockSpec(
                    (tile, hid),
                    lambda r, core: (jnp.where(r < half, (1 - core[0]) * half + r, core[0] * half + r - half), 0),
                ),
                pl.BlockSpec((hid, width), lambda r, core: (0, 0), pipeline_mode=pl.Buffered(1)),
            ],
            out_specs=[
                pl.BlockSpec((tile, width), lambda r, core: (jnp.minimum(r, half - 1), 0)),
                pl.BlockSpec((tile, width), lambda r, core: (jnp.maximum(r - half, 0), 0)),
            ],
        ),
        out_shape=[jax.ShapeDtypeStruct((count // 2, width), BF)] * 2,
        compiler_params=params(),
        cost_estimate=LIGHT,
        name="branch_rows",
    )(lax.axis_index("core").astype(jnp.int32)[None], hidden, down_w)


def merge_kernel(a_ref, *refs):
    *b_refs, out_ref, all_ref = refs
    rows = b_refs[0].shape[0]
    for at, ref in enumerate(b_refs):
        all_ref[pl.ds(at * rows, rows), :] = ref[...]
    out_ref[...] = t_mm(a_ref[...], all_ref[...]).astype(BF)


def merge_term(attended, pieces):
    cols, width = attended.shape[1], pieces[0].shape[1]
    return pl.pallas_call(
        merge_kernel,
        out_shape=jax.ShapeDtypeStruct((cols, width), BF),
        in_specs=in_vmem(1 + len(pieces)),
        out_specs=pl.BlockSpec(memory_space=pltpu.VMEM),
        scratch_shapes=[pltpu.VMEM((attended.shape[0], width), BF)],
        compiler_params=params(),
        cost_estimate=LIGHT,
        name="merge_term",
    )(attended, *pieces)


def heads_term_kernel(x_ref, g_ref, out_ref):
    n_fsdp, _, rows, cols = out_ref.shape
    out_ref[...] = t_mm(x_ref[...], g_ref[...]).astype(BF).reshape(n_fsdp, 1, rows, cols)


def heads_term(tokens, grad, n_ctx, n_fsdp):
    count, width = tokens.shape
    cols = grad.shape[1]
    rows = width // (n_ctx * n_fsdp)
    if n_fsdp * rows % 128:
        out = t_mm(tokens, grad).astype(BF).reshape(n_ctx, n_fsdp, rows, cols)
        return out.transpose(1, 0, 2, 3).reshape(width, cols)
    out = pl.pallas_call(
        heads_term_kernel,
        grid=(n_ctx,),
        in_specs=[
            pl.BlockSpec((count, n_fsdp * rows), lambda c: (0, c)),
            pl.BlockSpec((count, cols), lambda c: (0, 0), pipeline_mode=pl.Buffered(1)),
        ],
        out_specs=pl.BlockSpec((n_fsdp, 1, rows, cols), lambda c: (0, c, 0, 0)),
        out_shape=jax.ShapeDtypeStruct((n_fsdp, n_ctx, rows, cols), BF),
        compiler_params=params(),
        cost_estimate=LIGHT,
        name="heads_term",
    )(tokens, grad)
    return out.reshape(width, cols)


def back_kernel(g_ref, w_ref, out_ref):
    out_ref[...] = mm_t(g_ref[...], w_ref[...]).astype(BF)


def back_rows(grad, weight, half):
    count, cols = grad.shape
    width = weight.shape[0]
    tile = 256
    steps = count // 2 // tile
    return pl.pallas_call(
        back_kernel,
        grid=(steps,),
        in_specs=[
            pl.BlockSpec((tile, cols), lambda r: (half * steps + r, 0)),
            pl.BlockSpec((width, cols), lambda r: (0, 0), pipeline_mode=pl.Buffered(1)),
        ],
        out_specs=pl.BlockSpec((tile, width), lambda r: (r, 0)),
        out_shape=jax.ShapeDtypeStruct((count // 2, width), BF),
        compiler_params=params(),
        cost_estimate=LIGHT,
        name="back_rows",
    )(grad, weight)


def fold_heads_kernel(q_ref, k_ref, v_ref, gain_ref, out_ref):
    n_ctx, _, cols = out_ref.shape
    cols //= 3
    gain = gain_ref[...]
    for at, ref in enumerate((q_ref, k_ref, v_ref)):
        for to in range(n_ctx):
            part = ref[:, to * cols : (to + 1) * cols].astype(F32) * gain
            out_ref[to, :, at * cols : (at + 1) * cols] = part.astype(BF)


def fold_heads(weights, gain, n_ctx):
    rows, width = weights[0].shape
    return pl.pallas_call(
        fold_heads_kernel,
        out_shape=jax.ShapeDtypeStruct((n_ctx, rows, 3 * (width // n_ctx)), BF),
        in_specs=in_vmem(4),
        out_specs=pl.BlockSpec(memory_space=pltpu.VMEM),
        compiler_params=params(),
        cost_estimate=LIGHT,
        name="fold_heads",
    )(*weights, gain)


def unfold_heads_kernel(s_ref, q_ref, k_ref, v_ref, gain_ref, dq_ref, dk_ref, dv_ref, first_ref):
    n_ctx, rows, cols = s_ref.shape
    cols //= 3
    gain = gain_ref[...]
    total = jnp.zeros((rows, cols), F32)
    for at, (ref, out) in enumerate(((q_ref, dq_ref), (k_ref, dk_ref), (v_ref, dv_ref))):
        for to in range(n_ctx):
            span = slice(to * cols, (to + 1) * cols)
            part = s_ref[to, :, at * cols : (at + 1) * cols].astype(F32)
            total += part * ref[:, span].astype(F32)
            out[:, span] = part * gain
    first_ref[...] = jnp.sum(total, axis=1, keepdims=True)


def unfold_heads(sums, weights, gain):
    rows, width = weights[0].shape
    return pl.pallas_call(
        unfold_heads_kernel,
        out_shape=[jax.ShapeDtypeStruct((rows, width), F32)] * 3 + [jax.ShapeDtypeStruct((rows, 1), F32)],
        in_specs=in_vmem(5),
        out_specs=in_vmem(4),
        compiler_params=params(),
        cost_estimate=LIGHT,
        name="unfold_heads",
    )(sums, *weights, gain)


def fold_hidden_kernel(piece, w_ref, gain_ref, out_ref):
    n_core, n_fsdp, _, hid = out_ref.shape
    gain = gain_ref[...]
    for plane in range(hid // piece):
        for core in range(n_core):
            for line in range(n_fsdp):
                at = ((plane * n_core + core) * n_fsdp + line) * piece
                part = w_ref[:, at : at + piece].astype(F32) * gain
                out_ref[core, line, :, plane * piece : (plane + 1) * piece] = part.astype(BF)


def fold_hidden(weight, gain, n_plane, n_core, n_fsdp):
    rows, total = weight.shape
    piece = total // (n_plane * n_core * n_fsdp)
    if piece % 128:
        folded = (weight.astype(F32) * gain).astype(BF).reshape(rows, n_plane, n_core, n_fsdp, piece)
        return folded.transpose(2, 3, 0, 1, 4).reshape(n_core, n_fsdp, rows, n_plane * piece)
    return pl.pallas_call(
        functools.partial(fold_hidden_kernel, piece),
        out_shape=jax.ShapeDtypeStruct((n_core, n_fsdp, rows, n_plane * piece), BF),
        in_specs=in_vmem(2),
        out_specs=pl.BlockSpec(memory_space=pltpu.VMEM),
        compiler_params=params(),
        cost_estimate=LIGHT,
        name="fold_hidden",
    )(weight, gain)


def unfold_hidden_kernel(piece, at_ref, *refs):
    *s_refs, w_ref, gain_ref, out_ref, second_ref = refs
    n_fsdp = len(s_refs)
    n_core, rows, hid = s_refs[0].shape
    gain = gain_ref[...]
    total = jnp.zeros((rows, piece), F32)
    for mask, ref in enumerate(s_refs):
        line = jnp.bitwise_xor(at_ref[1], mask)
        for other in range(n_core):
            core = jnp.bitwise_xor(at_ref[0], other)
            for plane in range(hid // piece):
                at = ((plane * n_core + core) * n_fsdp + line) * piece
                span = pl.ds(pl.multiple_of(at, piece), piece)
                part = ref[other, :, plane * piece : (plane + 1) * piece].astype(F32)
                total += part * w_ref[:, span].astype(F32)
                out_ref[:, span] = part * gain
    second_ref[...] = jnp.sum(total, axis=1, keepdims=True)


def unfold_hidden(pieces, weight, gain, n_plane):
    rows, total = weight.shape
    n_core, _, hid = pieces[0].shape
    n_fsdp = len(pieces)
    piece = hid // n_plane
    core, line = lax.axis_index("core"), lax.axis_index("fsdp")
    if piece % 128:
        out = jnp.zeros((rows, n_plane, n_core, n_fsdp, piece), BF)
        for mask, block in enumerate(pieces):
            for other in range(n_core):
                part = block[other].reshape(rows, n_plane, 1, 1, piece)
                out = lax.dynamic_update_slice(out, part, (0, 0, core ^ other, line ^ mask, 0))
        out = out.reshape(rows, total).astype(F32)
        return out * gain, jnp.sum(out * weight.astype(F32), axis=1, keepdims=True)
    return pl.pallas_call(
        functools.partial(unfold_hidden_kernel, piece),
        out_shape=[jax.ShapeDtypeStruct((rows, total), F32), jax.ShapeDtypeStruct((rows, 1), F32)],
        in_specs=in_smem(1) + in_vmem(n_fsdp + 2),
        out_specs=in_vmem(2),
        compiler_params=params(),
        cost_estimate=LIGHT,
        name="unfold_hidden",
    )(jnp.stack([core, line]).astype(jnp.int32), *pieces, weight, gain)


def place_kernel(at_ref, *refs):
    *p_refs, out_ref = refs
    for i, ref in enumerate(p_refs):
        out_ref[at_ref[i]] = ref[...]


def place(pieces, index):
    n = len(pieces)
    moved = 2 * n * pieces[0].size * pieces[0].dtype.itemsize
    return pl.pallas_call(
        place_kernel,
        out_shape=jax.ShapeDtypeStruct((n,) + pieces[0].shape, pieces[0].dtype),
        in_specs=in_smem(1) + in_vmem(n),
        out_specs=pl.BlockSpec(memory_space=pltpu.VMEM),
        compiler_params=params(),
        cost_estimate=LIGHT,
        name="place",
    )(jnp.stack(index).astype(jnp.int32), *pieces)


def gather(value, axes, axis=0):
    return lax.all_gather(value, axes, axis=axis, tiled=True)


def scatter(value, axes):
    return lax.psum_scatter(value, axes, scatter_dimension=0, tiled=True)


def exchange(value, axes):
    return lax.all_to_all(value, axes, split_axis=0, concat_axis=0, tiled=True)


def together(values):
    return lax.optimization_barrier(values)


def core_swap(value):
    n = lax.axis_size("plane") * 2
    return lax.ppermute(value, CTX, [(i, i ^ 1) for i in range(n)])


def plane_step(value, step):
    steps, _ = relative(lax.axis_size("plane"))
    n = lax.axis_size("plane") * 2
    return lax.ppermute(value, CTX, [(i, i ^ (2 * steps[i % 2][step])) for i in range(n)])


def line_swap(value, mask):
    n = lax.axis_size("fsdp")
    return lax.ppermute(value, "fsdp", [(i, i ^ mask) for i in range(n)])


def plane_gather_more(pieces):
    step = len(pieces).bit_length() - 1
    return pieces + [plane_step(piece, step) for piece in pieces]


def plane_gather(value):
    pieces = [value]
    while len(pieces) < lax.axis_size("plane"):
        pieces = plane_gather_more(pieces)
    return pieces


def plane_send(chunks):
    n = len(chunks) // 2
    return [plane_step(chunk, n.bit_length() - 1) for chunk in chunks[n:]]


def plane_add(chunks, came):
    return [(mine.astype(F32) + chunk.astype(F32)).astype(BF) for mine, chunk in zip(chunks, came)]


def plane_scatter(chunks):
    while len(chunks) > 1:
        chunks = plane_add(chunks, plane_send(chunks))
    return chunks[0]


def plane_index():
    _, order = relative(lax.axis_size("plane"))
    core = lax.axis_index("core")
    plane = lax.axis_index("plane")
    return [plane ^ jnp.where(core == 0, a, b) for a, b in zip(*order)]


def part(value, at, size, axis):
    return lax.dynamic_slice_in_dim(value, at * size, size, axis)


def ctx_gather(value):
    mine = plane_gather(value)
    return mine + [core_swap(piece) for piece in mine]


def ctx_scatter(theirs, mine, n_plane):
    total = (mine.astype(F32) + core_swap(theirs).astype(F32)).astype(BF)
    rows = total.shape[0] // n_plane
    return plane_scatter([total[i * rows : (i + 1) * rows] for i in range(n_plane)])


def cores_pair(value):
    core = lax.axis_index("core")
    kept = lax.dynamic_index_in_dim(value, core, 0, keepdims=False)
    return kept, core_swap(lax.dynamic_index_in_dim(value, 1 - core, 0, keepdims=False))


def lines_parts(pair):
    line = lax.axis_index("fsdp")
    return [
        jnp.stack([lax.dynamic_index_in_dim(v, line ^ mask, 0, keepdims=False) for v in pair])
        for mask in range(lax.axis_size("fsdp"))
    ]


def lines_swap(parts):
    return parts[:1] + [line_swap(parts[mask], mask) for mask in range(1, len(parts))]


def lines_pair(pair):
    return lines_swap(lines_parts(pair))


def line_rows(pieces):
    core, line = lax.axis_index("core"), lax.axis_index("fsdp")
    n_fsdp = len(pieces)
    blocks = [(piece[other], (core ^ other) * n_fsdp + (line ^ mask)) for mask, piece in enumerate(pieces) for other in range(2)]
    return place([b for b, _ in blocks], [i for _, i in blocks])


def on_device(
    layer_input, pairing, query_weight, key_weight, value_weight, merge_weight,
    gate_weight, up_weight, down_weight, norm_first, norm_second, output_cotangent,
):
    n_plane = lax.axis_size("plane")
    n_core = lax.axis_size("core")
    n_fsdp = lax.axis_size("fsdp")
    n_ctx = n_plane * n_core
    n_tok = n_core * n_fsdp
    me = jnp.stack([lax.axis_index("plane"), lax.axis_index("core")]).astype(jnp.int32)
    index = plane_index()
    _, rows, width = layer_input.shape
    length = rows * n_ctx
    half = length // 2
    cols = width // n_ctx
    dev_rows = gate_weight.shape[0]
    piece = gate_weight.shape[1] // (n_ctx * n_fsdp)
    hid = piece * n_plane
    d_rows = n_tok * dev_rows
    tokens = layer_input.reshape(rows, width)
    cotangent = output_cotangent.reshape(rows, width)
    gain_first = norm_first.astype(F32)[:, None]
    gain_second = norm_second.astype(F32)[:, None]
    projections = (query_weight, key_weight, value_weight)

    merge_rows = gather(merge_weight, "fsdp")
    gate_moved = lines_pair(cores_pair(fold_hidden(gate_weight, gain_second, n_plane, n_core, n_fsdp)))
    own = exchange(fold_heads(projections, gain_first, n_ctx), CTX)
    x_pieces = ctx_gather(tokens)
    up_pair = cores_pair(fold_hidden(up_weight, gain_second, n_plane, n_core, n_fsdp))
    cosine, sine = rope_tables(length, cols)
    own, gate_moved, x_pieces, up_pair, merge_rows = together(
        (own, gate_moved, x_pieces, up_pair, merge_rows)
    )
    qkv_weight = gather(own[:, None], "fsdp", axis=1).reshape(width, 3 * cols)
    gate_pieces = plane_gather(line_rows(gate_moved).reshape(d_rows, hid))
    down_pieces = plane_gather_more([down_weight])
    x_all = jnp.concatenate(x_pieces, axis=0)
    x_all, gate_pieces, down_pieces = together((x_all, gate_pieces, down_pieces))
    up_moved = lines_pair(up_pair)
    cot_all = gather(cotangent, TOK)

    q, k, v, scale_all, attended, lse = attention_forward(pairing, me, x_all, qkv_weight, cosine, sine)
    while len(down_pieces) < n_plane:
        down_pieces = plane_gather_more(down_pieces)
    attended, down_pieces = together((attended, down_pieces))
    gate_rows = place(gate_pieces, index).reshape(width, hid)
    down_rows = place(down_pieces, index).reshape(hid, width)
    own_f = tokens.astype(F32)
    theirs = together(mm(attended[half:], merge_rows).astype(BF))
    mine = together(mm(attended[:half], merge_rows).astype(BF))
    mixed = own_f + ctx_scatter(theirs, mine, n_plane)
    mixed, up_moved = together((mixed, up_moved))
    up_pieces = plane_gather(line_rows(up_moved).reshape(d_rows, hid))

    scale_second = lax.rsqrt(jnp.mean(mixed * mixed, axis=-1, keepdims=True) + EPS)
    unit_second = mixed * scale_second
    normed_all = gather(unit_second.astype(BF), TOK)
    up_rows = place(up_pieces, index).reshape(width, hid)
    hidden, grad_gate, grad_up, theirs, mine = feed_forward(
        normed_all, cot_all, gate_rows, up_rows, down_rows
    )
    lse_rows = lse[:, :8].T
    e_two = (mine.astype(F32) + core_swap(theirs).astype(F32)).astype(BF)

    normed_w = [part(normed_all, at, d_rows, 1) for at in index]
    gate_late = [together(t_mm(rows_of, grad_gate).astype(BF)) for rows_of in normed_w[n_plane // 2 :]]
    hidden, grad_gate, grad_up, e_two = together((hidden, grad_gate, grad_up, e_two))
    gate_chunks = [together(t_mm(rows_of, grad_gate).astype(BF)) for rows_of in normed_w[: n_plane // 2]]
    gate_chunks += gate_late
    gate_came = plane_send(gate_chunks)
    up_chunks = [together(t_mm(rows_of, grad_up).astype(BF)) for rows_of in normed_w]
    theirs, mine = branch_rows(hidden, down_rows)
    gate_chunks, gate_came, up_chunks, theirs, mine, lse_rows = together(
        (gate_chunks, gate_came, up_chunks, theirs, mine, lse_rows)
    )
    gate_sum = plane_scatter(plane_add(gate_chunks, gate_came))
    branch = (mine.astype(F32) + core_swap(theirs).astype(F32)).astype(BF)
    e_two = scatter(e_two, "fsdp")
    e_two, gate_sum, up_chunks, branch = together((e_two, gate_sum, up_chunks, branch))
    branch_sum = scatter(branch, "fsdp")
    gate_parts = lines_parts(cores_pair(gate_sum.reshape(n_core, n_fsdp, dev_rows, hid)))
    e_two_f = e_two.astype(F32)
    grad_mixed = cotangent.astype(F32) + scale_second * (
        e_two_f - unit_second * jnp.mean(e_two_f * unit_second, axis=-1, keepdims=True)
    )
    branch_pieces = ctx_gather(grad_mixed.astype(BF))
    gate_back = lines_swap(gate_parts)

    branch_pieces, up_chunks = together((branch_pieces, up_chunks))
    up_came = plane_send(up_chunks)
    grad_qkv, grad_scaled = attention_backward(
        pairing, me, branch_pieces, merge_rows, q, k, v, scale_all, attended, lse_rows, cosine, sine
    )
    sums = heads_term(x_all, grad_scaled, n_ctx, n_fsdp)
    grad_qkv, up_chunks, up_came, gate_back, sums, attended, branch_sum = together(
        (grad_qkv, up_chunks, up_came, gate_back, sums, attended, branch_sum)
    )
    sums = scatter(sums, "fsdp")
    up_sum = plane_scatter(plane_add(up_chunks, up_came))
    attended, up_sum = together((attended, up_sum))
    merge_grad = scatter(merge_term(attended, branch_pieces), "fsdp")
    layer_output = (mixed + branch_sum.astype(F32)).astype(BF)
    theirs = back_rows(grad_qkv, qkv_weight, 1)
    mine = back_rows(grad_qkv, qkv_weight, 0)
    e_one = ctx_scatter(theirs, mine, n_plane)
    up_parts = lines_parts(cores_pair(up_sum.reshape(n_core, n_fsdp, dev_rows, hid)))
    hidden, mine = together((hidden, mine))
    down_chunks = [together(t_mm(part(hidden, at, piece, 1), cot_all).astype(BF)) for at in index]
    e_one, down_chunks = together((e_one, down_chunks))
    down_came = plane_send(down_chunks)
    sums, up_parts = together((sums, up_parts))
    up_back = lines_swap(up_parts)
    sums = exchange(sums.reshape(n_ctx, dev_rows, 3 * cols), CTX)
    sums, up_back, merge_grad = together((sums, up_back, merge_grad))
    scale_first = lax.rsqrt(jnp.mean(own_f * own_f, axis=-1, keepdims=True) + EPS)
    unit_first = own_f * scale_first
    input_grad = (
        grad_mixed
        + scale_first * (e_one - unit_first * jnp.mean(e_one * unit_first, axis=-1, keepdims=True))
    ).astype(BF)
    down_grad = plane_scatter(plane_add(down_chunks, down_came)).astype(F32)
    gate_grad, second_gate = unfold_hidden(gate_back, gate_weight, gain_second, n_plane)
    up_grad, second_up = unfold_hidden(up_back, up_weight, gain_second, n_plane)
    second_grad = (second_gate + second_up)[:, 0]
    query_grad, key_grad, value_grad, first_grad = unfold_heads(sums, projections, gain_first)
    return (
        layer_output.reshape(1, rows, width),
        input_grad.reshape(1, rows, width),
        query_grad,
        key_grad,
        value_grad,
        merge_grad.astype(F32),
        gate_grad,
        up_grad,
        down_grad,
        first_grad[:, 0],
        second_grad,
    )


def solution(mesh):
    n_ctx, n_fsdp = mesh.shape["ctx"], mesh.shape["fsdp"]
    inner = Mesh(mesh.devices.reshape(n_ctx // 2, 2, n_fsdp), ("plane", "core", "fsdp"))
    token = P("fsdp", CTX, None)
    weight = P(("plane", "core", "fsdp"), None)
    gain = P(("plane", "core", "fsdp"))
    return jax.shard_map(
        on_device,
        mesh=inner,
        in_specs=(token, P("fsdp", None)) + (weight,) * 7 + (gain, gain, token),
        out_specs=(token, token) + (weight,) * 7 + (gain, gain),
        check_vma=False,
    )
```

```python
import functools

import jax
import jax.numpy as jnp
from jax import lax
from jax.experimental import pallas as pl
from jax.experimental.pallas import tpu as pltpu
from jax.sharding import Mesh, PartitionSpec as P

HEAD_DIM = 64
THETA = 130000.0
EPS = 1e-05
SCALE = HEAD_DIM**-0.5
NEG = -1e30
BF = jnp.bfloat16
F32 = jnp.float32
CTX = ("plane", "core")
TOK = ("core", "fsdp")
VMEM_LIMIT = 56 * 1024 * 1024
VMEM_SMALL = 30 * 1024 * 1024
LIGHT = pl.CostEstimate(flops=1024, bytes_accessed=1024, transcendentals=0)


def mm(left, right):
    return jnp.dot(left, right, preferred_element_type=F32)


def mm_t(left, right):
    return lax.dot_general(left, right, (((1,), (1,)), ((), ())), preferred_element_type=F32)


def t_mm(left, right):
    return lax.dot_general(left, right, (((0,), (0,)), ((), ())), preferred_element_type=F32)


def rope_tables(length, cols):
    half = HEAD_DIM // 2
    freq = THETA ** (-2.0 * jnp.arange(half, dtype=F32) / HEAD_DIM)
    angle = jnp.arange(length, dtype=jnp.int32).astype(F32)[:, None] * freq
    cosine, sine = jnp.cos(angle), jnp.sin(angle)
    heads = cols // HEAD_DIM
    return (
        jnp.tile(jnp.concatenate([cosine, cosine], axis=1), (1, heads)),
        jnp.tile(jnp.concatenate([-sine, sine], axis=1), (1, heads)),
    )


def swap_halves(values):
    cols = values.shape[1]
    half = HEAD_DIM // 2
    lane = lax.broadcasted_iota(jnp.int32, values.shape, 1)
    up = pltpu.roll(values, half, 1)
    down = pltpu.roll(values, cols - half, 1)
    return jnp.where(lane % HEAD_DIM < half, down, up)


def relative(n_plane):
    bits = n_plane.bit_length() - 1
    steps = [[1 << ((s + c) % bits) for s in range(bits)] for c in range(2)]
    order = []
    for masks in steps:
        found = [0]
        for mask in masks:
            found += [m ^ mask for m in found]
        order.append(found)
    return steps, order


def slot_block(pair_ref, me_ref, slot, n_ctx):
    _, order = relative(n_ctx // 2)
    at, half = slot // 2, n_ctx // 2
    plane, core = me_ref[0], me_ref[1]
    if at < half:
        holder = jnp.bitwise_xor(plane, jnp.where(core == 0, order[0][at], order[1][at])) * 2 + core
    else:
        at -= half
        holder = jnp.bitwise_xor(plane, jnp.where(core == 0, order[1][at], order[0][at])) * 2 + 1 - core
    low = pair_ref[0, holder]
    return low if slot % 2 == 0 else 2 * n_ctx - 1 - low


def head_mask(shape, head):
    lane = lax.broadcasted_iota(jnp.int32, shape, 1)
    return lane // HEAD_DIM == head


def params(grant=VMEM_SMALL):
    return pltpu.CompilerParams(vmem_limit_bytes=grant)


def in_vmem(n):
    return [pl.BlockSpec(memory_space=pltpu.VMEM)] * n


def in_smem(n):
    return [pl.BlockSpec(memory_space=pltpu.SMEM)] * n


def forward_kernel(
    n_ctx, qblk, pair_ref, me_ref, x_ref, w_ref, turn_ref, kept_ref, r_ref, o_ref, lse_ref, acc_ref
):
    q_ref, k_ref, v_ref = (kept_ref.at[i] for i in range(3))
    cos_ref, sin_ref = turn_ref.at[0], turn_ref.at[1]
    length, cols = q_ref.shape
    blk = length // (2 * n_ctx)
    heads = cols // HEAD_DIM
    for at in range(n_ctx):
        x = x_ref[pl.ds(at * 2 * blk, 2 * blk), :]
        x_f = x.astype(F32)
        scale = lax.rsqrt(jnp.mean(x_f * x_f, axis=1, keepdims=True) + EPS)
        r_ref[pl.ds(at * 2 * blk, 2 * blk), :] = scale
        qkv = mm(x, w_ref[...]) * scale
        for second in range(2):
            to = pl.ds(pl.multiple_of(slot_block(pair_ref, me_ref, 2 * at + second, n_ctx) * blk, blk), blk)
            cosine, sine = cos_ref[to, :], sin_ref[to, :]
            query = qkv[second * blk : (second + 1) * blk, :cols]
            key = qkv[second * blk : (second + 1) * blk, cols : 2 * cols]
            q_ref[to, :] = (query * cosine + swap_halves(query) * sine).astype(BF)
            k_ref[to, :] = (key * cosine + swap_halves(key) * sine).astype(BF)
            v_ref[to, :] = qkv[second * blk : (second + 1) * blk, 2 * cols :].astype(BF)
    acc_ref[...] = jnp.zeros_like(acc_ref)
    lse_ref[...] = jnp.zeros_like(lse_ref)

    def one_head(head, carry):
        mask = head_mask((qblk, cols), head)
        here = lax.broadcasted_iota(jnp.int32, (qblk, lse_ref.shape[1]), 1) == head
        below = lax.broadcasted_iota(jnp.int32, (qblk, qblk), 1) <= lax.broadcasted_iota(jnp.int32, (qblk, qblk), 0)
        for i in range(length // qblk):
            rows = pl.ds(i * qblk, qblk)
            query = jnp.where(mask, q_ref[rows, :], jnp.zeros((), BF))
            last = jnp.where(below, mm_t(query, k_ref[rows, :]), NEG)
            peak = jnp.max(last, axis=1, keepdims=True)
            if i:
                before = mm_t(query, k_ref[: i * qblk, :])
                peak = jnp.maximum(peak, jnp.max(before, axis=1, keepdims=True))
            shift = peak * SCALE
            last = jnp.exp(last * SCALE - shift)
            total = jnp.sum(last, axis=1, keepdims=True)
            out = mm(last.astype(BF), v_ref[rows, :])
            if i:
                before = jnp.exp(before * SCALE - shift)
                total += jnp.sum(before, axis=1, keepdims=True)
                out += mm(before.astype(BF), v_ref[: i * qblk, :])
            acc_ref[rows, :] = jnp.where(mask, out * (1.0 / total), acc_ref[rows, :])
            lse_ref[rows, :] = jnp.where(here, shift + jnp.log(total), lse_ref[rows, :])
        return carry

    lax.fori_loop(0, heads, one_head, 0)
    for slot in range(2 * n_ctx):
        at = pl.multiple_of(slot_block(pair_ref, me_ref, slot, n_ctx) * blk, blk)
        o_ref[pl.ds(slot * blk, blk), :] = acc_ref[pl.ds(at, blk), :].astype(BF)
    kept_ref[3] = acc_ref[...].astype(BF)


def attention_forward(pair, me, tokens, weight, turn):
    _, length, cols = turn.shape
    width = weight.shape[0]
    n_ctx = width // cols
    return pl.pallas_call(
        functools.partial(forward_kernel, n_ctx, 256),
        out_shape=[
            jax.ShapeDtypeStruct((4, length, cols), BF),
            jax.ShapeDtypeStruct((length, 1), F32),
            jax.ShapeDtypeStruct((length, cols), BF),
            jax.ShapeDtypeStruct((length, 128), F32),
        ],
        in_specs=in_smem(2) + in_vmem(3),
        out_specs=in_vmem(4),
        scratch_shapes=[pltpu.VMEM((length, cols), F32)],
        compiler_params=params(VMEM_LIMIT),
        cost_estimate=LIGHT,
        name="attention_forward",
    )(pair, me, tokens, weight, turn)


def backward_kernel(
    n_ctx, qblk, pair_ref, me_ref, do_ref, kept_ref, r_ref, lse_ref, turn_ref,
    g_ref, gr_ref, go_ref, dq_ref, dk_ref, dv_ref, centre_ref,
):
    q_ref, k_ref, v_ref, o_ref = (kept_ref.at[i] for i in range(4))
    cos_ref, sin_ref = turn_ref.at[0], turn_ref.at[1]
    length, cols = q_ref.shape
    blk = length // (2 * n_ctx)
    heads = cols // HEAD_DIM
    for slot in range(2 * n_ctx):
        at = pl.multiple_of(slot_block(pair_ref, me_ref, slot, n_ctx) * blk, blk)
        go_ref[pl.ds(at, blk), :] = do_ref[pl.ds(slot * blk, blk), :]
    dq_ref[...] = jnp.zeros_like(dq_ref)
    dk_ref[...] = jnp.zeros_like(dk_ref)
    dv_ref[...] = jnp.zeros_like(dv_ref)

    pick = head_mask((8, cols), lax.broadcasted_iota(jnp.int32, (8, cols), 0)).astype(F32)
    centre_ref[...] = lax.dot_general(
        pick,
        go_ref[...].astype(F32) * o_ref[...].astype(F32),
        (((1,), (1,)), ((), ())),
        precision=lax.Precision.HIGHEST,
        preferred_element_type=F32,
    )

    def one_head(head, carry):
        mask = head_mask((qblk, cols), head)
        below = lax.broadcasted_iota(jnp.int32, (qblk, qblk), 0) <= lax.broadcasted_iota(jnp.int32, (qblk, qblk), 1)
        for i in range(length // qblk):
            rows = pl.ds(i * qblk, qblk)
            query = jnp.where(mask, q_ref[rows, :], jnp.zeros((), BF))
            grad = jnp.where(mask, go_ref[rows, :], jnp.zeros((), BF))
            lse = lse_ref[pl.ds(head, 1), rows]
            centre = centre_ref[pl.ds(head, 1), rows]
            out = None
            for at, size in ((i * qblk, qblk), (0, i * qblk)):
                if not size:
                    continue
                keys = pl.ds(at, size)
                probs = jnp.exp(mm_t(k_ref[keys, :], query) * SCALE - lse)
                if at or not i:
                    probs = jnp.where(below, probs, 0.0)
                grad_probs = mm_t(v_ref[keys, :], grad)
                grad_scores = (probs * (grad_probs - centre)).astype(BF)
                dk_ref[keys, :] += mm(grad_scores, query)
                dv_ref[keys, :] += mm(probs.astype(BF), grad)
                term = t_mm(grad_scores, k_ref[keys, :])
                out = term if out is None else out + term
            dq_ref[rows, :] = jnp.where(mask, out, dq_ref[rows, :])
        return carry

    lax.fori_loop(0, heads, one_head, 0)
    for slot in range(2 * n_ctx):
        at = pl.multiple_of(slot_block(pair_ref, me_ref, slot, n_ctx) * blk, blk)
        rows = pl.ds(slot * blk, blk)
        to = pl.ds(at, blk)
        cosine, sine = cos_ref[to, :], sin_ref[to, :]
        scale = r_ref[rows, :]
        query = (dq_ref[to, :] * SCALE).astype(BF).astype(F32)
        key = (dk_ref[to, :] * SCALE).astype(BF).astype(F32)
        value = dv_ref[to, :].astype(BF).astype(F32)
        query = query * cosine - swap_halves(query) * sine
        key = key * cosine - swap_halves(key) * sine
        for at_col, part in enumerate((query, key, value)):
            span = pl.ds(at_col * cols, cols)
            g_ref[rows, span] = part.astype(BF)
            gr_ref[rows, span] = (part * scale).astype(BF)


def attention_backward(pair, me, n_ctx, grad, kept, scale, lse, turn):
    _, length, cols = turn.shape
    return pl.pallas_call(
        functools.partial(backward_kernel, n_ctx, 256),
        out_shape=[jax.ShapeDtypeStruct((length, 3 * cols), BF)] * 2,
        in_specs=in_smem(2) + in_vmem(5),
        out_specs=in_vmem(2),
        scratch_shapes=[pltpu.VMEM((length, cols), BF)]
        + [pltpu.VMEM((length, cols), F32)] * 3
        + [pltpu.VMEM((8, length), F32)],
        compiler_params=params(),
        cost_estimate=LIGHT,
        name="attention_backward",
    )(pair, me, grad, kept, scale, lse, turn)


def feed_forward_kernel(
    core_ref, n_ref, c_ref, g_ref, u_ref, d_ref, h_ref, dg_ref, du_ref, theirs_ref, mine_ref
):
    rows, cot = n_ref[...], c_ref[...]
    hid, tile = g_ref.shape[1], 256
    for at in range(0, hid, tile):
        span = slice(at, at + tile)
        gate = mm(rows, g_ref[:, span])
        up = mm(rows, u_ref[:, span])
        grad = mm_t(cot, d_ref[span, :])
        sig = 1.0 / (1.0 + jnp.exp(-gate))
        active = gate * sig
        h_ref[:, span] = (active * up).astype(BF)
        dg_ref[:, span] = (grad * up * sig * (1.0 + gate * (1.0 - sig))).astype(BF)
        du_ref[:, span] = (grad * active).astype(BF)
    back = (mm_t(dg_ref[...], g_ref[...]) + mm_t(du_ref[...], u_ref[...])).astype(BF)
    first = pl.program_id(0) < pl.num_programs(0) // 2

    @pl.when(first)
    def _():
        theirs_ref[...] = back

    @pl.when(jnp.logical_not(first))
    def _():
        mine_ref[...] = back


def feed_forward(normed, cotangent, gate_w, up_w, down_w):
    count, width = normed.shape
    hid = gate_w.shape[1]
    tile = 256
    half = count // tile // 2

    def rows_of(r, core):
        return (jnp.where(r < half, (1 - core[0]) * half + r, core[0] * half + r - half), 0)

    def fixed(r, core):
        return (0, 0)

    once = pl.Buffered(1)
    return pl.pallas_call(
        feed_forward_kernel,
        grid_spec=pltpu.PrefetchScalarGridSpec(
            num_scalar_prefetch=1,
            grid=(2 * half,),
            in_specs=[
                pl.BlockSpec((tile, width), rows_of),
                pl.BlockSpec((tile, width), rows_of),
                pl.BlockSpec((width, hid), fixed, pipeline_mode=once),
                pl.BlockSpec((width, hid), fixed, pipeline_mode=once),
                pl.BlockSpec((hid, width), fixed, pipeline_mode=once),
            ],
            out_specs=[pl.BlockSpec((tile, hid), rows_of)] * 3
            + [
                pl.BlockSpec((tile, width), lambda r, core: (jnp.minimum(r, half - 1), 0)),
                pl.BlockSpec((tile, width), lambda r, core: (jnp.maximum(r - half, 0), 0)),
            ],
        ),
        out_shape=[jax.ShapeDtypeStruct((count, hid), BF)] * 3
        + [jax.ShapeDtypeStruct((count // 2, width), BF)] * 2,
        compiler_params=params(VMEM_LIMIT),
        cost_estimate=LIGHT,
        name="feed_forward",
    )(lax.axis_index("core").astype(jnp.int32)[None], normed, cotangent, gate_w, up_w, down_w)


def branch_kernel(core_ref, h_ref, d_ref, theirs_ref, mine_ref):
    out = mm(h_ref[...], d_ref[...]).astype(BF)
    first = pl.program_id(0) < pl.num_programs(0) // 2

    @pl.when(first)
    def _():
        theirs_ref[...] = out

    @pl.when(jnp.logical_not(first))
    def _():
        mine_ref[...] = out


def branch_rows(hidden, down_w):
    count, hid = hidden.shape
    width = down_w.shape[1]
    tile = 256
    half = count // tile // 2
    return pl.pallas_call(
        branch_kernel,
        grid_spec=pltpu.PrefetchScalarGridSpec(
            num_scalar_prefetch=1,
            grid=(2 * half,),
            in_specs=[
                pl.BlockSpec(
                    (tile, hid),
                    lambda r, core: (jnp.where(r < half, (1 - core[0]) * half + r, core[0] * half + r - half), 0),
                ),
                pl.BlockSpec((hid, width), lambda r, core: (0, 0), pipeline_mode=pl.Buffered(1)),
            ],
            out_specs=[
                pl.BlockSpec((tile, width), lambda r, core: (jnp.minimum(r, half - 1), 0)),
                pl.BlockSpec((tile, width), lambda r, core: (jnp.maximum(r - half, 0), 0)),
            ],
        ),
        out_shape=[jax.ShapeDtypeStruct((count // 2, width), BF)] * 2,
        compiler_params=params(),
        cost_estimate=LIGHT,
        name="branch_rows",
    )(lax.axis_index("core").astype(jnp.int32)[None], hidden, down_w)


def merge_kernel(a_ref, m_ref, *refs):
    *b_refs, go_ref, out_ref, all_ref = refs
    rows = b_refs[0].shape[0]
    for at, ref in enumerate(b_refs):
        all_ref[pl.ds(at * rows, rows), :] = ref[...]
    go_ref[...] = mm_t(all_ref[...], m_ref[...]).astype(BF)
    out_ref[...] = t_mm(a_ref[...], all_ref[...]).astype(BF)


def merge_terms(attended, merge_rows, pieces):
    length, cols = attended.shape
    width = merge_rows.shape[1]
    return pl.pallas_call(
        merge_kernel,
        out_shape=[jax.ShapeDtypeStruct((length, cols), BF), jax.ShapeDtypeStruct((cols, width), BF)],
        in_specs=in_vmem(2 + len(pieces)),
        out_specs=in_vmem(2),
        scratch_shapes=[pltpu.VMEM((length, width), BF)],
        compiler_params=params(),
        cost_estimate=LIGHT,
        name="merge_terms",
    )(attended, merge_rows, *pieces)


def heads_term_kernel(x_ref, g_ref, out_ref):
    out_ref[...] = mm(x_ref[...], g_ref[...]).astype(BF)


def heads_term(tokens_t, grad):
    width, count = tokens_t.shape
    cols = grad.shape[1]
    tile = 512
    return pl.pallas_call(
        heads_term_kernel,
        grid=(width // tile,),
        in_specs=[
            pl.BlockSpec((tile, count), lambda i: (i, 0)),
            pl.BlockSpec((count, cols), lambda i: (0, 0), pipeline_mode=pl.Buffered(1)),
        ],
        out_specs=pl.BlockSpec((tile, cols), lambda i: (i, 0)),
        out_shape=jax.ShapeDtypeStruct((width, cols), BF),
        compiler_params=params(),
        cost_estimate=LIGHT,
        name="heads_term",
    )(tokens_t, grad)


def weight_rows_kernel(at_ref, left_ref, right_ref, *out_refs):
    out = t_mm(left_ref[...], right_ref[...]).astype(BF)
    for i, ref in enumerate(out_refs):

        @pl.when(pl.program_id(0) == i)
        def _(ref=ref):
            ref[...] = out


def weight_rows(left, right, index, size):
    count, n = left.shape[0], len(index)
    width = right.shape[1]
    return pl.pallas_call(
        weight_rows_kernel,
        grid_spec=pltpu.PrefetchScalarGridSpec(
            num_scalar_prefetch=1,
            grid=(n,),
            in_specs=[
                pl.BlockSpec((count, size), lambda i, at: (0, at[i])),
                pl.BlockSpec((count, width), lambda i, at: (0, 0), pipeline_mode=pl.Buffered(1)),
            ],
            out_specs=[pl.BlockSpec((size, width), lambda i, at: (0, 0), pipeline_mode=pl.Buffered(1))] * n,
        ),
        out_shape=[jax.ShapeDtypeStruct((size, width), BF)] * n,
        compiler_params=params(),
        cost_estimate=LIGHT,
        name="weight_rows",
    )(jnp.stack(index).astype(jnp.int32), left, right)


def back_kernel(g_ref, w_ref, out_ref):
    out_ref[...] = mm_t(g_ref[...], w_ref[...]).astype(BF)


def back_rows(grad, weight, half):
    count, cols = grad.shape
    width = weight.shape[0]
    tile = 256
    steps = count // 2 // tile
    return pl.pallas_call(
        back_kernel,
        grid=(steps,),
        in_specs=[
            pl.BlockSpec((tile, cols), lambda r: (half * steps + r, 0)),
            pl.BlockSpec((width, cols), lambda r: (0, 0), pipeline_mode=pl.Buffered(1)),
        ],
        out_specs=pl.BlockSpec((tile, width), lambda r: (r, 0)),
        out_shape=jax.ShapeDtypeStruct((count // 2, width), BF),
        compiler_params=params(),
        cost_estimate=LIGHT,
        name="back_rows",
    )(grad, weight)


def fold_heads_kernel(q_ref, k_ref, v_ref, gain_ref, out_ref):
    n_ctx, _, cols = out_ref.shape
    cols //= 3
    gain = gain_ref[...]
    for at, ref in enumerate((q_ref, k_ref, v_ref)):
        for to in range(n_ctx):
            part = ref[:, to * cols : (to + 1) * cols].astype(F32) * gain
            out_ref[to, :, at * cols : (at + 1) * cols] = part.astype(BF)


def fold_heads(weights, gain, n_ctx):
    rows, width = weights[0].shape
    return pl.pallas_call(
        fold_heads_kernel,
        out_shape=jax.ShapeDtypeStruct((n_ctx, rows, 3 * (width // n_ctx)), BF),
        in_specs=in_vmem(4),
        out_specs=pl.BlockSpec(memory_space=pltpu.VMEM),
        compiler_params=params(),
        cost_estimate=LIGHT,
        name="fold_heads",
    )(*weights, gain)


def unfold_heads_kernel(s_ref, q_ref, k_ref, v_ref, gain_ref, dq_ref, dk_ref, dv_ref, first_ref):
    n_ctx, rows, cols = s_ref.shape
    cols //= 3
    gain = gain_ref[...]
    total = jnp.zeros((rows, cols), F32)
    for at, (ref, out) in enumerate(((q_ref, dq_ref), (k_ref, dk_ref), (v_ref, dv_ref))):
        for to in range(n_ctx):
            span = slice(to * cols, (to + 1) * cols)
            part = s_ref[to, :, at * cols : (at + 1) * cols].astype(F32)
            total += part * ref[:, span].astype(F32)
            out[:, span] = part * gain
    first_ref[...] = jnp.sum(total, axis=1, keepdims=True)


def unfold_heads(sums, weights, gain):
    rows, width = weights[0].shape
    return pl.pallas_call(
        unfold_heads_kernel,
        out_shape=[jax.ShapeDtypeStruct((rows, width), F32)] * 3 + [jax.ShapeDtypeStruct((rows, 1), F32)],
        in_specs=in_vmem(5),
        out_specs=in_vmem(4),
        compiler_params=params(),
        cost_estimate=LIGHT,
        name="unfold_heads",
    )(sums, *weights, gain)


def fold_hidden_kernel(piece, w_ref, gain_ref, out_ref):
    n_core, n_fsdp, _, hid = out_ref.shape
    gain = gain_ref[...]
    for plane in range(hid // piece):
        for core in range(n_core):
            for line in range(n_fsdp):
                at = ((plane * n_core + core) * n_fsdp + line) * piece
                part = w_ref[:, at : at + piece].astype(F32) * gain
                out_ref[core, line, :, plane * piece : (plane + 1) * piece] = part.astype(BF)


def fold_hidden(weight, gain, n_plane, n_core, n_fsdp):
    rows, total = weight.shape
    piece = total // (n_plane * n_core * n_fsdp)
    if piece % 128:
        folded = (weight.astype(F32) * gain).astype(BF).reshape(rows, n_plane, n_core, n_fsdp, piece)
        return folded.transpose(2, 3, 0, 1, 4).reshape(n_core, n_fsdp, rows, n_plane * piece)
    return pl.pallas_call(
        functools.partial(fold_hidden_kernel, piece),
        out_shape=jax.ShapeDtypeStruct((n_core, n_fsdp, rows, n_plane * piece), BF),
        in_specs=in_vmem(2),
        out_specs=pl.BlockSpec(memory_space=pltpu.VMEM),
        compiler_params=params(),
        cost_estimate=LIGHT,
        name="fold_hidden",
    )(weight, gain)


def unfold_hidden_kernel(piece, at_ref, *refs):
    *s_refs, w_ref, gain_ref, out_ref, second_ref = refs
    n_fsdp = len(s_refs)
    n_core, rows, hid = s_refs[0].shape
    gain = gain_ref[...]
    total = jnp.zeros((rows, piece), F32)
    for mask, ref in enumerate(s_refs):
        line = jnp.bitwise_xor(at_ref[1], mask)
        for other in range(n_core):
            core = jnp.bitwise_xor(at_ref[0], other)
            for plane in range(hid // piece):
                at = ((plane * n_core + core) * n_fsdp + line) * piece
                span = pl.ds(pl.multiple_of(at, piece), piece)
                part = ref[other, :, plane * piece : (plane + 1) * piece].astype(F32)
                total += part * w_ref[:, span].astype(F32)
                out_ref[:, span] = part * gain
    second_ref[...] = jnp.sum(total, axis=1, keepdims=True)


def unfold_hidden(pieces, weight, gain, n_plane):
    rows, total = weight.shape
    n_core, _, hid = pieces[0].shape
    n_fsdp = len(pieces)
    piece = hid // n_plane
    core, line = lax.axis_index("core"), lax.axis_index("fsdp")
    if piece % 128:
        out = jnp.zeros((rows, n_plane, n_core, n_fsdp, piece), BF)
        for mask, block in enumerate(pieces):
            for other in range(n_core):
                part = block[other].reshape(rows, n_plane, 1, 1, piece)
                out = lax.dynamic_update_slice(out, part, (0, 0, core ^ other, line ^ mask, 0))
        out = out.reshape(rows, total).astype(F32)
        return out * gain, jnp.sum(out * weight.astype(F32), axis=1, keepdims=True)
    return pl.pallas_call(
        functools.partial(unfold_hidden_kernel, piece),
        out_shape=[jax.ShapeDtypeStruct((rows, total), F32), jax.ShapeDtypeStruct((rows, 1), F32)],
        in_specs=in_smem(1) + in_vmem(n_fsdp + 2),
        out_specs=in_vmem(2),
        compiler_params=params(),
        cost_estimate=LIGHT,
        name="unfold_hidden",
    )(jnp.stack([core, line]).astype(jnp.int32), *pieces, weight, gain)


def place_kernel(at_ref, *refs):
    *p_refs, out_ref = refs
    for i, ref in enumerate(p_refs):
        out_ref[at_ref[i]] = ref[...]


def place(pieces, index, room=None):
    n = len(pieces)
    moved = 2 * n * pieces[0].size * pieces[0].dtype.itemsize
    return pl.pallas_call(
        place_kernel,
        out_shape=jax.ShapeDtypeStruct((room or n,) + pieces[0].shape, pieces[0].dtype),
        in_specs=in_smem(1) + in_vmem(n),
        out_specs=pl.BlockSpec(memory_space=pltpu.VMEM),
        compiler_params=params(VMEM_LIMIT),
        cost_estimate=LIGHT,
        name="place",
    )(jnp.stack(index).astype(jnp.int32), *pieces)


def gather(value, axes, axis=0):
    return lax.all_gather(value, axes, axis=axis, tiled=True)


def scatter(value, axes):
    return lax.psum_scatter(value, axes, scatter_dimension=0, tiled=True)


def exchange(value, axes):
    return lax.all_to_all(value, axes, split_axis=0, concat_axis=0, tiled=True)


def together(values):
    return lax.optimization_barrier(values)


def core_swap(value):
    n = lax.axis_size("plane") * 2
    return lax.ppermute(value, CTX, [(i, i ^ 1) for i in range(n)])


def plane_step(value, step):
    steps, _ = relative(lax.axis_size("plane"))
    n = lax.axis_size("plane") * 2
    return lax.ppermute(value, CTX, [(i, i ^ (2 * steps[i % 2][step])) for i in range(n)])


def line_swap(value, mask):
    n = lax.axis_size("fsdp")
    return lax.ppermute(value, "fsdp", [(i, i ^ mask) for i in range(n)])


def plane_gather_more(pieces):
    step = len(pieces).bit_length() - 1
    return pieces + [plane_step(piece, step) for piece in pieces]


def plane_gather(value):
    pieces = [value]
    while len(pieces) < lax.axis_size("plane"):
        pieces = plane_gather_more(pieces)
    return pieces


def plane_send(chunks):
    n = len(chunks) // 2
    return [plane_step(chunk, n.bit_length() - 1) for chunk in chunks[n:]]


def plane_add(chunks, came):
    return [(mine.astype(F32) + chunk.astype(F32)).astype(BF) for mine, chunk in zip(chunks, came)]


def plane_scatter(chunks):
    while len(chunks) > 1:
        chunks = plane_add(chunks, plane_send(chunks))
    return chunks[0]


def plane_index():
    _, order = relative(lax.axis_size("plane"))
    core = lax.axis_index("core")
    plane = lax.axis_index("plane")
    return [plane ^ jnp.where(core == 0, a, b) for a, b in zip(*order)]


def part(value, at, size, axis):
    return lax.dynamic_slice_in_dim(value, at * size, size, axis)


def ctx_gather(value):
    mine = plane_gather(value)
    return mine + [core_swap(piece) for piece in mine]


def ctx_scatter(theirs, mine, n_plane):
    total = (mine.astype(F32) + core_swap(theirs).astype(F32)).astype(BF)
    rows = total.shape[0] // n_plane
    return plane_scatter([total[i * rows : (i + 1) * rows] for i in range(n_plane)])


def cores_pair(value):
    core = lax.axis_index("core")
    kept = lax.dynamic_index_in_dim(value, core, 0, keepdims=False)
    return kept, core_swap(lax.dynamic_index_in_dim(value, 1 - core, 0, keepdims=False))


def lines_parts(pair):
    line = lax.axis_index("fsdp")
    return [
        jnp.stack([lax.dynamic_index_in_dim(v, line ^ mask, 0, keepdims=False) for v in pair])
        for mask in range(lax.axis_size("fsdp"))
    ]


def lines_swap(parts):
    return parts[:1] + [line_swap(parts[mask], mask) for mask in range(1, len(parts))]


def lines_pair(pair):
    return lines_swap(lines_parts(pair))


def line_rows_kernel(at_ref, *refs):
    *p_refs, out_ref = refs
    n_fsdp = len(p_refs)
    for mask, ref in enumerate(p_refs):
        line = jnp.bitwise_xor(at_ref[1], mask)
        for other in range(2):
            core = jnp.bitwise_xor(at_ref[0], other)
            out_ref[core * n_fsdp + line] = ref[other]


def line_rows(pieces):
    n = 2 * len(pieces)
    at = jnp.stack([lax.axis_index("core"), lax.axis_index("fsdp")]).astype(jnp.int32)
    return pl.pallas_call(
        line_rows_kernel,
        out_shape=jax.ShapeDtypeStruct((n,) + pieces[0].shape[1:], pieces[0].dtype),
        in_specs=in_smem(1) + in_vmem(len(pieces)),
        out_specs=pl.BlockSpec(memory_space=pltpu.VMEM),
        compiler_params=params(VMEM_LIMIT),
        cost_estimate=LIGHT,
        name="line_rows",
    )(at, *pieces)


def on_device(
    layer_input, pairing, query_weight, key_weight, value_weight, merge_weight,
    gate_weight, up_weight, down_weight, norm_first, norm_second, output_cotangent,
):
    n_plane = lax.axis_size("plane")
    n_core = lax.axis_size("core")
    n_fsdp = lax.axis_size("fsdp")
    n_ctx = n_plane * n_core
    n_tok = n_core * n_fsdp
    me = jnp.stack([lax.axis_index("plane"), lax.axis_index("core")]).astype(jnp.int32)
    index = plane_index()
    _, rows, width = layer_input.shape
    length = rows * n_ctx
    half = length // 2
    cols = width // n_ctx
    dev_rows = gate_weight.shape[0]
    piece = gate_weight.shape[1] // (n_ctx * n_fsdp)
    hid = piece * n_plane
    d_rows = n_tok * dev_rows
    tokens = layer_input.reshape(rows, width)
    cotangent = output_cotangent.reshape(rows, width)
    gain_first = norm_first.astype(F32)[:, None]
    gain_second = norm_second.astype(F32)[:, None]
    projections = (query_weight, key_weight, value_weight)

    merge_rows = gather(merge_weight, "fsdp")
    gate_moved = lines_pair(cores_pair(fold_hidden(gate_weight, gain_second, n_plane, n_core, n_fsdp)))
    own = exchange(fold_heads(projections, gain_first, n_ctx), CTX)
    x_pieces = ctx_gather(tokens)
    up_pair = cores_pair(fold_hidden(up_weight, gain_second, n_plane, n_core, n_fsdp))
    turn = jnp.stack(rope_tables(length, cols))
    own, gate_moved, x_pieces, up_pair, merge_rows = together(
        (own, gate_moved, x_pieces, up_pair, merge_rows)
    )
    qkv_weight = gather(own[:, None], "fsdp", axis=1).reshape(width, 3 * cols)
    gate_pieces = plane_gather(line_rows(gate_moved).reshape(d_rows, hid))
    down_pieces = plane_gather_more([down_weight])
    x_all = jnp.concatenate(x_pieces, axis=0)
    x_all, gate_pieces, down_pieces = together((x_all, gate_pieces, down_pieces))
    up_moved = lines_pair(up_pair)
    cot_all = gather(cotangent, TOK)

    kept, scale_all, attended, lse = attention_forward(pairing, me, x_all, qkv_weight, turn)
    while len(down_pieces) < n_plane:
        down_pieces = plane_gather_more(down_pieces)
    attended, down_pieces = together((attended, down_pieces))
    down_rows = place(down_pieces, index).reshape(hid, width)
    own_f = tokens.astype(F32)
    theirs = together(mm(attended[half:], merge_rows).astype(BF))
    mine = together(mm(attended[:half], merge_rows).astype(BF))
    mixed = own_f + ctx_scatter(theirs, mine, n_plane)
    lse_rows = lse[:, :8].T
    x_t = x_all.reshape(length, n_ctx, n_fsdp, dev_rows).transpose(2, 1, 3, 0).reshape(width, length)
    gate_rows = place(gate_pieces, index).reshape(width, hid)
    mixed, up_moved, lse_rows, x_t, down_rows, gate_rows = together(
        (mixed, up_moved, lse_rows, x_t, down_rows, gate_rows)
    )
    up_pieces = plane_gather(line_rows(up_moved).reshape(d_rows, hid))
    up_rows = place(up_pieces[:-1], index[:-1], n_plane)
    up_rows = lax.dynamic_update_slice(up_rows, up_pieces[-1][None], (index[-1], 0, 0)).reshape(width, hid)

    scale_second = lax.rsqrt(jnp.mean(mixed * mixed, axis=-1, keepdims=True) + EPS)
    unit_second = mixed * scale_second
    normed_all = gather(unit_second.astype(BF), TOK)
    hidden, grad_gate, grad_up, theirs, mine = feed_forward(
        normed_all, cot_all, gate_rows, up_rows, down_rows
    )
    e_two = (mine.astype(F32) + core_swap(theirs).astype(F32)).astype(BF)

    hidden, grad_gate, grad_up, e_two = together((hidden, grad_gate, grad_up, e_two))
    gate_late = weight_rows(normed_all, grad_gate, index[n_plane // 2 :], d_rows)
    gate_chunks = list(weight_rows(normed_all, grad_gate, index[: n_plane // 2], d_rows)) + list(gate_late)
    gate_came = plane_send(gate_chunks)
    up_chunks = [together(t_mm(part(normed_all, at, d_rows, 1), grad_up).astype(BF)) for at in index]
    theirs, mine = branch_rows(hidden, down_rows)
    gate_chunks, gate_came, up_chunks, theirs, mine = together(
        (gate_chunks, gate_came, up_chunks, theirs, mine)
    )
    gate_chunks = plane_add(gate_chunks, gate_came)
    branch = (mine.astype(F32) + core_swap(theirs).astype(F32)).astype(BF)
    e_two = scatter(e_two, "fsdp")
    e_two, gate_chunks, up_chunks, branch = together((e_two, gate_chunks, up_chunks, branch))
    branch_sum = scatter(branch, "fsdp")
    gate_sum = plane_scatter(gate_chunks)
    e_two_f = e_two.astype(F32)
    grad_mixed = cotangent.astype(F32) + scale_second * (
        e_two_f - unit_second * jnp.mean(e_two_f * unit_second, axis=-1, keepdims=True)
    )
    branch_pieces = plane_gather_more([grad_mixed.astype(BF)])
    branch_pieces, gate_sum = together((branch_pieces, gate_sum))
    gate_parts = lines_parts(cores_pair(gate_sum.reshape(n_core, n_fsdp, dev_rows, hid)))
    while len(branch_pieces) < n_plane:
        branch_pieces = plane_gather_more(branch_pieces)
    branch_pieces = branch_pieces + [core_swap(value) for value in branch_pieces]
    gate_back = lines_swap(gate_parts)

    branch_pieces, up_chunks = together((branch_pieces, up_chunks))
    up_came = plane_send(up_chunks)
    grad_attended, merge_grad = merge_terms(attended, merge_rows, branch_pieces)
    merge_grad, grad_attended = together((merge_grad, grad_attended))
    merge_grad = scatter(merge_grad, "fsdp")
    grad_qkv, grad_scaled = attention_backward(
        pairing, me, n_ctx, grad_attended, kept, scale_all, lse_rows, turn
    )
    grad_scaled, branch_sum = together((grad_scaled, branch_sum))
    sums = heads_term(x_t, grad_scaled)
    grad_qkv, up_chunks, up_came, gate_back, sums, merge_grad, branch_sum = together(
        (grad_qkv, up_chunks, up_came, gate_back, sums, merge_grad, branch_sum)
    )
    sums = scatter(sums, "fsdp")
    up_sum = plane_scatter(plane_add(up_chunks, up_came))
    layer_output = (mixed + branch_sum.astype(F32)).astype(BF)
    theirs = back_rows(grad_qkv, qkv_weight, 1)
    mine = back_rows(grad_qkv, qkv_weight, 0)
    e_one = ctx_scatter(theirs, mine, n_plane)
    up_parts = lines_parts(cores_pair(up_sum.reshape(n_core, n_fsdp, dev_rows, hid)))
    hidden, mine = together((hidden, mine))
    down_chunks = [together(t_mm(part(hidden, at, piece, 1), cot_all).astype(BF)) for at in index]
    e_one, down_chunks = together((e_one, down_chunks))
    down_came = plane_send(down_chunks)
    sums, up_parts = together((sums, up_parts))
    up_back = lines_swap(up_parts)
    sums = exchange(sums.reshape(n_ctx, dev_rows, 3 * cols), CTX)
    query_grad, key_grad, value_grad, first_grad = unfold_heads(sums, projections, gain_first)
    query_grad, key_grad, value_grad, first_grad, up_back, merge_grad = together(
        (query_grad, key_grad, value_grad, first_grad, up_back, merge_grad)
    )
    scale_first = lax.rsqrt(jnp.mean(own_f * own_f, axis=-1, keepdims=True) + EPS)
    unit_first = own_f * scale_first
    input_grad = (
        grad_mixed
        + scale_first * (e_one - unit_first * jnp.mean(e_one * unit_first, axis=-1, keepdims=True))
    ).astype(BF)
    down_grad = plane_scatter(plane_add(down_chunks, down_came)).astype(F32)
    gate_grad, second_gate = unfold_hidden(gate_back, gate_weight, gain_second, n_plane)
    up_grad, second_up = unfold_hidden(up_back, up_weight, gain_second, n_plane)
    second_grad = (second_gate + second_up)[:, 0]
    return (
        layer_output.reshape(1, rows, width),
        input_grad.reshape(1, rows, width),
        query_grad,
        key_grad,
        value_grad,
        merge_grad.astype(F32),
        gate_grad,
        up_grad,
        down_grad,
        first_grad[:, 0],
        second_grad,
    )


def solution(mesh):
    n_ctx, n_fsdp = mesh.shape["ctx"], mesh.shape["fsdp"]
    inner = Mesh(mesh.devices.reshape(n_ctx // 2, 2, n_fsdp), ("plane", "core", "fsdp"))
    token = P("fsdp", CTX, None)
    weight = P(("plane", "core", "fsdp"), None)
    gain = P(("plane", "core", "fsdp"))
    return jax.shard_map(
        on_device,
        mesh=inner,
        in_specs=(token, P("fsdp", None)) + (weight,) * 7 + (gain, gain, token),
        out_specs=(token, token) + (weight,) * 7 + (gain, gain),
        check_vma=False,
    )
```

```python
import functools

import jax
import jax.numpy as jnp
from jax import lax
from jax.experimental import pallas as pl
from jax.experimental.pallas import tpu as pltpu
from jax.sharding import Mesh, PartitionSpec as P

HEAD_DIM = 64
THETA = 130000.0
EPS = 1e-05
SCALE = HEAD_DIM**-0.5
NEG = -1e30
BF = jnp.bfloat16
F32 = jnp.float32
CTX = ("plane", "core")
TOK = ("core", "fsdp")
VMEM_LIMIT = 56 * 1024 * 1024
VMEM_SMALL = 30 * 1024 * 1024
LIGHT = pl.CostEstimate(flops=1024, bytes_accessed=1024, transcendentals=0)


def mm(left, right):
    return jnp.dot(left, right, preferred_element_type=F32)


def mm_t(left, right):
    return lax.dot_general(left, right, (((1,), (1,)), ((), ())), preferred_element_type=F32)


def t_mm(left, right):
    return lax.dot_general(left, right, (((0,), (0,)), ((), ())), preferred_element_type=F32)


def rope_tables(length, cols):
    half = HEAD_DIM // 2
    freq = THETA ** (-2.0 * jnp.arange(half, dtype=F32) / HEAD_DIM)
    angle = jnp.arange(length, dtype=jnp.int32).astype(F32)[:, None] * freq
    cosine, sine = jnp.cos(angle), jnp.sin(angle)
    heads = cols // HEAD_DIM
    return (
        jnp.tile(jnp.concatenate([cosine, cosine], axis=1), (1, heads)),
        jnp.tile(jnp.concatenate([-sine, sine], axis=1), (1, heads)),
    )


def swap_halves(values):
    cols = values.shape[1]
    half = HEAD_DIM // 2
    lane = lax.broadcasted_iota(jnp.int32, values.shape, 1)
    up = pltpu.roll(values, half, 1)
    down = pltpu.roll(values, cols - half, 1)
    return jnp.where(lane % HEAD_DIM < half, down, up)


def relative(n_plane):
    bits = n_plane.bit_length() - 1
    steps = [[1 << ((s + c) % bits) for s in range(bits)] for c in range(2)]
    order = []
    for masks in steps:
        found = [0]
        for mask in masks:
            found += [m ^ mask for m in found]
        order.append(found)
    return steps, order


def slot_block(pair_ref, me_ref, slot, n_ctx):
    _, order = relative(n_ctx // 2)
    at, half = slot // 2, n_ctx // 2
    plane, core = me_ref[0], me_ref[1]
    if at < half:
        holder = jnp.bitwise_xor(plane, jnp.where(core == 0, order[0][at], order[1][at])) * 2 + core
    else:
        at -= half
        holder = jnp.bitwise_xor(plane, jnp.where(core == 0, order[1][at], order[0][at])) * 2 + 1 - core
    low = pair_ref[0, holder]
    return low if slot % 2 == 0 else 2 * n_ctx - 1 - low


def head_mask(shape, head):
    lane = lax.broadcasted_iota(jnp.int32, shape, 1)
    return lane // HEAD_DIM == head


def params(grant=VMEM_SMALL):
    return pltpu.CompilerParams(vmem_limit_bytes=grant)


def in_vmem(n):
    return [pl.BlockSpec(memory_space=pltpu.VMEM)] * n


def in_smem(n):
    return [pl.BlockSpec(memory_space=pltpu.SMEM)] * n


def forward_kernel(
    n_ctx, qblk, pair_ref, me_ref, x_ref, w_ref, turn_ref, kept_ref, r_ref, o_ref, lse_ref, acc_ref
):
    q_ref, k_ref, v_ref = (kept_ref.at[i] for i in range(3))
    cos_ref, sin_ref = turn_ref.at[0], turn_ref.at[1]
    length, cols = q_ref.shape
    blk = length // (2 * n_ctx)
    heads = cols // HEAD_DIM
    for at in range(n_ctx):
        x = x_ref[pl.ds(at * 2 * blk, 2 * blk), :]
        x_f = x.astype(F32)
        scale = lax.rsqrt(jnp.mean(x_f * x_f, axis=1, keepdims=True) + EPS)
        r_ref[pl.ds(at * 2 * blk, 2 * blk), :] = scale
        qkv = mm(x, w_ref[...]) * scale
        for second in range(2):
            to = pl.ds(pl.multiple_of(slot_block(pair_ref, me_ref, 2 * at + second, n_ctx) * blk, blk), blk)
            cosine, sine = cos_ref[to, :], sin_ref[to, :]
            query = qkv[second * blk : (second + 1) * blk, :cols]
            key = qkv[second * blk : (second + 1) * blk, cols : 2 * cols]
            q_ref[to, :] = (query * cosine + swap_halves(query) * sine).astype(BF)
            k_ref[to, :] = (key * cosine + swap_halves(key) * sine).astype(BF)
            v_ref[to, :] = qkv[second * blk : (second + 1) * blk, 2 * cols :].astype(BF)
    acc_ref[...] = jnp.zeros_like(acc_ref)
    lse_ref[...] = jnp.zeros_like(lse_ref)

    def one_head(head, carry):
        mask = head_mask((qblk, cols), head)
        here = lax.broadcasted_iota(jnp.int32, (qblk, lse_ref.shape[1]), 1) == head
        below = lax.broadcasted_iota(jnp.int32, (qblk, qblk), 1) <= lax.broadcasted_iota(jnp.int32, (qblk, qblk), 0)
        for i in range(length // qblk):
            rows = pl.ds(i * qblk, qblk)
            query = jnp.where(mask, q_ref[rows, :], jnp.zeros((), BF))
            last = jnp.where(below, mm_t(query, k_ref[rows, :]), NEG)
            peak = jnp.max(last, axis=1, keepdims=True)
            if i:
                before = mm_t(query, k_ref[: i * qblk, :])
                peak = jnp.maximum(peak, jnp.max(before, axis=1, keepdims=True))
            shift = peak * SCALE
            last = jnp.exp(last * SCALE - shift)
            total = jnp.sum(last, axis=1, keepdims=True)
            out = mm(last.astype(BF), v_ref[rows, :])
            if i:
                before = jnp.exp(before * SCALE - shift)
                total += jnp.sum(before, axis=1, keepdims=True)
                out += mm(before.astype(BF), v_ref[: i * qblk, :])
            acc_ref[rows, :] = jnp.where(mask, out * (1.0 / total), acc_ref[rows, :])
            lse_ref[rows, :] = jnp.where(here, shift + jnp.log(total), lse_ref[rows, :])
        return carry

    lax.fori_loop(0, heads, one_head, 0)
    for slot in range(2 * n_ctx):
        at = pl.multiple_of(slot_block(pair_ref, me_ref, slot, n_ctx) * blk, blk)
        o_ref[pl.ds(slot * blk, blk), :] = acc_ref[pl.ds(at, blk), :].astype(BF)
    kept_ref[3] = acc_ref[...].astype(BF)


def attention_forward(pair, me, tokens, weight, turn):
    _, length, cols = turn.shape
    width = weight.shape[0]
    n_ctx = width // cols
    return pl.pallas_call(
        functools.partial(forward_kernel, n_ctx, 256),
        out_shape=[
            jax.ShapeDtypeStruct((4, length, cols), BF),
            jax.ShapeDtypeStruct((length, 1), F32),
            jax.ShapeDtypeStruct((length, cols), BF),
            jax.ShapeDtypeStruct((length, 128), F32),
        ],
        in_specs=in_smem(2) + in_vmem(3),
        out_specs=in_vmem(4),
        scratch_shapes=[pltpu.VMEM((length, cols), F32)],
        compiler_params=params(VMEM_LIMIT),
        cost_estimate=LIGHT,
        name="attention_forward",
    )(pair, me, tokens, weight, turn)


def backward_kernel(
    n_ctx, qblk, pair_ref, me_ref, do_ref, kept_ref, r_ref, lse_ref, turn_ref,
    g_ref, gr_ref, go_ref, dq_ref, dk_ref, dv_ref, centre_ref,
):
    q_ref, k_ref, v_ref, o_ref = (kept_ref.at[i] for i in range(4))
    cos_ref, sin_ref = turn_ref.at[0], turn_ref.at[1]
    length, cols = q_ref.shape
    blk = length // (2 * n_ctx)
    heads = cols // HEAD_DIM
    for slot in range(2 * n_ctx):
        at = pl.multiple_of(slot_block(pair_ref, me_ref, slot, n_ctx) * blk, blk)
        go_ref[pl.ds(at, blk), :] = do_ref[pl.ds(slot * blk, blk), :]
    dq_ref[...] = jnp.zeros_like(dq_ref)
    dk_ref[...] = jnp.zeros_like(dk_ref)
    dv_ref[...] = jnp.zeros_like(dv_ref)

    pick = head_mask((8, cols), lax.broadcasted_iota(jnp.int32, (8, cols), 0)).astype(F32)
    centre_ref[...] = lax.dot_general(
        pick,
        go_ref[...].astype(F32) * o_ref[...].astype(F32),
        (((1,), (1,)), ((), ())),
        precision=lax.Precision.HIGHEST,
        preferred_element_type=F32,
    )

    def one_head(head, carry):
        mask = head_mask((qblk, cols), head)
        below = lax.broadcasted_iota(jnp.int32, (qblk, qblk), 0) <= lax.broadcasted_iota(jnp.int32, (qblk, qblk), 1)
        for i in range(length // qblk):
            rows = pl.ds(i * qblk, qblk)
            query = jnp.where(mask, q_ref[rows, :], jnp.zeros((), BF))
            grad = jnp.where(mask, go_ref[rows, :], jnp.zeros((), BF))
            lse = lse_ref[pl.ds(head, 1), rows]
            centre = centre_ref[pl.ds(head, 1), rows]
            out = None
            for at, size in ((i * qblk, qblk), (0, i * qblk)):
                if not size:
                    continue
                keys = pl.ds(at, size)
                probs = jnp.exp(mm_t(k_ref[keys, :], query) * SCALE - lse)
                if at or not i:
                    probs = jnp.where(below, probs, 0.0)
                grad_probs = mm_t(v_ref[keys, :], grad)
                grad_scores = (probs * (grad_probs - centre)).astype(BF)
                dk_ref[keys, :] += mm(grad_scores, query)
                dv_ref[keys, :] += mm(probs.astype(BF), grad)
                term = t_mm(grad_scores, k_ref[keys, :])
                out = term if out is None else out + term
            dq_ref[rows, :] = jnp.where(mask, out, dq_ref[rows, :])
        return carry

    lax.fori_loop(0, heads, one_head, 0)
    for slot in range(2 * n_ctx):
        at = pl.multiple_of(slot_block(pair_ref, me_ref, slot, n_ctx) * blk, blk)
        rows = pl.ds(slot * blk, blk)
        to = pl.ds(at, blk)
        cosine, sine = cos_ref[to, :], sin_ref[to, :]
        scale = r_ref[rows, :]
        query = (dq_ref[to, :] * SCALE).astype(BF).astype(F32)
        key = (dk_ref[to, :] * SCALE).astype(BF).astype(F32)
        value = dv_ref[to, :].astype(BF).astype(F32)
        query = query * cosine - swap_halves(query) * sine
        key = key * cosine - swap_halves(key) * sine
        for at_col, part in enumerate((query, key, value)):
            span = pl.ds(at_col * cols, cols)
            g_ref[rows, span] = part.astype(BF)
            gr_ref[rows, span] = (part * scale).astype(BF)


def attention_backward(pair, me, n_ctx, grad, kept, scale, lse, turn):
    _, length, cols = turn.shape
    return pl.pallas_call(
        functools.partial(backward_kernel, n_ctx, 256),
        out_shape=[jax.ShapeDtypeStruct((length, 3 * cols), BF)] * 2,
        in_specs=in_smem(2) + in_vmem(5),
        out_specs=in_vmem(2),
        scratch_shapes=[pltpu.VMEM((length, cols), BF)]
        + [pltpu.VMEM((length, cols), F32)] * 3
        + [pltpu.VMEM((8, length), F32)],
        compiler_params=params(),
        cost_estimate=LIGHT,
        name="attention_backward",
    )(pair, me, grad, kept, scale, lse, turn)


def feed_forward_kernel(
    core_ref, n_ref, c_ref, g_ref, u_ref, d_ref, h_ref, dg_ref, du_ref, theirs_ref, mine_ref
):
    rows, cot = n_ref[...], c_ref[...]
    hid, tile = g_ref.shape[1], 256
    for at in range(0, hid, tile):
        span = slice(at, at + tile)
        gate = mm(rows, g_ref[:, span])
        up = mm(rows, u_ref[:, span])
        grad = mm_t(cot, d_ref[span, :])
        sig = 1.0 / (1.0 + jnp.exp(-gate))
        active = gate * sig
        h_ref[:, span] = (active * up).astype(BF)
        dg_ref[:, span] = (grad * up * sig * (1.0 + gate * (1.0 - sig))).astype(BF)
        du_ref[:, span] = (grad * active).astype(BF)
    back = (mm_t(dg_ref[...], g_ref[...]) + mm_t(du_ref[...], u_ref[...])).astype(BF)
    first = pl.program_id(0) < pl.num_programs(0) // 2

    @pl.when(first)
    def _():
        theirs_ref[...] = back

    @pl.when(jnp.logical_not(first))
    def _():
        mine_ref[...] = back


def feed_forward(normed, cotangent, gate_w, up_w, down_w):
    count, width = normed.shape
    hid = gate_w.shape[1]
    tile = 256
    half = count // tile // 2

    def rows_of(r, core):
        return (jnp.where(r < half, (1 - core[0]) * half + r, core[0] * half + r - half), 0)

    def fixed(r, core):
        return (0, 0)

    once = pl.Buffered(1)
    return pl.pallas_call(
        feed_forward_kernel,
        grid_spec=pltpu.PrefetchScalarGridSpec(
            num_scalar_prefetch=1,
            grid=(2 * half,),
            in_specs=[
                pl.BlockSpec((tile, width), rows_of),
                pl.BlockSpec((tile, width), rows_of),
                pl.BlockSpec((width, hid), fixed, pipeline_mode=once),
                pl.BlockSpec((width, hid), fixed, pipeline_mode=once),
                pl.BlockSpec((hid, width), fixed, pipeline_mode=once),
            ],
            out_specs=[pl.BlockSpec((tile, hid), rows_of)] * 3
            + [
                pl.BlockSpec((tile, width), lambda r, core: (jnp.minimum(r, half - 1), 0)),
                pl.BlockSpec((tile, width), lambda r, core: (jnp.maximum(r - half, 0), 0)),
            ],
        ),
        out_shape=[jax.ShapeDtypeStruct((count, hid), BF)] * 3
        + [jax.ShapeDtypeStruct((count // 2, width), BF)] * 2,
        compiler_params=params(VMEM_LIMIT),
        cost_estimate=LIGHT,
        name="feed_forward",
    )(lax.axis_index("core").astype(jnp.int32)[None], normed, cotangent, gate_w, up_w, down_w)


def branch_kernel(core_ref, h_ref, d_ref, theirs_ref, mine_ref):
    out = mm(h_ref[...], d_ref[...]).astype(BF)
    first = pl.program_id(0) < pl.num_programs(0) // 2

    @pl.when(first)
    def _():
        theirs_ref[...] = out

    @pl.when(jnp.logical_not(first))
    def _():
        mine_ref[...] = out


def branch_rows(hidden, down_w):
    count, hid = hidden.shape
    width = down_w.shape[1]
    tile = 256
    half = count // tile // 2
    return pl.pallas_call(
        branch_kernel,
        grid_spec=pltpu.PrefetchScalarGridSpec(
            num_scalar_prefetch=1,
            grid=(2 * half,),
            in_specs=[
                pl.BlockSpec(
                    (tile, hid),
                    lambda r, core: (jnp.where(r < half, (1 - core[0]) * half + r, core[0] * half + r - half), 0),
                ),
                pl.BlockSpec((hid, width), lambda r, core: (0, 0), pipeline_mode=pl.Buffered(1)),
            ],
            out_specs=[
                pl.BlockSpec((tile, width), lambda r, core: (jnp.minimum(r, half - 1), 0)),
                pl.BlockSpec((tile, width), lambda r, core: (jnp.maximum(r - half, 0), 0)),
            ],
        ),
        out_shape=[jax.ShapeDtypeStruct((count // 2, width), BF)] * 2,
        compiler_params=params(),
        cost_estimate=LIGHT,
        name="branch_rows",
    )(lax.axis_index("core").astype(jnp.int32)[None], hidden, down_w)


def merge_kernel(a_ref, m_ref, *refs):
    *b_refs, go_ref, out_ref, all_ref = refs
    rows = b_refs[0].shape[0]
    for at, ref in enumerate(b_refs):
        all_ref[pl.ds(at * rows, rows), :] = ref[...]
    go_ref[...] = mm_t(all_ref[...], m_ref[...]).astype(BF)
    out_ref[...] = t_mm(a_ref[...], all_ref[...]).astype(BF)


def merge_terms(attended, merge_rows, pieces):
    length, cols = attended.shape
    width = merge_rows.shape[1]
    return pl.pallas_call(
        merge_kernel,
        out_shape=[jax.ShapeDtypeStruct((length, cols), BF), jax.ShapeDtypeStruct((cols, width), BF)],
        in_specs=in_vmem(2 + len(pieces)),
        out_specs=in_vmem(2),
        scratch_shapes=[pltpu.VMEM((length, width), BF)],
        compiler_params=params(),
        cost_estimate=LIGHT,
        name="merge_terms",
    )(attended, merge_rows, *pieces)


def heads_term_kernel(x_ref, g_ref, out_ref):
    out_ref[...] = mm(x_ref[...], g_ref[...]).astype(BF)


def heads_term(tokens_t, grad):
    width, count = tokens_t.shape
    cols = grad.shape[1]
    tile = 512
    return pl.pallas_call(
        heads_term_kernel,
        grid=(width // tile,),
        in_specs=[
            pl.BlockSpec((tile, count), lambda i: (i, 0)),
            pl.BlockSpec((count, cols), lambda i: (0, 0), pipeline_mode=pl.Buffered(1)),
        ],
        out_specs=pl.BlockSpec((tile, cols), lambda i: (i, 0)),
        out_shape=jax.ShapeDtypeStruct((width, cols), BF),
        compiler_params=params(),
        cost_estimate=LIGHT,
        name="heads_term",
    )(tokens_t, grad)


def weight_rows_kernel(at_ref, left_ref, right_ref, *out_refs):
    out = t_mm(left_ref[...], right_ref[...]).astype(BF)
    for i, ref in enumerate(out_refs):

        @pl.when(pl.program_id(0) == i)
        def _(ref=ref):
            ref[...] = out


def weight_rows(left, right, index, size):
    count, n = left.shape[0], len(index)
    width = right.shape[1]
    return pl.pallas_call(
        weight_rows_kernel,
        grid_spec=pltpu.PrefetchScalarGridSpec(
            num_scalar_prefetch=1,
            grid=(n,),
            in_specs=[
                pl.BlockSpec((count, size), lambda i, at: (0, at[i])),
                pl.BlockSpec((count, width), lambda i, at: (0, 0), pipeline_mode=pl.Buffered(1)),
            ],
            out_specs=[pl.BlockSpec((size, width), lambda i, at: (0, 0), pipeline_mode=pl.Buffered(1))] * n,
        ),
        out_shape=[jax.ShapeDtypeStruct((size, width), BF)] * n,
        compiler_params=params(),
        cost_estimate=LIGHT,
        name="weight_rows",
    )(jnp.stack(index).astype(jnp.int32), left, right)


def back_kernel(g_ref, w_ref, out_ref):
    out_ref[...] = mm_t(g_ref[...], w_ref[...]).astype(BF)


def back_rows(grad, weight, half):
    count, cols = grad.shape
    width = weight.shape[0]
    tile = 256
    steps = count // 2 // tile
    return pl.pallas_call(
        back_kernel,
        grid=(steps,),
        in_specs=[
            pl.BlockSpec((tile, cols), lambda r: (half * steps + r, 0)),
            pl.BlockSpec((width, cols), lambda r: (0, 0), pipeline_mode=pl.Buffered(1)),
        ],
        out_specs=pl.BlockSpec((tile, width), lambda r: (r, 0)),
        out_shape=jax.ShapeDtypeStruct((count // 2, width), BF),
        compiler_params=params(),
        cost_estimate=LIGHT,
        name="back_rows",
    )(grad, weight)


def fold_heads_kernel(q_ref, k_ref, v_ref, gain_ref, out_ref):
    n_ctx, _, cols = out_ref.shape
    cols //= 3
    gain = gain_ref[...]
    for at, ref in enumerate((q_ref, k_ref, v_ref)):
        for to in range(n_ctx):
            part = ref[:, to * cols : (to + 1) * cols].astype(F32) * gain
            out_ref[to, :, at * cols : (at + 1) * cols] = part.astype(BF)


def fold_heads(weights, gain, n_ctx):
    rows, width = weights[0].shape
    return pl.pallas_call(
        fold_heads_kernel,
        out_shape=jax.ShapeDtypeStruct((n_ctx, rows, 3 * (width // n_ctx)), BF),
        in_specs=in_vmem(4),
        out_specs=pl.BlockSpec(memory_space=pltpu.VMEM),
        compiler_params=params(),
        cost_estimate=LIGHT,
        name="fold_heads",
    )(*weights, gain)


def unfold_heads_kernel(s_ref, q_ref, k_ref, v_ref, gain_ref, dq_ref, dk_ref, dv_ref, first_ref):
    n_ctx, rows, cols = s_ref.shape
    cols //= 3
    gain = gain_ref[...]
    total = jnp.zeros((rows, cols), F32)
    for at, (ref, out) in enumerate(((q_ref, dq_ref), (k_ref, dk_ref), (v_ref, dv_ref))):
        for to in range(n_ctx):
            span = slice(to * cols, (to + 1) * cols)
            part = s_ref[to, :, at * cols : (at + 1) * cols].astype(F32)
            total += part * ref[:, span].astype(F32)
            out[:, span] = part * gain
    first_ref[...] = jnp.sum(total, axis=1, keepdims=True)


def unfold_heads(sums, weights, gain):
    rows, width = weights[0].shape
    return pl.pallas_call(
        unfold_heads_kernel,
        out_shape=[jax.ShapeDtypeStruct((rows, width), F32)] * 3 + [jax.ShapeDtypeStruct((rows, 1), F32)],
        in_specs=in_vmem(5),
        out_specs=in_vmem(4),
        compiler_params=params(),
        cost_estimate=LIGHT,
        name="unfold_heads",
    )(sums, *weights, gain)


def fold_hidden_kernel(piece, w_ref, gain_ref, out_ref):
    n_core, n_fsdp, _, hid = out_ref.shape
    gain = gain_ref[...]
    for plane in range(hid // piece):
        for core in range(n_core):
            for line in range(n_fsdp):
                at = ((plane * n_core + core) * n_fsdp + line) * piece
                part = w_ref[:, at : at + piece].astype(F32) * gain
                out_ref[core, line, :, plane * piece : (plane + 1) * piece] = part.astype(BF)


def fold_hidden(weight, gain, n_plane, n_core, n_fsdp):
    rows, total = weight.shape
    piece = total // (n_plane * n_core * n_fsdp)
    if piece % 128:
        folded = (weight.astype(F32) * gain).astype(BF).reshape(rows, n_plane, n_core, n_fsdp, piece)
        return folded.transpose(2, 3, 0, 1, 4).reshape(n_core, n_fsdp, rows, n_plane * piece)
    return pl.pallas_call(
        functools.partial(fold_hidden_kernel, piece),
        out_shape=jax.ShapeDtypeStruct((n_core, n_fsdp, rows, n_plane * piece), BF),
        in_specs=in_vmem(2),
        out_specs=pl.BlockSpec(memory_space=pltpu.VMEM),
        compiler_params=params(),
        cost_estimate=LIGHT,
        name="fold_hidden",
    )(weight, gain)


def unfold_hidden_kernel(piece, at_ref, *refs):
    *s_refs, w_ref, gain_ref, out_ref, second_ref = refs
    n_fsdp = len(s_refs)
    n_core, rows, hid = s_refs[0].shape
    gain = gain_ref[...]
    total = jnp.zeros((rows, piece), F32)
    for mask, ref in enumerate(s_refs):
        line = jnp.bitwise_xor(at_ref[1], mask)
        for other in range(n_core):
            core = jnp.bitwise_xor(at_ref[0], other)
            for plane in range(hid // piece):
                at = ((plane * n_core + core) * n_fsdp + line) * piece
                span = pl.ds(pl.multiple_of(at, piece), piece)
                part = ref[other, :, plane * piece : (plane + 1) * piece].astype(F32)
                total += part * w_ref[:, span].astype(F32)
                out_ref[:, span] = part * gain
    second_ref[...] = jnp.sum(total, axis=1, keepdims=True)


def unfold_hidden(pieces, weight, gain, n_plane):
    rows, total = weight.shape
    n_core, _, hid = pieces[0].shape
    n_fsdp = len(pieces)
    piece = hid // n_plane
    core, line = lax.axis_index("core"), lax.axis_index("fsdp")
    if piece % 128:
        out = jnp.zeros((rows, n_plane, n_core, n_fsdp, piece), BF)
        for mask, block in enumerate(pieces):
            for other in range(n_core):
                part = block[other].reshape(rows, n_plane, 1, 1, piece)
                out = lax.dynamic_update_slice(out, part, (0, 0, core ^ other, line ^ mask, 0))
        out = out.reshape(rows, total).astype(F32)
        return out * gain, jnp.sum(out * weight.astype(F32), axis=1, keepdims=True)
    return pl.pallas_call(
        functools.partial(unfold_hidden_kernel, piece),
        out_shape=[jax.ShapeDtypeStruct((rows, total), F32), jax.ShapeDtypeStruct((rows, 1), F32)],
        in_specs=in_smem(1) + in_vmem(n_fsdp + 2),
        out_specs=in_vmem(2),
        compiler_params=params(),
        cost_estimate=LIGHT,
        name="unfold_hidden",
    )(jnp.stack([core, line]).astype(jnp.int32), *pieces, weight, gain)


def place_kernel(at_ref, *refs):
    *p_refs, out_ref = refs
    for i, ref in enumerate(p_refs):
        out_ref[at_ref[i]] = ref[...]


def place(pieces, index, room=None):
    n = len(pieces)
    moved = 2 * n * pieces[0].size * pieces[0].dtype.itemsize
    return pl.pallas_call(
        place_kernel,
        out_shape=jax.ShapeDtypeStruct((room or n,) + pieces[0].shape, pieces[0].dtype),
        in_specs=in_smem(1) + in_vmem(n),
        out_specs=pl.BlockSpec(memory_space=pltpu.VMEM),
        compiler_params=params(VMEM_LIMIT),
        cost_estimate=LIGHT,
        name="place",
    )(jnp.stack(index).astype(jnp.int32), *pieces)


def gather(value, axes, axis=0):
    return lax.all_gather(value, axes, axis=axis, tiled=True)


def scatter(value, axes):
    return lax.psum_scatter(value, axes, scatter_dimension=0, tiled=True)


def exchange(value, axes):
    return lax.all_to_all(value, axes, split_axis=0, concat_axis=0, tiled=True)


def together(values):
    return lax.optimization_barrier(values)


def core_swap(value):
    n = lax.axis_size("plane") * 2
    return lax.ppermute(value, CTX, [(i, i ^ 1) for i in range(n)])


def plane_step(value, step):
    steps, _ = relative(lax.axis_size("plane"))
    n = lax.axis_size("plane") * 2
    return lax.ppermute(value, CTX, [(i, i ^ (2 * steps[i % 2][step])) for i in range(n)])


def line_swap(value, mask):
    n = lax.axis_size("fsdp")
    return lax.ppermute(value, "fsdp", [(i, i ^ mask) for i in range(n)])


def plane_gather_more(pieces):
    step = len(pieces).bit_length() - 1
    return pieces + [plane_step(piece, step) for piece in pieces]


def plane_gather(value):
    pieces = [value]
    while len(pieces) < lax.axis_size("plane"):
        pieces = plane_gather_more(pieces)
    return pieces


def plane_send(chunks):
    n = len(chunks) // 2
    return [plane_step(chunk, n.bit_length() - 1) for chunk in chunks[n:]]


def plane_add(chunks, came):
    return [(mine.astype(F32) + chunk.astype(F32)).astype(BF) for mine, chunk in zip(chunks, came)]


def plane_scatter(chunks):
    while len(chunks) > 1:
        chunks = plane_add(chunks, plane_send(chunks))
    return chunks[0]


def plane_index():
    _, order = relative(lax.axis_size("plane"))
    core = lax.axis_index("core")
    plane = lax.axis_index("plane")
    return [plane ^ jnp.where(core == 0, a, b) for a, b in zip(*order)]


def part(value, at, size, axis):
    return lax.dynamic_slice_in_dim(value, at * size, size, axis)


def ctx_gather(value):
    mine = plane_gather(value)
    return mine + [core_swap(piece) for piece in mine]


def ctx_scatter(theirs, mine, n_plane):
    total = (mine.astype(F32) + core_swap(theirs).astype(F32)).astype(BF)
    rows = total.shape[0] // n_plane
    return plane_scatter([total[i * rows : (i + 1) * rows] for i in range(n_plane)])


def cores_pair(value):
    core = lax.axis_index("core")
    kept = lax.dynamic_index_in_dim(value, core, 0, keepdims=False)
    return kept, core_swap(lax.dynamic_index_in_dim(value, 1 - core, 0, keepdims=False))


def lines_parts(pair):
    line = lax.axis_index("fsdp")
    return [
        jnp.stack([lax.dynamic_index_in_dim(v, line ^ mask, 0, keepdims=False) for v in pair])
        for mask in range(lax.axis_size("fsdp"))
    ]


def lines_swap(parts):
    return parts[:1] + [line_swap(parts[mask], mask) for mask in range(1, len(parts))]


def lines_pair(pair):
    return lines_swap(lines_parts(pair))


def line_rows_kernel(at_ref, *refs):
    *p_refs, out_ref = refs
    n_fsdp = len(p_refs)
    for mask, ref in enumerate(p_refs):
        line = jnp.bitwise_xor(at_ref[1], mask)
        for other in range(2):
            core = jnp.bitwise_xor(at_ref[0], other)
            out_ref[core * n_fsdp + line] = ref[other]


def line_rows(pieces):
    n = 2 * len(pieces)
    at = jnp.stack([lax.axis_index("core"), lax.axis_index("fsdp")]).astype(jnp.int32)
    return pl.pallas_call(
        line_rows_kernel,
        out_shape=jax.ShapeDtypeStruct((n,) + pieces[0].shape[1:], pieces[0].dtype),
        in_specs=in_smem(1) + in_vmem(len(pieces)),
        out_specs=pl.BlockSpec(memory_space=pltpu.VMEM),
        compiler_params=params(VMEM_LIMIT),
        cost_estimate=LIGHT,
        name="line_rows",
    )(at, *pieces)


def on_device(
    layer_input, pairing, query_weight, key_weight, value_weight, merge_weight,
    gate_weight, up_weight, down_weight, norm_first, norm_second, output_cotangent,
):
    n_plane = lax.axis_size("plane")
    n_core = lax.axis_size("core")
    n_fsdp = lax.axis_size("fsdp")
    n_ctx = n_plane * n_core
    n_tok = n_core * n_fsdp
    me = jnp.stack([lax.axis_index("plane"), lax.axis_index("core")]).astype(jnp.int32)
    index = plane_index()
    _, rows, width = layer_input.shape
    length = rows * n_ctx
    half = length // 2
    cols = width // n_ctx
    dev_rows = gate_weight.shape[0]
    piece = gate_weight.shape[1] // (n_ctx * n_fsdp)
    hid = piece * n_plane
    d_rows = n_tok * dev_rows
    tokens = layer_input.reshape(rows, width)
    cotangent = output_cotangent.reshape(rows, width)
    gain_first = norm_first.astype(F32)[:, None]
    gain_second = norm_second.astype(F32)[:, None]
    projections = (query_weight, key_weight, value_weight)

    merge_rows = gather(merge_weight, "fsdp")
    gate_moved = lines_pair(cores_pair(fold_hidden(gate_weight, gain_second, n_plane, n_core, n_fsdp)))
    own = exchange(fold_heads(projections, gain_first, n_ctx), CTX)
    x_pieces = ctx_gather(tokens)
    up_pair = cores_pair(fold_hidden(up_weight, gain_second, n_plane, n_core, n_fsdp))
    turn = jnp.stack(rope_tables(length, cols))
    own, gate_moved, x_pieces, up_pair, merge_rows = together(
        (own, gate_moved, x_pieces, up_pair, merge_rows)
    )
    qkv_weight = gather(own[:, None], "fsdp", axis=1).reshape(width, 3 * cols)
    gate_pieces = plane_gather(line_rows(gate_moved).reshape(d_rows, hid))
    down_pieces = plane_gather_more([down_weight])
    x_all = jnp.concatenate(x_pieces, axis=0)
    x_all, gate_pieces, down_pieces = together((x_all, gate_pieces, down_pieces))
    up_moved = lines_pair(up_pair)
    cot_all = gather(cotangent, TOK)

    kept, scale_all, attended, lse = attention_forward(pairing, me, x_all, qkv_weight, turn)
    while len(down_pieces) < n_plane:
        down_pieces = plane_gather_more(down_pieces)
    attended, down_pieces = together((attended, down_pieces))
    down_rows = place(down_pieces, index).reshape(hid, width)
    own_f = tokens.astype(F32)
    theirs = together(mm(attended[half:], merge_rows).astype(BF))
    mine = together(mm(attended[:half], merge_rows).astype(BF))
    mixed = own_f + ctx_scatter(theirs, mine, n_plane)
    lse_rows = lse[:, :8].T
    x_t = x_all.reshape(length, n_ctx, n_fsdp, dev_rows).transpose(2, 1, 3, 0).reshape(width, length)
    gate_rows = place(gate_pieces, index).reshape(width, hid)
    mixed, up_moved, lse_rows, x_t, down_rows, gate_rows = together(
        (mixed, up_moved, lse_rows, x_t, down_rows, gate_rows)
    )
    up_pieces = plane_gather(line_rows(up_moved).reshape(d_rows, hid))
    up_rows = place(up_pieces[:-1], index[:-1], n_plane)
    up_rows = lax.dynamic_update_slice(up_rows, up_pieces[-1][None], (index[-1], 0, 0)).reshape(width, hid)

    scale_second = lax.rsqrt(jnp.mean(mixed * mixed, axis=-1, keepdims=True) + EPS)
    unit_second = mixed * scale_second
    normed_all = gather(unit_second.astype(BF), TOK)
    hidden, grad_gate, grad_up, theirs, mine = feed_forward(
        normed_all, cot_all, gate_rows, up_rows, down_rows
    )
    e_two = (mine.astype(F32) + core_swap(theirs).astype(F32)).astype(BF)

    hidden, grad_gate, grad_up, e_two = together((hidden, grad_gate, grad_up, e_two))
    gate_late = weight_rows(normed_all, grad_gate, index[n_plane // 2 :], d_rows)
    gate_chunks = list(weight_rows(normed_all, grad_gate, index[: n_plane // 2], d_rows)) + list(gate_late)
    gate_came = plane_send(gate_chunks)
    up_chunks = [together(t_mm(part(normed_all, at, d_rows, 1), grad_up).astype(BF)) for at in index]
    theirs, mine = branch_rows(hidden, down_rows)
    gate_chunks, gate_came, up_chunks, theirs, mine = together(
        (gate_chunks, gate_came, up_chunks, theirs, mine)
    )
    gate_chunks = plane_add(gate_chunks, gate_came)
    branch = (mine.astype(F32) + core_swap(theirs).astype(F32)).astype(BF)
    e_two = scatter(e_two, "fsdp")
    e_two, gate_chunks, up_chunks, branch = together((e_two, gate_chunks, up_chunks, branch))
    branch_sum = scatter(branch, "fsdp")
    gate_sum = plane_scatter(gate_chunks)
    e_two_f = e_two.astype(F32)
    grad_mixed = cotangent.astype(F32) + scale_second * (
        e_two_f - unit_second * jnp.mean(e_two_f * unit_second, axis=-1, keepdims=True)
    )
    branch_pieces = plane_gather_more([grad_mixed.astype(BF)])
    branch_pieces, gate_sum = together((branch_pieces, gate_sum))
    gate_parts = lines_parts(cores_pair(gate_sum.reshape(n_core, n_fsdp, dev_rows, hid)))
    while len(branch_pieces) < n_plane:
        branch_pieces = plane_gather_more(branch_pieces)
    branch_pieces = branch_pieces + [core_swap(value) for value in branch_pieces]
    gate_back = lines_swap(gate_parts)

    branch_pieces, up_chunks = together((branch_pieces, up_chunks))
    up_came = plane_send(up_chunks)
    grad_attended, merge_grad = merge_terms(attended, merge_rows, branch_pieces)
    merge_grad, grad_attended = together((merge_grad, grad_attended))
    merge_grad = scatter(merge_grad, "fsdp")
    grad_qkv, grad_scaled = attention_backward(
        pairing, me, n_ctx, grad_attended, kept, scale_all, lse_rows, turn
    )
    grad_scaled, branch_sum = together((grad_scaled, branch_sum))
    sums = heads_term(x_t, grad_scaled)
    grad_qkv, up_chunks, up_came, gate_back, sums, merge_grad, branch_sum = together(
        (grad_qkv, up_chunks, up_came, gate_back, sums, merge_grad, branch_sum)
    )
    sums = scatter(sums, "fsdp")
    up_sum = plane_scatter(plane_add(up_chunks, up_came))
    layer_output = (mixed + branch_sum.astype(F32)).astype(BF)
    theirs = back_rows(grad_qkv, qkv_weight, 1)
    mine = back_rows(grad_qkv, qkv_weight, 0)
    e_one = ctx_scatter(theirs, mine, n_plane)
    up_parts = lines_parts(cores_pair(up_sum.reshape(n_core, n_fsdp, dev_rows, hid)))
    hidden, mine = together((hidden, mine))
    down_chunks = [together(t_mm(part(hidden, at, piece, 1), cot_all).astype(BF)) for at in index]
    e_one, down_chunks = together((e_one, down_chunks))
    down_came = plane_send(down_chunks)
    sums, up_parts, merge_grad = together((sums, up_parts, merge_grad.astype(F32)))
    up_back = lines_swap(up_parts)
    sums = exchange(sums.reshape(n_ctx, dev_rows, 3 * cols), CTX)
    query_grad, key_grad, value_grad, first_grad = unfold_heads(sums, projections, gain_first)
    query_grad, key_grad, value_grad, first_grad, up_back = together(
        (query_grad, key_grad, value_grad, first_grad, up_back)
    )
    scale_first = lax.rsqrt(jnp.mean(own_f * own_f, axis=-1, keepdims=True) + EPS)
    unit_first = own_f * scale_first
    input_grad = (
        grad_mixed
        + scale_first * (e_one - unit_first * jnp.mean(e_one * unit_first, axis=-1, keepdims=True))
    ).astype(BF)
    down_grad = plane_scatter(plane_add(down_chunks, down_came)).astype(F32)
    gate_grad, second_gate = unfold_hidden(gate_back, gate_weight, gain_second, n_plane)
    up_grad, second_up = unfold_hidden(up_back, up_weight, gain_second, n_plane)
    second_grad = (second_gate + second_up)[:, 0]
    return (
        layer_output.reshape(1, rows, width),
        input_grad.reshape(1, rows, width),
        query_grad,
        key_grad,
        value_grad,
        merge_grad,
        gate_grad,
        up_grad,
        down_grad,
        first_grad[:, 0],
        second_grad,
    )


def solution(mesh):
    n_ctx, n_fsdp = mesh.shape["ctx"], mesh.shape["fsdp"]
    inner = Mesh(mesh.devices.reshape(n_ctx // 2, 2, n_fsdp), ("plane", "core", "fsdp"))
    token = P("fsdp", CTX, None)
    weight = P(("plane", "core", "fsdp"), None)
    gain = P(("plane", "core", "fsdp"))
    return jax.shard_map(
        on_device,
        mesh=inner,
        in_specs=(token, P("fsdp", None)) + (weight,) * 7 + (gain, gain, token),
        out_specs=(token, token) + (weight,) * 7 + (gain, gain),
        check_vma=False,
    )
```

```python
import functools

import jax
import jax.numpy as jnp
from jax import lax
from jax.experimental import pallas as pl
from jax.experimental.pallas import tpu as pltpu
from jax.sharding import Mesh, PartitionSpec as P

HEAD_DIM = 64
THETA = 130000.0
EPS = 1e-05
SCALE = HEAD_DIM**-0.5
NEG = -1e30
BF = jnp.bfloat16
F32 = jnp.float32
CTX = ("plane", "core")
TOK = ("core", "fsdp")
VMEM_LIMIT = 56 * 1024 * 1024
VMEM_SMALL = 30 * 1024 * 1024
LIGHT = pl.CostEstimate(flops=1024, bytes_accessed=1024, transcendentals=0)


def mm(left, right):
    return jnp.dot(left, right, preferred_element_type=F32)


def mm_t(left, right):
    return lax.dot_general(left, right, (((1,), (1,)), ((), ())), preferred_element_type=F32)


def t_mm(left, right):
    return lax.dot_general(left, right, (((0,), (0,)), ((), ())), preferred_element_type=F32)


def rope_tables(length, cols):
    half = HEAD_DIM // 2
    freq = THETA ** (-2.0 * jnp.arange(half, dtype=F32) / HEAD_DIM)
    angle = jnp.arange(length, dtype=jnp.int32).astype(F32)[:, None] * freq
    cosine, sine = jnp.cos(angle), jnp.sin(angle)
    heads = cols // HEAD_DIM
    return (
        jnp.tile(jnp.concatenate([cosine, cosine], axis=1), (1, heads)),
        jnp.tile(jnp.concatenate([-sine, sine], axis=1), (1, heads)),
    )


def swap_halves(values):
    cols = values.shape[1]
    half = HEAD_DIM // 2
    lane = lax.broadcasted_iota(jnp.int32, values.shape, 1)
    up = pltpu.roll(values, half, 1)
    down = pltpu.roll(values, cols - half, 1)
    return jnp.where(lane % HEAD_DIM < half, down, up)


def relative(n_plane):
    bits = n_plane.bit_length() - 1
    steps = [[1 << ((s + c) % bits) for s in range(bits)] for c in range(2)]
    order = []
    for masks in steps:
        found = [0]
        for mask in masks:
            found += [m ^ mask for m in found]
        order.append(found)
    return steps, order


def slot_block(pair_ref, me_ref, slot, n_ctx):
    _, order = relative(n_ctx // 2)
    at, half = slot // 2, n_ctx // 2
    plane, core = me_ref[0], me_ref[1]
    if at < half:
        holder = jnp.bitwise_xor(plane, jnp.where(core == 0, order[0][at], order[1][at])) * 2 + core
    else:
        at -= half
        holder = jnp.bitwise_xor(plane, jnp.where(core == 0, order[1][at], order[0][at])) * 2 + 1 - core
    low = pair_ref[0, holder]
    return low if slot % 2 == 0 else 2 * n_ctx - 1 - low


def head_mask(shape, head):
    lane = lax.broadcasted_iota(jnp.int32, shape, 1)
    return lane // HEAD_DIM == head


def params(grant=VMEM_SMALL):
    return pltpu.CompilerParams(vmem_limit_bytes=grant)


def in_vmem(n):
    return [pl.BlockSpec(memory_space=pltpu.VMEM)] * n


def in_smem(n):
    return [pl.BlockSpec(memory_space=pltpu.SMEM)] * n


def forward_kernel(
    n_ctx, qblk, pair_ref, me_ref, x_ref, w_ref, turn_ref, kept_ref, r_ref, o_ref, lse_ref, acc_ref
):
    q_ref, k_ref, v_ref = (kept_ref.at[i] for i in range(3))
    cos_ref, sin_ref = turn_ref.at[0], turn_ref.at[1]
    length, cols = q_ref.shape
    blk = length // (2 * n_ctx)
    heads = cols // HEAD_DIM
    for at in range(n_ctx):
        x = x_ref[pl.ds(at * 2 * blk, 2 * blk), :]
        x_f = x.astype(F32)
        scale = lax.rsqrt(jnp.mean(x_f * x_f, axis=1, keepdims=True) + EPS)
        r_ref[pl.ds(at * 2 * blk, 2 * blk), :] = scale
        qkv = mm(x, w_ref[...]) * scale
        for second in range(2):
            to = pl.ds(pl.multiple_of(slot_block(pair_ref, me_ref, 2 * at + second, n_ctx) * blk, blk), blk)
            cosine, sine = cos_ref[to, :], sin_ref[to, :]
            query = qkv[second * blk : (second + 1) * blk, :cols]
            key = qkv[second * blk : (second + 1) * blk, cols : 2 * cols]
            q_ref[to, :] = (query * cosine + swap_halves(query) * sine).astype(BF)
            k_ref[to, :] = (key * cosine + swap_halves(key) * sine).astype(BF)
            v_ref[to, :] = qkv[second * blk : (second + 1) * blk, 2 * cols :].astype(BF)
    acc_ref[...] = jnp.zeros_like(acc_ref)
    lse_ref[...] = jnp.zeros_like(lse_ref)

    def one_head(head, carry):
        mask = head_mask((qblk, cols), head)
        here = lax.broadcasted_iota(jnp.int32, (qblk, lse_ref.shape[1]), 1) == head
        below = lax.broadcasted_iota(jnp.int32, (qblk, qblk), 1) <= lax.broadcasted_iota(jnp.int32, (qblk, qblk), 0)
        for i in range(length // qblk):
            rows = pl.ds(i * qblk, qblk)
            query = jnp.where(mask, q_ref[rows, :], jnp.zeros((), BF))
            last = jnp.where(below, mm_t(query, k_ref[rows, :]), NEG)
            peak = jnp.max(last, axis=1, keepdims=True)
            if i:
                before = mm_t(query, k_ref[: i * qblk, :])
                peak = jnp.maximum(peak, jnp.max(before, axis=1, keepdims=True))
            shift = peak * SCALE
            last = jnp.exp(last * SCALE - shift)
            total = jnp.sum(last, axis=1, keepdims=True)
            out = mm(last.astype(BF), v_ref[rows, :])
            if i:
                before = jnp.exp(before * SCALE - shift)
                total += jnp.sum(before, axis=1, keepdims=True)
                out += mm(before.astype(BF), v_ref[: i * qblk, :])
            acc_ref[rows, :] = jnp.where(mask, out * (1.0 / total), acc_ref[rows, :])
            lse_ref[rows, :] = jnp.where(here, shift + jnp.log(total), lse_ref[rows, :])
        return carry

    lax.fori_loop(0, heads, one_head, 0)
    for slot in range(2 * n_ctx):
        at = pl.multiple_of(slot_block(pair_ref, me_ref, slot, n_ctx) * blk, blk)
        o_ref[pl.ds(slot * blk, blk), :] = acc_ref[pl.ds(at, blk), :].astype(BF)
    kept_ref[3] = acc_ref[...].astype(BF)


def attention_forward(pair, me, tokens, weight, turn):
    _, length, cols = turn.shape
    width = weight.shape[0]
    n_ctx = width // cols
    return pl.pallas_call(
        functools.partial(forward_kernel, n_ctx, 256),
        out_shape=[
            jax.ShapeDtypeStruct((4, length, cols), BF),
            jax.ShapeDtypeStruct((length, 1), F32),
            jax.ShapeDtypeStruct((length, cols), BF),
            jax.ShapeDtypeStruct((length, 128), F32),
        ],
        in_specs=in_smem(2) + in_vmem(3),
        out_specs=in_vmem(4),
        scratch_shapes=[pltpu.VMEM((length, cols), F32)],
        compiler_params=params(VMEM_LIMIT),
        cost_estimate=LIGHT,
        name="attention_forward",
    )(pair, me, tokens, weight, turn)


def backward_kernel(
    n_ctx, qblk, pair_ref, me_ref, do_ref, kept_ref, r_ref, lse_ref, turn_ref,
    g_ref, gr_ref, go_ref, dq_ref, dk_ref, dv_ref, centre_ref,
):
    q_ref, k_ref, v_ref, o_ref = (kept_ref.at[i] for i in range(4))
    cos_ref, sin_ref = turn_ref.at[0], turn_ref.at[1]
    length, cols = q_ref.shape
    blk = length // (2 * n_ctx)
    heads = cols // HEAD_DIM
    for slot in range(2 * n_ctx):
        at = pl.multiple_of(slot_block(pair_ref, me_ref, slot, n_ctx) * blk, blk)
        go_ref[pl.ds(at, blk), :] = do_ref[pl.ds(slot * blk, blk), :]
    dq_ref[...] = jnp.zeros_like(dq_ref)
    dk_ref[...] = jnp.zeros_like(dk_ref)
    dv_ref[...] = jnp.zeros_like(dv_ref)

    pick = head_mask((8, cols), lax.broadcasted_iota(jnp.int32, (8, cols), 0)).astype(F32)
    centre_ref[...] = lax.dot_general(
        pick,
        go_ref[...].astype(F32) * o_ref[...].astype(F32),
        (((1,), (1,)), ((), ())),
        precision=lax.Precision.HIGHEST,
        preferred_element_type=F32,
    )

    def one_head(head, carry):
        mask = head_mask((qblk, cols), head)
        below = lax.broadcasted_iota(jnp.int32, (qblk, qblk), 0) <= lax.broadcasted_iota(jnp.int32, (qblk, qblk), 1)
        for i in range(length // qblk):
            rows = pl.ds(i * qblk, qblk)
            query = jnp.where(mask, q_ref[rows, :], jnp.zeros((), BF))
            grad = jnp.where(mask, go_ref[rows, :], jnp.zeros((), BF))
            lse = lse_ref[pl.ds(head, 1), rows]
            centre = centre_ref[pl.ds(head, 1), rows]
            out = None
            for at, size in ((i * qblk, qblk), (0, i * qblk)):
                if not size:
                    continue
                keys = pl.ds(at, size)
                probs = jnp.exp(mm_t(k_ref[keys, :], query) * SCALE - lse)
                if at or not i:
                    probs = jnp.where(below, probs, 0.0)
                grad_probs = mm_t(v_ref[keys, :], grad)
                grad_scores = (probs * (grad_probs - centre)).astype(BF)
                dk_ref[keys, :] += mm(grad_scores, query)
                dv_ref[keys, :] += mm(probs.astype(BF), grad)
                term = t_mm(grad_scores, k_ref[keys, :])
                out = term if out is None else out + term
            dq_ref[rows, :] = jnp.where(mask, out, dq_ref[rows, :])
        return carry

    lax.fori_loop(0, heads, one_head, 0)
    for slot in range(2 * n_ctx):
        at = pl.multiple_of(slot_block(pair_ref, me_ref, slot, n_ctx) * blk, blk)
        rows = pl.ds(slot * blk, blk)
        to = pl.ds(at, blk)
        cosine, sine = cos_ref[to, :], sin_ref[to, :]
        scale = r_ref[rows, :]
        query = (dq_ref[to, :] * SCALE).astype(BF).astype(F32)
        key = (dk_ref[to, :] * SCALE).astype(BF).astype(F32)
        value = dv_ref[to, :].astype(BF).astype(F32)
        query = query * cosine - swap_halves(query) * sine
        key = key * cosine - swap_halves(key) * sine
        for at_col, part in enumerate((query, key, value)):
            span = pl.ds(at_col * cols, cols)
            g_ref[rows, span] = part.astype(BF)
            gr_ref[rows, span] = (part * scale).astype(BF)


def attention_backward(pair, me, n_ctx, grad, kept, scale, lse, turn):
    _, length, cols = turn.shape
    return pl.pallas_call(
        functools.partial(backward_kernel, n_ctx, 256),
        out_shape=[jax.ShapeDtypeStruct((length, 3 * cols), BF)] * 2,
        in_specs=in_smem(2) + in_vmem(5),
        out_specs=in_vmem(2),
        scratch_shapes=[pltpu.VMEM((length, cols), BF)]
        + [pltpu.VMEM((length, cols), F32)] * 3
        + [pltpu.VMEM((8, length), F32)],
        compiler_params=params(),
        cost_estimate=LIGHT,
        name="attention_backward",
    )(pair, me, grad, kept, scale, lse, turn)


def feed_forward_kernel(
    core_ref, n_ref, c_ref, g_ref, u_ref, d_ref, h_ref, dg_ref, du_ref, theirs_ref, mine_ref
):
    rows, cot = n_ref[...], c_ref[...]
    hid, tile = g_ref.shape[1], 256
    for at in range(0, hid, tile):
        span = slice(at, at + tile)
        gate = mm(rows, g_ref[:, span])
        up = mm(rows, u_ref[:, span])
        grad = mm_t(cot, d_ref[span, :])
        sig = 1.0 / (1.0 + jnp.exp(-gate))
        active = gate * sig
        h_ref[:, span] = (active * up).astype(BF)
        dg_ref[:, span] = (grad * up * sig * (1.0 + gate * (1.0 - sig))).astype(BF)
        du_ref[:, span] = (grad * active).astype(BF)
    back = (mm_t(dg_ref[...], g_ref[...]) + mm_t(du_ref[...], u_ref[...])).astype(BF)
    first = pl.program_id(0) < pl.num_programs(0) // 2

    @pl.when(first)
    def _():
        theirs_ref[...] = back

    @pl.when(jnp.logical_not(first))
    def _():
        mine_ref[...] = back


def feed_forward(normed, cotangent, gate_w, up_w, down_w):
    count, width = normed.shape
    hid = gate_w.shape[1]
    tile = 256
    half = count // tile // 2

    def rows_of(r, core):
        return (jnp.where(r < half, (1 - core[0]) * half + r, core[0] * half + r - half), 0)

    def fixed(r, core):
        return (0, 0)

    once = pl.Buffered(1)
    return pl.pallas_call(
        feed_forward_kernel,
        grid_spec=pltpu.PrefetchScalarGridSpec(
            num_scalar_prefetch=1,
            grid=(2 * half,),
            in_specs=[
                pl.BlockSpec((tile, width), rows_of),
                pl.BlockSpec((tile, width), rows_of),
                pl.BlockSpec((width, hid), fixed, pipeline_mode=once),
                pl.BlockSpec((width, hid), fixed, pipeline_mode=once),
                pl.BlockSpec((hid, width), fixed, pipeline_mode=once),
            ],
            out_specs=[pl.BlockSpec((tile, hid), rows_of)] * 3
            + [
                pl.BlockSpec((tile, width), lambda r, core: (jnp.minimum(r, half - 1), 0)),
                pl.BlockSpec((tile, width), lambda r, core: (jnp.maximum(r - half, 0), 0)),
            ],
        ),
        out_shape=[jax.ShapeDtypeStruct((count, hid), BF)] * 3
        + [jax.ShapeDtypeStruct((count // 2, width), BF)] * 2,
        compiler_params=params(VMEM_LIMIT),
        cost_estimate=LIGHT,
        name="feed_forward",
    )(lax.axis_index("core").astype(jnp.int32)[None], normed, cotangent, gate_w, up_w, down_w)


def branch_kernel(core_ref, h_ref, d_ref, theirs_ref, mine_ref):
    out = mm(h_ref[...], d_ref[...]).astype(BF)
    first = pl.program_id(0) < pl.num_programs(0) // 2

    @pl.when(first)
    def _():
        theirs_ref[...] = out

    @pl.when(jnp.logical_not(first))
    def _():
        mine_ref[...] = out


def branch_rows(hidden, down_w):
    count, hid = hidden.shape
    width = down_w.shape[1]
    tile = 256
    half = count // tile // 2
    return pl.pallas_call(
        branch_kernel,
        grid_spec=pltpu.PrefetchScalarGridSpec(
            num_scalar_prefetch=1,
            grid=(2 * half,),
            in_specs=[
                pl.BlockSpec(
                    (tile, hid),
                    lambda r, core: (jnp.where(r < half, (1 - core[0]) * half + r, core[0] * half + r - half), 0),
                ),
                pl.BlockSpec((hid, width), lambda r, core: (0, 0), pipeline_mode=pl.Buffered(1)),
            ],
            out_specs=[
                pl.BlockSpec((tile, width), lambda r, core: (jnp.minimum(r, half - 1), 0)),
                pl.BlockSpec((tile, width), lambda r, core: (jnp.maximum(r - half, 0), 0)),
            ],
        ),
        out_shape=[jax.ShapeDtypeStruct((count // 2, width), BF)] * 2,
        compiler_params=params(),
        cost_estimate=LIGHT,
        name="branch_rows",
    )(lax.axis_index("core").astype(jnp.int32)[None], hidden, down_w)


def merge_kernel(a_ref, m_ref, *refs):
    *b_refs, go_ref, out_ref, all_ref = refs
    rows = b_refs[0].shape[0]
    for at, ref in enumerate(b_refs):
        all_ref[pl.ds(at * rows, rows), :] = ref[...]
    go_ref[...] = mm_t(all_ref[...], m_ref[...]).astype(BF)
    out_ref[...] = t_mm(a_ref[...], all_ref[...]).astype(BF)


def merge_terms(attended, merge_rows, pieces):
    length, cols = attended.shape
    width = merge_rows.shape[1]
    return pl.pallas_call(
        merge_kernel,
        out_shape=[jax.ShapeDtypeStruct((length, cols), BF), jax.ShapeDtypeStruct((cols, width), BF)],
        in_specs=in_vmem(2 + len(pieces)),
        out_specs=in_vmem(2),
        scratch_shapes=[pltpu.VMEM((length, width), BF)],
        compiler_params=params(),
        cost_estimate=LIGHT,
        name="merge_terms",
    )(attended, merge_rows, *pieces)


def heads_term_kernel(x_ref, g_ref, out_ref):
    out_ref[...] = mm(x_ref[...], g_ref[...]).astype(BF)


def heads_term(tokens_t, grad):
    width, count = tokens_t.shape
    cols = grad.shape[1]
    tile = 512
    return pl.pallas_call(
        heads_term_kernel,
        grid=(width // tile,),
        in_specs=[
            pl.BlockSpec((tile, count), lambda i: (i, 0)),
            pl.BlockSpec((count, cols), lambda i: (0, 0), pipeline_mode=pl.Buffered(1)),
        ],
        out_specs=pl.BlockSpec((tile, cols), lambda i: (i, 0)),
        out_shape=jax.ShapeDtypeStruct((width, cols), BF),
        compiler_params=params(),
        cost_estimate=LIGHT,
        name="heads_term",
    )(tokens_t, grad)


def weight_rows_kernel(at_ref, left_ref, right_ref, *out_refs):
    out = t_mm(left_ref[...], right_ref[...]).astype(BF)
    for i, ref in enumerate(out_refs):

        @pl.when(pl.program_id(0) == i)
        def _(ref=ref):
            ref[...] = out


def weight_rows(left, right, index, size):
    count, n = left.shape[0], len(index)
    width = right.shape[1]
    return pl.pallas_call(
        weight_rows_kernel,
        grid_spec=pltpu.PrefetchScalarGridSpec(
            num_scalar_prefetch=1,
            grid=(n,),
            in_specs=[
                pl.BlockSpec((count, size), lambda i, at: (0, at[i])),
                pl.BlockSpec((count, width), lambda i, at: (0, 0), pipeline_mode=pl.Buffered(1)),
            ],
            out_specs=[pl.BlockSpec((size, width), lambda i, at: (0, 0), pipeline_mode=pl.Buffered(1))] * n,
        ),
        out_shape=[jax.ShapeDtypeStruct((size, width), BF)] * n,
        compiler_params=params(),
        cost_estimate=LIGHT,
        name="weight_rows",
    )(jnp.stack(index).astype(jnp.int32), left, right)


def back_kernel(g_ref, w_ref, out_ref):
    out_ref[...] = mm_t(g_ref[...], w_ref[...]).astype(BF)


def back_rows(grad, weight, half):
    count, cols = grad.shape
    width = weight.shape[0]
    tile = 256
    steps = count // 2 // tile
    return pl.pallas_call(
        back_kernel,
        grid=(steps,),
        in_specs=[
            pl.BlockSpec((tile, cols), lambda r: (half * steps + r, 0)),
            pl.BlockSpec((width, cols), lambda r: (0, 0), pipeline_mode=pl.Buffered(1)),
        ],
        out_specs=pl.BlockSpec((tile, width), lambda r: (r, 0)),
        out_shape=jax.ShapeDtypeStruct((count // 2, width), BF),
        compiler_params=params(),
        cost_estimate=LIGHT,
        name="back_rows",
    )(grad, weight)


def fold_heads_kernel(q_ref, k_ref, v_ref, gain_ref, out_ref):
    n_ctx, _, cols = out_ref.shape
    cols //= 3
    gain = gain_ref[...]
    for at, ref in enumerate((q_ref, k_ref, v_ref)):
        for to in range(n_ctx):
            part = ref[:, to * cols : (to + 1) * cols].astype(F32) * gain
            out_ref[to, :, at * cols : (at + 1) * cols] = part.astype(BF)


def fold_heads(weights, gain, n_ctx):
    rows, width = weights[0].shape
    return pl.pallas_call(
        fold_heads_kernel,
        out_shape=jax.ShapeDtypeStruct((n_ctx, rows, 3 * (width // n_ctx)), BF),
        in_specs=in_vmem(4),
        out_specs=pl.BlockSpec(memory_space=pltpu.VMEM),
        compiler_params=params(),
        cost_estimate=LIGHT,
        name="fold_heads",
    )(*weights, gain)


def unfold_heads_kernel(s_ref, q_ref, k_ref, v_ref, gain_ref, dq_ref, dk_ref, dv_ref, first_ref):
    n_ctx, rows, cols = s_ref.shape
    cols //= 3
    gain = gain_ref[...]
    total = jnp.zeros((rows, cols), F32)
    for at, (ref, out) in enumerate(((q_ref, dq_ref), (k_ref, dk_ref), (v_ref, dv_ref))):
        for to in range(n_ctx):
            span = slice(to * cols, (to + 1) * cols)
            part = s_ref[to, :, at * cols : (at + 1) * cols].astype(F32)
            total += part * ref[:, span].astype(F32)
            out[:, span] = part * gain
    first_ref[...] = jnp.sum(total, axis=1, keepdims=True)


def unfold_heads(sums, weights, gain):
    rows, width = weights[0].shape
    return pl.pallas_call(
        unfold_heads_kernel,
        out_shape=[jax.ShapeDtypeStruct((rows, width), F32)] * 3 + [jax.ShapeDtypeStruct((rows, 1), F32)],
        in_specs=in_vmem(5),
        out_specs=in_vmem(4),
        compiler_params=params(),
        cost_estimate=LIGHT,
        name="unfold_heads",
    )(sums, *weights, gain)


def fold_hidden_kernel(piece, w_ref, gain_ref, out_ref):
    n_core, n_fsdp, _, hid = out_ref.shape
    gain = gain_ref[...]
    for plane in range(hid // piece):
        for core in range(n_core):
            for line in range(n_fsdp):
                at = ((plane * n_core + core) * n_fsdp + line) * piece
                part = w_ref[:, at : at + piece].astype(F32) * gain
                out_ref[core, line, :, plane * piece : (plane + 1) * piece] = part.astype(BF)


def fold_hidden(weight, gain, n_plane, n_core, n_fsdp):
    rows, total = weight.shape
    piece = total // (n_plane * n_core * n_fsdp)
    if piece % 128:
        folded = (weight.astype(F32) * gain).astype(BF).reshape(rows, n_plane, n_core, n_fsdp, piece)
        return folded.transpose(2, 3, 0, 1, 4).reshape(n_core, n_fsdp, rows, n_plane * piece)
    return pl.pallas_call(
        functools.partial(fold_hidden_kernel, piece),
        out_shape=jax.ShapeDtypeStruct((n_core, n_fsdp, rows, n_plane * piece), BF),
        in_specs=in_vmem(2),
        out_specs=pl.BlockSpec(memory_space=pltpu.VMEM),
        compiler_params=params(),
        cost_estimate=LIGHT,
        name="fold_hidden",
    )(weight, gain)


def unfold_hidden_kernel(piece, at_ref, *refs):
    *s_refs, w_ref, gain_ref, out_ref, second_ref = refs
    n_fsdp = len(s_refs)
    n_core, rows, hid = s_refs[0].shape
    gain = gain_ref[...]
    total = jnp.zeros((rows, piece), F32)
    for mask, ref in enumerate(s_refs):
        line = jnp.bitwise_xor(at_ref[1], mask)
        for other in range(n_core):
            core = jnp.bitwise_xor(at_ref[0], other)
            for plane in range(hid // piece):
                at = ((plane * n_core + core) * n_fsdp + line) * piece
                span = pl.ds(pl.multiple_of(at, piece), piece)
                part = ref[other, :, plane * piece : (plane + 1) * piece].astype(F32)
                total += part * w_ref[:, span].astype(F32)
                out_ref[:, span] = part * gain
    second_ref[...] = jnp.sum(total, axis=1, keepdims=True)


def unfold_hidden(pieces, weight, gain, n_plane):
    rows, total = weight.shape
    n_core, _, hid = pieces[0].shape
    n_fsdp = len(pieces)
    piece = hid // n_plane
    core, line = lax.axis_index("core"), lax.axis_index("fsdp")
    if piece % 128:
        out = jnp.zeros((rows, n_plane, n_core, n_fsdp, piece), BF)
        for mask, block in enumerate(pieces):
            for other in range(n_core):
                part = block[other].reshape(rows, n_plane, 1, 1, piece)
                out = lax.dynamic_update_slice(out, part, (0, 0, core ^ other, line ^ mask, 0))
        out = out.reshape(rows, total).astype(F32)
        return out * gain, jnp.sum(out * weight.astype(F32), axis=1, keepdims=True)
    return pl.pallas_call(
        functools.partial(unfold_hidden_kernel, piece),
        out_shape=[jax.ShapeDtypeStruct((rows, total), F32), jax.ShapeDtypeStruct((rows, 1), F32)],
        in_specs=in_smem(1) + in_vmem(n_fsdp + 2),
        out_specs=in_vmem(2),
        compiler_params=params(),
        cost_estimate=LIGHT,
        name="unfold_hidden",
    )(jnp.stack([core, line]).astype(jnp.int32), *pieces, weight, gain)


def place_kernel(at_ref, *refs):
    *p_refs, out_ref = refs
    for i, ref in enumerate(p_refs):
        out_ref[at_ref[i]] = ref[...]


def place(pieces, index, room=None):
    n = len(pieces)
    moved = 2 * n * pieces[0].size * pieces[0].dtype.itemsize
    return pl.pallas_call(
        place_kernel,
        out_shape=jax.ShapeDtypeStruct((room or n,) + pieces[0].shape, pieces[0].dtype),
        in_specs=in_smem(1) + in_vmem(n),
        out_specs=pl.BlockSpec(memory_space=pltpu.VMEM),
        compiler_params=params(VMEM_LIMIT),
        cost_estimate=LIGHT,
        name="place",
    )(jnp.stack(index).astype(jnp.int32), *pieces)


def gather(value, axes, axis=0):
    return lax.all_gather(value, axes, axis=axis, tiled=True)


def scatter(value, axes):
    return lax.psum_scatter(value, axes, scatter_dimension=0, tiled=True)


def exchange(value, axes):
    return lax.all_to_all(value, axes, split_axis=0, concat_axis=0, tiled=True)


def together(values):
    return lax.optimization_barrier(values)


def core_swap(value):
    n = lax.axis_size("plane") * 2
    return lax.ppermute(value, CTX, [(i, i ^ 1) for i in range(n)])


def plane_step(value, step):
    steps, _ = relative(lax.axis_size("plane"))
    n = lax.axis_size("plane") * 2
    return lax.ppermute(value, CTX, [(i, i ^ (2 * steps[i % 2][step])) for i in range(n)])


def line_swap(value, mask):
    n = lax.axis_size("fsdp")
    return lax.ppermute(value, "fsdp", [(i, i ^ mask) for i in range(n)])


def plane_gather_more(pieces):
    step = len(pieces).bit_length() - 1
    return pieces + [plane_step(piece, step) for piece in pieces]


def plane_gather(value):
    pieces = [value]
    while len(pieces) < lax.axis_size("plane"):
        pieces = plane_gather_more(pieces)
    return pieces


def plane_send(chunks):
    n = len(chunks) // 2
    return [plane_step(chunk, n.bit_length() - 1) for chunk in chunks[n:]]


def plane_add(chunks, came):
    return [(mine.astype(F32) + chunk.astype(F32)).astype(BF) for mine, chunk in zip(chunks, came)]


def plane_scatter(chunks):
    while len(chunks) > 1:
        chunks = plane_add(chunks, plane_send(chunks))
    return chunks[0]


def plane_index():
    _, order = relative(lax.axis_size("plane"))
    core = lax.axis_index("core")
    plane = lax.axis_index("plane")
    return [plane ^ jnp.where(core == 0, a, b) for a, b in zip(*order)]


def part(value, at, size, axis):
    return lax.dynamic_slice_in_dim(value, at * size, size, axis)


def ctx_gather(value):
    mine = plane_gather(value)
    return mine + [core_swap(piece) for piece in mine]


def ctx_scatter(theirs, mine, n_plane):
    total = (mine.astype(F32) + core_swap(theirs).astype(F32)).astype(BF)
    rows = total.shape[0] // n_plane
    return plane_scatter([total[i * rows : (i + 1) * rows] for i in range(n_plane)])


def cores_pair(value):
    core = lax.axis_index("core")
    kept = lax.dynamic_index_in_dim(value, core, 0, keepdims=False)
    return kept, core_swap(lax.dynamic_index_in_dim(value, 1 - core, 0, keepdims=False))


def lines_parts(pair):
    line = lax.axis_index("fsdp")
    return [
        jnp.stack([lax.dynamic_index_in_dim(v, line ^ mask, 0, keepdims=False) for v in pair])
        for mask in range(lax.axis_size("fsdp"))
    ]


def lines_swap(parts):
    return parts[:1] + [line_swap(parts[mask], mask) for mask in range(1, len(parts))]


def lines_pair(pair):
    return lines_swap(lines_parts(pair))


def line_rows_kernel(at_ref, *refs):
    *p_refs, out_ref = refs
    n_fsdp = len(p_refs)
    for mask, ref in enumerate(p_refs):
        line = jnp.bitwise_xor(at_ref[1], mask)
        for other in range(2):
            core = jnp.bitwise_xor(at_ref[0], other)
            out_ref[core * n_fsdp + line] = ref[other]


def line_rows(pieces):
    n = 2 * len(pieces)
    at = jnp.stack([lax.axis_index("core"), lax.axis_index("fsdp")]).astype(jnp.int32)
    return pl.pallas_call(
        line_rows_kernel,
        out_shape=jax.ShapeDtypeStruct((n,) + pieces[0].shape[1:], pieces[0].dtype),
        in_specs=in_smem(1) + in_vmem(len(pieces)),
        out_specs=pl.BlockSpec(memory_space=pltpu.VMEM),
        compiler_params=params(VMEM_LIMIT),
        cost_estimate=LIGHT,
        name="line_rows",
    )(at, *pieces)


def on_device(
    layer_input, pairing, query_weight, key_weight, value_weight, merge_weight,
    gate_weight, up_weight, down_weight, norm_first, norm_second, output_cotangent,
):
    n_plane = lax.axis_size("plane")
    n_core = lax.axis_size("core")
    n_fsdp = lax.axis_size("fsdp")
    n_ctx = n_plane * n_core
    n_tok = n_core * n_fsdp
    me = jnp.stack([lax.axis_index("plane"), lax.axis_index("core")]).astype(jnp.int32)
    index = plane_index()
    _, rows, width = layer_input.shape
    length = rows * n_ctx
    half = length // 2
    cols = width // n_ctx
    dev_rows = gate_weight.shape[0]
    piece = gate_weight.shape[1] // (n_ctx * n_fsdp)
    hid = piece * n_plane
    d_rows = n_tok * dev_rows
    tokens = layer_input.reshape(rows, width)
    cotangent = output_cotangent.reshape(rows, width)
    gain_first = norm_first.astype(F32)[:, None]
    gain_second = norm_second.astype(F32)[:, None]
    projections = (query_weight, key_weight, value_weight)

    merge_rows = gather(merge_weight, "fsdp")
    gate_moved = lines_pair(cores_pair(fold_hidden(gate_weight, gain_second, n_plane, n_core, n_fsdp)))
    own = exchange(fold_heads(projections, gain_first, n_ctx), CTX)
    x_pieces = ctx_gather(tokens)
    up_pair = cores_pair(fold_hidden(up_weight, gain_second, n_plane, n_core, n_fsdp))
    turn = jnp.stack(rope_tables(length, cols))
    own, gate_moved[3:], x_pieces, up_pair, merge_rows = together(
        (own, gate_moved[3:], x_pieces, up_pair, merge_rows)
    )
    qkv_weight = gather(own[:, None], "fsdp", axis=1).reshape(width, 3 * cols)
    gate_pieces = plane_gather(line_rows(gate_moved).reshape(d_rows, hid))
    down_pieces = plane_gather_more([down_weight])
    x_all = jnp.concatenate(x_pieces, axis=0)
    x_all, gate_pieces = together((x_all, gate_pieces))
    up_moved = lines_pair(up_pair)
    cot_all = gather(cotangent, TOK)

    kept, scale_all, attended, lse = attention_forward(pairing, me, x_all, qkv_weight, turn)
    while len(down_pieces) < n_plane:
        down_pieces = plane_gather_more(down_pieces)
    attended, down_pieces = together((attended, down_pieces))
    down_rows = place(down_pieces, index).reshape(hid, width)
    own_f = tokens.astype(F32)
    theirs = together(mm(attended[half:], merge_rows).astype(BF))
    mine = together(mm(attended[:half], merge_rows).astype(BF))
    mixed = own_f + ctx_scatter(theirs, mine, n_plane)
    lse_rows = lse[:, :8].T
    gate_rows = place(gate_pieces, index).reshape(width, hid)
    mixed, up_moved, lse_rows = together((mixed, up_moved, lse_rows))
    up_pieces = plane_gather_more([line_rows(up_moved).reshape(d_rows, hid)])
    gate_rows, down_rows, up_pieces = together((gate_rows, down_rows, up_pieces))
    while len(up_pieces) < n_plane:
        up_pieces = plane_gather_more(up_pieces)
    up_rows = place(up_pieces[:-1], index[:-1], n_plane)
    up_rows = lax.dynamic_update_slice(up_rows, up_pieces[-1][None], (index[-1], 0, 0)).reshape(width, hid)

    scale_second = lax.rsqrt(jnp.mean(mixed * mixed, axis=-1, keepdims=True) + EPS)
    unit_second = mixed * scale_second
    normed_all = gather(unit_second.astype(BF), TOK)
    hidden, grad_gate, grad_up, theirs, mine = feed_forward(
        normed_all, cot_all, gate_rows, up_rows, down_rows
    )
    theirs = core_swap(theirs)
    gate_late = weight_rows(normed_all, grad_gate, index[n_plane // 2 :], d_rows)
    theirs, gate_late = together((theirs, gate_late))
    e_two = (mine.astype(F32) + theirs.astype(F32)).astype(BF)

    hidden, grad_gate, grad_up, e_two = together((hidden, grad_gate, grad_up, e_two))
    gate_chunks = list(weight_rows(normed_all, grad_gate, index[: n_plane // 2], d_rows)) + list(gate_late)
    gate_came = plane_send(gate_chunks)
    up_chunks = [together(t_mm(part(normed_all, at, d_rows, 1), grad_up).astype(BF)) for at in index]
    theirs, mine = branch_rows(hidden, down_rows)
    gate_chunks, gate_came, up_chunks, theirs, mine = together(
        (gate_chunks, gate_came, up_chunks, theirs, mine)
    )
    gate_chunks = plane_add(gate_chunks, gate_came)
    branch = (mine.astype(F32) + core_swap(theirs).astype(F32)).astype(BF)
    e_two = scatter(e_two, "fsdp")
    gate_sum = plane_scatter(gate_chunks)
    e_two, gate_sum, up_chunks, branch = together((e_two, gate_sum, up_chunks, branch))
    branch_sum = scatter(branch, "fsdp")
    e_two_f = e_two.astype(F32)
    grad_mixed = cotangent.astype(F32) + scale_second * (
        e_two_f - unit_second * jnp.mean(e_two_f * unit_second, axis=-1, keepdims=True)
    )
    branch_pieces = plane_gather_more([grad_mixed.astype(BF)])
    x_t = x_all.reshape(length, n_ctx, n_fsdp, dev_rows).transpose(2, 1, 3, 0).reshape(width, length)
    branch_pieces, gate_sum, x_t = together((branch_pieces, gate_sum, x_t))
    gate_parts = lines_parts(cores_pair(gate_sum.reshape(n_core, n_fsdp, dev_rows, hid)))
    while len(branch_pieces) < n_plane:
        branch_pieces = plane_gather_more(branch_pieces)
    branch_pieces = branch_pieces + [core_swap(value) for value in branch_pieces]
    gate_back = lines_swap(gate_parts)

    branch_pieces, up_chunks = together((branch_pieces, up_chunks))
    up_came = plane_send(up_chunks)
    grad_attended, merge_grad = merge_terms(attended, merge_rows, branch_pieces)
    merge_grad, grad_attended = together((merge_grad, grad_attended))
    merge_grad = scatter(merge_grad, "fsdp")
    grad_qkv, grad_scaled = attention_backward(
        pairing, me, n_ctx, grad_attended, kept, scale_all, lse_rows, turn
    )
    grad_scaled, branch_sum = together((grad_scaled, branch_sum))
    sums = heads_term(x_t, grad_scaled)
    grad_qkv, up_chunks, up_came, gate_back, sums, merge_grad, branch_sum = together(
        (grad_qkv, up_chunks, up_came, gate_back, sums, merge_grad, branch_sum)
    )
    sums = scatter(sums, "fsdp")
    up_sum = plane_scatter(plane_add(up_chunks, up_came))
    layer_output = (mixed + branch_sum.astype(F32)).astype(BF)
    theirs = back_rows(grad_qkv, qkv_weight, 1)
    mine = back_rows(grad_qkv, qkv_weight, 0)
    e_one = ctx_scatter(theirs, mine, n_plane)
    up_parts = lines_parts(cores_pair(up_sum.reshape(n_core, n_fsdp, dev_rows, hid)))
    hidden, mine = together((hidden, mine))
    down_chunks = [together(t_mm(part(hidden, at, piece, 1), cot_all).astype(BF)) for at in index]
    e_one, down_chunks = together((e_one, down_chunks))
    down_came = plane_send(down_chunks)
    sums, up_parts, merge_grad = together((sums, up_parts, merge_grad.astype(F32)))
    up_back = lines_swap(up_parts)
    sums = exchange(sums.reshape(n_ctx, dev_rows, 3 * cols), CTX)
    query_grad, key_grad, value_grad, first_grad = unfold_heads(sums, projections, gain_first)
    query_grad, key_grad, value_grad, first_grad, up_back = together(
        (query_grad, key_grad, value_grad, first_grad, up_back)
    )
    scale_first = lax.rsqrt(jnp.mean(own_f * own_f, axis=-1, keepdims=True) + EPS)
    unit_first = own_f * scale_first
    input_grad = (
        grad_mixed
        + scale_first * (e_one - unit_first * jnp.mean(e_one * unit_first, axis=-1, keepdims=True))
    ).astype(BF)
    down_grad = plane_scatter(plane_add(down_chunks, down_came)).astype(F32)
    gate_grad, second_gate = unfold_hidden(gate_back, gate_weight, gain_second, n_plane)
    up_grad, second_up = unfold_hidden(up_back, up_weight, gain_second, n_plane)
    second_grad = (second_gate + second_up)[:, 0]
    return (
        layer_output.reshape(1, rows, width),
        input_grad.reshape(1, rows, width),
        query_grad,
        key_grad,
        value_grad,
        merge_grad,
        gate_grad,
        up_grad,
        down_grad,
        first_grad[:, 0],
        second_grad,
    )


def solution(mesh):
    n_ctx, n_fsdp = mesh.shape["ctx"], mesh.shape["fsdp"]
    inner = Mesh(mesh.devices.reshape(n_ctx // 2, 2, n_fsdp), ("plane", "core", "fsdp"))
    token = P("fsdp", CTX, None)
    weight = P(("plane", "core", "fsdp"), None)
    gain = P(("plane", "core", "fsdp"))
    return jax.shard_map(
        on_device,
        mesh=inner,
        in_specs=(token, P("fsdp", None)) + (weight,) * 7 + (gain, gain, token),
        out_specs=(token, token) + (weight,) * 7 + (gain, gain),
        check_vma=False,
    )
```

```python
import functools

import jax
import jax.numpy as jnp
from jax import lax
from jax.experimental import pallas as pl
from jax.experimental.pallas import tpu as pltpu
from jax.sharding import Mesh, PartitionSpec as P

HEAD_DIM = 64
THETA = 130000.0
EPS = 1e-05
SCALE = HEAD_DIM**-0.5
NEG = -1e30
BF = jnp.bfloat16
F32 = jnp.float32
CTX = ("plane", "core")
TOK = ("core", "fsdp")
VMEM_LIMIT = 56 * 1024 * 1024
VMEM_SMALL = 30 * 1024 * 1024
LIGHT = pl.CostEstimate(flops=1024, bytes_accessed=1024, transcendentals=0)


def mm(left, right):
    return jnp.dot(left, right, preferred_element_type=F32)


def mm_t(left, right):
    return lax.dot_general(left, right, (((1,), (1,)), ((), ())), preferred_element_type=F32)


def t_mm(left, right):
    return lax.dot_general(left, right, (((0,), (0,)), ((), ())), preferred_element_type=F32)


def rope_tables(length, cols):
    half = HEAD_DIM // 2
    freq = THETA ** (-2.0 * jnp.arange(half, dtype=F32) / HEAD_DIM)
    angle = jnp.arange(length, dtype=jnp.int32).astype(F32)[:, None] * freq
    cosine, sine = jnp.cos(angle), jnp.sin(angle)
    heads = cols // HEAD_DIM
    return (
        jnp.tile(jnp.concatenate([cosine, cosine], axis=1), (1, heads)),
        jnp.tile(jnp.concatenate([-sine, sine], axis=1), (1, heads)),
    )


def swap_halves(values):
    cols = values.shape[1]
    half = HEAD_DIM // 2
    lane = lax.broadcasted_iota(jnp.int32, values.shape, 1)
    up = pltpu.roll(values, half, 1)
    down = pltpu.roll(values, cols - half, 1)
    return jnp.where(lane % HEAD_DIM < half, down, up)


def relative(n_plane):
    bits = n_plane.bit_length() - 1
    steps = [[1 << ((s + c) % bits) for s in range(bits)] for c in range(2)]
    order = []
    for masks in steps:
        found = [0]
        for mask in masks:
            found += [m ^ mask for m in found]
        order.append(found)
    return steps, order


def slot_block(pair_ref, me_ref, slot, n_ctx):
    _, order = relative(n_ctx // 2)
    at, half = slot // 2, n_ctx // 2
    plane, core = me_ref[0], me_ref[1]
    if at < half:
        holder = jnp.bitwise_xor(plane, jnp.where(core == 0, order[0][at], order[1][at])) * 2 + core
    else:
        at -= half
        holder = jnp.bitwise_xor(plane, jnp.where(core == 0, order[1][at], order[0][at])) * 2 + 1 - core
    low = pair_ref[0, holder]
    return low if slot % 2 == 0 else 2 * n_ctx - 1 - low


def head_mask(shape, head):
    lane = lax.broadcasted_iota(jnp.int32, shape, 1)
    return lane // HEAD_DIM == head


def params(grant=VMEM_SMALL):
    return pltpu.CompilerParams(vmem_limit_bytes=grant)


def in_vmem(n):
    return [pl.BlockSpec(memory_space=pltpu.VMEM)] * n


def in_smem(n):
    return [pl.BlockSpec(memory_space=pltpu.SMEM)] * n


def forward_kernel(
    n_ctx, qblk, pair_ref, me_ref, x_ref, w_ref, turn_ref, kept_ref, r_ref, o_ref, lse_ref, acc_ref
):
    q_ref, k_ref, v_ref = (kept_ref.at[i] for i in range(3))
    cos_ref, sin_ref = turn_ref.at[0], turn_ref.at[1]
    length, cols = q_ref.shape
    blk = length // (2 * n_ctx)
    heads = cols // HEAD_DIM
    for at in range(n_ctx):
        x = x_ref[pl.ds(at * 2 * blk, 2 * blk), :]
        x_f = x.astype(F32)
        scale = lax.rsqrt(jnp.mean(x_f * x_f, axis=1, keepdims=True) + EPS)
        r_ref[pl.ds(at * 2 * blk, 2 * blk), :] = scale
        qkv = mm(x, w_ref[...]) * scale
        for second in range(2):
            to = pl.ds(pl.multiple_of(slot_block(pair_ref, me_ref, 2 * at + second, n_ctx) * blk, blk), blk)
            cosine, sine = cos_ref[to, :], sin_ref[to, :]
            query = qkv[second * blk : (second + 1) * blk, :cols]
            key = qkv[second * blk : (second + 1) * blk, cols : 2 * cols]
            q_ref[to, :] = (query * cosine + swap_halves(query) * sine).astype(BF)
            k_ref[to, :] = (key * cosine + swap_halves(key) * sine).astype(BF)
            v_ref[to, :] = qkv[second * blk : (second + 1) * blk, 2 * cols :].astype(BF)
    acc_ref[...] = jnp.zeros_like(acc_ref)
    lse_ref[...] = jnp.zeros_like(lse_ref)

    def one_head(head, carry):
        mask = head_mask((qblk, cols), head)
        here = lax.broadcasted_iota(jnp.int32, (qblk, lse_ref.shape[1]), 1) == head
        below = lax.broadcasted_iota(jnp.int32, (qblk, qblk), 1) <= lax.broadcasted_iota(jnp.int32, (qblk, qblk), 0)
        for i in range(length // qblk):
            rows = pl.ds(i * qblk, qblk)
            query = jnp.where(mask, q_ref[rows, :], jnp.zeros((), BF))
            last = jnp.where(below, mm_t(query, k_ref[rows, :]), NEG)
            peak = jnp.max(last, axis=1, keepdims=True)
            if i:
                before = mm_t(query, k_ref[: i * qblk, :])
                peak = jnp.maximum(peak, jnp.max(before, axis=1, keepdims=True))
            shift = peak * SCALE
            last = jnp.exp(last * SCALE - shift)
            total = jnp.sum(last, axis=1, keepdims=True)
            out = mm(last.astype(BF), v_ref[rows, :])
            if i:
                before = jnp.exp(before * SCALE - shift)
                total += jnp.sum(before, axis=1, keepdims=True)
                out += mm(before.astype(BF), v_ref[: i * qblk, :])
            acc_ref[rows, :] = jnp.where(mask, out * (1.0 / total), acc_ref[rows, :])
            lse_ref[rows, :] = jnp.where(here, shift + jnp.log(total), lse_ref[rows, :])
        return carry

    lax.fori_loop(0, heads, one_head, 0)
    for slot in range(2 * n_ctx):
        at = pl.multiple_of(slot_block(pair_ref, me_ref, slot, n_ctx) * blk, blk)
        o_ref[pl.ds(slot * blk, blk), :] = acc_ref[pl.ds(at, blk), :].astype(BF)
    kept_ref[3] = acc_ref[...].astype(BF)


def attention_forward(pair, me, tokens, weight, turn):
    _, length, cols = turn.shape
    width = weight.shape[0]
    n_ctx = width // cols
    return pl.pallas_call(
        functools.partial(forward_kernel, n_ctx, 256),
        out_shape=[
            jax.ShapeDtypeStruct((4, length, cols), BF),
            jax.ShapeDtypeStruct((length, 1), F32),
            jax.ShapeDtypeStruct((length, cols), BF),
            jax.ShapeDtypeStruct((length, 128), F32),
        ],
        in_specs=in_smem(2) + in_vmem(3),
        out_specs=in_vmem(4),
        scratch_shapes=[pltpu.VMEM((length, cols), F32)],
        compiler_params=params(VMEM_LIMIT),
        cost_estimate=LIGHT,
        name="attention_forward",
    )(pair, me, tokens, weight, turn)


def backward_kernel(
    n_ctx, qblk, pair_ref, me_ref, do_ref, kept_ref, r_ref, lse_ref, turn_ref,
    g_ref, gr_ref, go_ref, dq_ref, dk_ref, dv_ref, centre_ref,
):
    q_ref, k_ref, v_ref, o_ref = (kept_ref.at[i] for i in range(4))
    cos_ref, sin_ref = turn_ref.at[0], turn_ref.at[1]
    length, cols = q_ref.shape
    blk = length // (2 * n_ctx)
    heads = cols // HEAD_DIM
    for slot in range(2 * n_ctx):
        at = pl.multiple_of(slot_block(pair_ref, me_ref, slot, n_ctx) * blk, blk)
        go_ref[pl.ds(at, blk), :] = do_ref[pl.ds(slot * blk, blk), :]
    dq_ref[...] = jnp.zeros_like(dq_ref)
    dk_ref[...] = jnp.zeros_like(dk_ref)
    dv_ref[...] = jnp.zeros_like(dv_ref)

    pick = head_mask((8, cols), lax.broadcasted_iota(jnp.int32, (8, cols), 0)).astype(F32)
    centre_ref[...] = lax.dot_general(
        pick,
        go_ref[...].astype(F32) * o_ref[...].astype(F32),
        (((1,), (1,)), ((), ())),
        precision=lax.Precision.HIGHEST,
        preferred_element_type=F32,
    )

    def one_head(head, carry):
        mask = head_mask((qblk, cols), head)
        below = lax.broadcasted_iota(jnp.int32, (qblk, qblk), 0) <= lax.broadcasted_iota(jnp.int32, (qblk, qblk), 1)
        for i in range(length // qblk):
            rows = pl.ds(i * qblk, qblk)
            query = jnp.where(mask, q_ref[rows, :], jnp.zeros((), BF))
            grad = jnp.where(mask, go_ref[rows, :], jnp.zeros((), BF))
            lse = lse_ref[pl.ds(head, 1), rows]
            centre = centre_ref[pl.ds(head, 1), rows]
            out = None
            for at, size in ((i * qblk, qblk), (0, i * qblk)):
                if not size:
                    continue
                keys = pl.ds(at, size)
                probs = jnp.exp(mm_t(k_ref[keys, :], query) * SCALE - lse)
                if at or not i:
                    probs = jnp.where(below, probs, 0.0)
                grad_probs = mm_t(v_ref[keys, :], grad)
                grad_scores = (probs * (grad_probs - centre)).astype(BF)
                dk_ref[keys, :] += mm(grad_scores, query)
                dv_ref[keys, :] += mm(probs.astype(BF), grad)
                term = t_mm(grad_scores, k_ref[keys, :])
                out = term if out is None else out + term
            dq_ref[rows, :] = jnp.where(mask, out, dq_ref[rows, :])
        return carry

    lax.fori_loop(0, heads, one_head, 0)
    for slot in range(2 * n_ctx):
        at = pl.multiple_of(slot_block(pair_ref, me_ref, slot, n_ctx) * blk, blk)
        rows = pl.ds(slot * blk, blk)
        to = pl.ds(at, blk)
        cosine, sine = cos_ref[to, :], sin_ref[to, :]
        scale = r_ref[rows, :]
        query = (dq_ref[to, :] * SCALE).astype(BF).astype(F32)
        key = (dk_ref[to, :] * SCALE).astype(BF).astype(F32)
        value = dv_ref[to, :].astype(BF).astype(F32)
        query = query * cosine - swap_halves(query) * sine
        key = key * cosine - swap_halves(key) * sine
        for at_col, part in enumerate((query, key, value)):
            span = pl.ds(at_col * cols, cols)
            g_ref[rows, span] = part.astype(BF)
            gr_ref[rows, span] = (part * scale).astype(BF)


def attention_backward(pair, me, n_ctx, grad, kept, scale, lse, turn):
    _, length, cols = turn.shape
    return pl.pallas_call(
        functools.partial(backward_kernel, n_ctx, 256),
        out_shape=[jax.ShapeDtypeStruct((length, 3 * cols), BF)] * 2,
        in_specs=in_smem(2) + in_vmem(5),
        out_specs=in_vmem(2),
        scratch_shapes=[pltpu.VMEM((length, cols), BF)]
        + [pltpu.VMEM((length, cols), F32)] * 3
        + [pltpu.VMEM((8, length), F32)],
        compiler_params=params(),
        cost_estimate=LIGHT,
        name="attention_backward",
    )(pair, me, grad, kept, scale, lse, turn)


def feed_forward_kernel(
    core_ref, n_ref, c_ref, g_ref, u_ref, d_ref, h_ref, dg_ref, du_ref, theirs_ref, mine_ref
):
    rows, cot = n_ref[...], c_ref[...]
    hid, tile = g_ref.shape[1], 256
    for at in range(0, hid, tile):
        span = slice(at, at + tile)
        gate = mm(rows, g_ref[:, span])
        up = mm(rows, u_ref[:, span])
        grad = mm_t(cot, d_ref[span, :])
        sig = 1.0 / (1.0 + jnp.exp(-gate))
        active = gate * sig
        h_ref[:, span] = (active * up).astype(BF)
        dg_ref[:, span] = (grad * up * sig * (1.0 + gate * (1.0 - sig))).astype(BF)
        du_ref[:, span] = (grad * active).astype(BF)
    back = (mm_t(dg_ref[...], g_ref[...]) + mm_t(du_ref[...], u_ref[...])).astype(BF)
    first = pl.program_id(0) < pl.num_programs(0) // 2

    @pl.when(first)
    def _():
        theirs_ref[...] = back

    @pl.when(jnp.logical_not(first))
    def _():
        mine_ref[...] = back


def feed_forward(normed, cotangent, gate_w, up_w, down_w):
    count, width = normed.shape
    hid = gate_w.shape[1]
    tile = 256
    half = count // tile // 2

    def rows_of(r, core):
        return (jnp.where(r < half, (1 - core[0]) * half + r, core[0] * half + r - half), 0)

    def fixed(r, core):
        return (0, 0)

    once = pl.Buffered(1)
    return pl.pallas_call(
        feed_forward_kernel,
        grid_spec=pltpu.PrefetchScalarGridSpec(
            num_scalar_prefetch=1,
            grid=(2 * half,),
            in_specs=[
                pl.BlockSpec((tile, width), rows_of),
                pl.BlockSpec((tile, width), rows_of),
                pl.BlockSpec((width, hid), fixed, pipeline_mode=once),
                pl.BlockSpec((width, hid), fixed, pipeline_mode=once),
                pl.BlockSpec((hid, width), fixed, pipeline_mode=once),
            ],
            out_specs=[pl.BlockSpec((tile, hid), rows_of)] * 3
            + [
                pl.BlockSpec((tile, width), lambda r, core: (jnp.minimum(r, half - 1), 0)),
                pl.BlockSpec((tile, width), lambda r, core: (jnp.maximum(r - half, 0), 0)),
            ],
        ),
        out_shape=[jax.ShapeDtypeStruct((count, hid), BF)] * 3
        + [jax.ShapeDtypeStruct((count // 2, width), BF)] * 2,
        compiler_params=params(VMEM_LIMIT),
        cost_estimate=LIGHT,
        name="feed_forward",
    )(lax.axis_index("core").astype(jnp.int32)[None], normed, cotangent, gate_w, up_w, down_w)


def branch_kernel(core_ref, h_ref, d_ref, theirs_ref, mine_ref):
    out = mm(h_ref[...], d_ref[...]).astype(BF)
    first = pl.program_id(0) < pl.num_programs(0) // 2

    @pl.when(first)
    def _():
        theirs_ref[...] = out

    @pl.when(jnp.logical_not(first))
    def _():
        mine_ref[...] = out


def branch_rows(hidden, down_w):
    count, hid = hidden.shape
    width = down_w.shape[1]
    tile = 256
    half = count // tile // 2
    return pl.pallas_call(
        branch_kernel,
        grid_spec=pltpu.PrefetchScalarGridSpec(
            num_scalar_prefetch=1,
            grid=(2 * half,),
            in_specs=[
                pl.BlockSpec(
                    (tile, hid),
                    lambda r, core: (jnp.where(r < half, (1 - core[0]) * half + r, core[0] * half + r - half), 0),
                ),
                pl.BlockSpec((hid, width), lambda r, core: (0, 0), pipeline_mode=pl.Buffered(1)),
            ],
            out_specs=[
                pl.BlockSpec((tile, width), lambda r, core: (jnp.minimum(r, half - 1), 0)),
                pl.BlockSpec((tile, width), lambda r, core: (jnp.maximum(r - half, 0), 0)),
            ],
        ),
        out_shape=[jax.ShapeDtypeStruct((count // 2, width), BF)] * 2,
        compiler_params=params(),
        cost_estimate=LIGHT,
        name="branch_rows",
    )(lax.axis_index("core").astype(jnp.int32)[None], hidden, down_w)


def merge_kernel(a_ref, m_ref, *refs):
    *b_refs, go_ref, out_ref, all_ref = refs
    rows = b_refs[0].shape[0]
    for at, ref in enumerate(b_refs):
        all_ref[pl.ds(at * rows, rows), :] = ref[...]
    go_ref[...] = mm_t(all_ref[...], m_ref[...]).astype(BF)
    out_ref[...] = t_mm(a_ref[...], all_ref[...]).astype(BF)


def merge_terms(attended, merge_rows, pieces):
    length, cols = attended.shape
    width = merge_rows.shape[1]
    return pl.pallas_call(
        merge_kernel,
        out_shape=[jax.ShapeDtypeStruct((length, cols), BF), jax.ShapeDtypeStruct((cols, width), BF)],
        in_specs=in_vmem(2 + len(pieces)),
        out_specs=in_vmem(2),
        scratch_shapes=[pltpu.VMEM((length, width), BF)],
        compiler_params=params(),
        cost_estimate=LIGHT,
        name="merge_terms",
    )(attended, merge_rows, *pieces)


def heads_term_kernel(x_ref, g_ref, out_ref):
    out_ref[...] = mm(x_ref[...], g_ref[...]).astype(BF)


def heads_term(tokens_t, grad):
    width, count = tokens_t.shape
    cols = grad.shape[1]
    tile = 512
    return pl.pallas_call(
        heads_term_kernel,
        grid=(width // tile,),
        in_specs=[
            pl.BlockSpec((tile, count), lambda i: (i, 0)),
            pl.BlockSpec((count, cols), lambda i: (0, 0), pipeline_mode=pl.Buffered(1)),
        ],
        out_specs=pl.BlockSpec((tile, cols), lambda i: (i, 0)),
        out_shape=jax.ShapeDtypeStruct((width, cols), BF),
        compiler_params=params(),
        cost_estimate=LIGHT,
        name="heads_term",
    )(tokens_t, grad)


def weight_rows_kernel(at_ref, left_ref, right_ref, *out_refs):
    out = t_mm(left_ref[...], right_ref[...]).astype(BF)
    for i, ref in enumerate(out_refs):

        @pl.when(pl.program_id(0) == i)
        def _(ref=ref):
            ref[...] = out


def weight_rows(left, right, index, size):
    count, n = left.shape[0], len(index)
    width = right.shape[1]
    return pl.pallas_call(
        weight_rows_kernel,
        grid_spec=pltpu.PrefetchScalarGridSpec(
            num_scalar_prefetch=1,
            grid=(n,),
            in_specs=[
                pl.BlockSpec((count, size), lambda i, at: (0, at[i])),
                pl.BlockSpec((count, width), lambda i, at: (0, 0), pipeline_mode=pl.Buffered(1)),
            ],
            out_specs=[pl.BlockSpec((size, width), lambda i, at: (0, 0), pipeline_mode=pl.Buffered(1))] * n,
        ),
        out_shape=[jax.ShapeDtypeStruct((size, width), BF)] * n,
        compiler_params=params(),
        cost_estimate=LIGHT,
        name="weight_rows",
    )(jnp.stack(index).astype(jnp.int32), left, right)


def back_kernel(g_ref, w_ref, out_ref):
    out_ref[...] = mm_t(g_ref[...], w_ref[...]).astype(BF)


def back_rows(grad, weight, half):
    count, cols = grad.shape
    width = weight.shape[0]
    tile = 256
    steps = count // 2 // tile
    return pl.pallas_call(
        back_kernel,
        grid=(steps,),
        in_specs=[
            pl.BlockSpec((tile, cols), lambda r: (half * steps + r, 0)),
            pl.BlockSpec((width, cols), lambda r: (0, 0), pipeline_mode=pl.Buffered(1)),
        ],
        out_specs=pl.BlockSpec((tile, width), lambda r: (r, 0)),
        out_shape=jax.ShapeDtypeStruct((count // 2, width), BF),
        compiler_params=params(),
        cost_estimate=LIGHT,
        name="back_rows",
    )(grad, weight)


def fold_heads_kernel(q_ref, k_ref, v_ref, gain_ref, out_ref):
    n_ctx, _, cols = out_ref.shape
    cols //= 3
    gain = gain_ref[...]
    for at, ref in enumerate((q_ref, k_ref, v_ref)):
        for to in range(n_ctx):
            part = ref[:, to * cols : (to + 1) * cols].astype(F32) * gain
            out_ref[to, :, at * cols : (at + 1) * cols] = part.astype(BF)


def fold_heads(weights, gain, n_ctx):
    rows, width = weights[0].shape
    return pl.pallas_call(
        fold_heads_kernel,
        out_shape=jax.ShapeDtypeStruct((n_ctx, rows, 3 * (width // n_ctx)), BF),
        in_specs=in_vmem(4),
        out_specs=pl.BlockSpec(memory_space=pltpu.VMEM),
        compiler_params=params(),
        cost_estimate=LIGHT,
        name="fold_heads",
    )(*weights, gain)


def unfold_heads_kernel(s_ref, q_ref, k_ref, v_ref, gain_ref, dq_ref, dk_ref, dv_ref, first_ref):
    n_ctx, rows, cols = s_ref.shape
    cols //= 3
    gain = gain_ref[...]
    total = jnp.zeros((rows, cols), F32)
    for at, (ref, out) in enumerate(((q_ref, dq_ref), (k_ref, dk_ref), (v_ref, dv_ref))):
        for to in range(n_ctx):
            span = slice(to * cols, (to + 1) * cols)
            part = s_ref[to, :, at * cols : (at + 1) * cols].astype(F32)
            total += part * ref[:, span].astype(F32)
            out[:, span] = part * gain
    first_ref[...] = jnp.sum(total, axis=1, keepdims=True)


def unfold_heads(sums, weights, gain):
    rows, width = weights[0].shape
    return pl.pallas_call(
        unfold_heads_kernel,
        out_shape=[jax.ShapeDtypeStruct((rows, width), F32)] * 3 + [jax.ShapeDtypeStruct((rows, 1), F32)],
        in_specs=in_vmem(5),
        out_specs=in_vmem(4),
        compiler_params=params(),
        cost_estimate=LIGHT,
        name="unfold_heads",
    )(sums, *weights, gain)


def fold_hidden_kernel(piece, w_ref, gain_ref, out_ref):
    n_core, n_fsdp, _, hid = out_ref.shape
    gain = gain_ref[...]
    for plane in range(hid // piece):
        for core in range(n_core):
            for line in range(n_fsdp):
                at = ((plane * n_core + core) * n_fsdp + line) * piece
                part = w_ref[:, at : at + piece].astype(F32) * gain
                out_ref[core, line, :, plane * piece : (plane + 1) * piece] = part.astype(BF)


def fold_hidden(weight, gain, n_plane, n_core, n_fsdp):
    rows, total = weight.shape
    piece = total // (n_plane * n_core * n_fsdp)
    if piece % 128:
        folded = (weight.astype(F32) * gain).astype(BF).reshape(rows, n_plane, n_core, n_fsdp, piece)
        return folded.transpose(2, 3, 0, 1, 4).reshape(n_core, n_fsdp, rows, n_plane * piece)
    return pl.pallas_call(
        functools.partial(fold_hidden_kernel, piece),
        out_shape=jax.ShapeDtypeStruct((n_core, n_fsdp, rows, n_plane * piece), BF),
        in_specs=in_vmem(2),
        out_specs=pl.BlockSpec(memory_space=pltpu.VMEM),
        compiler_params=params(),
        cost_estimate=LIGHT,
        name="fold_hidden",
    )(weight, gain)


def unfold_hidden_kernel(piece, at_ref, *refs):
    *s_refs, w_ref, gain_ref, out_ref, second_ref = refs
    n_fsdp = len(s_refs)
    n_core, rows, hid = s_refs[0].shape
    gain = gain_ref[...]
    total = jnp.zeros((rows, piece), F32)
    for mask, ref in enumerate(s_refs):
        line = jnp.bitwise_xor(at_ref[1], mask)
        for other in range(n_core):
            core = jnp.bitwise_xor(at_ref[0], other)
            for plane in range(hid // piece):
                at = ((plane * n_core + core) * n_fsdp + line) * piece
                span = pl.ds(pl.multiple_of(at, piece), piece)
                part = ref[other, :, plane * piece : (plane + 1) * piece].astype(F32)
                total += part * w_ref[:, span].astype(F32)
                out_ref[:, span] = part * gain
    second_ref[...] = jnp.sum(total, axis=1, keepdims=True)


def unfold_hidden(pieces, weight, gain, n_plane):
    rows, total = weight.shape
    n_core, _, hid = pieces[0].shape
    n_fsdp = len(pieces)
    piece = hid // n_plane
    core, line = lax.axis_index("core"), lax.axis_index("fsdp")
    if piece % 128:
        out = jnp.zeros((rows, n_plane, n_core, n_fsdp, piece), BF)
        for mask, block in enumerate(pieces):
            for other in range(n_core):
                part = block[other].reshape(rows, n_plane, 1, 1, piece)
                out = lax.dynamic_update_slice(out, part, (0, 0, core ^ other, line ^ mask, 0))
        out = out.reshape(rows, total).astype(F32)
        return out * gain, jnp.sum(out * weight.astype(F32), axis=1, keepdims=True)
    return pl.pallas_call(
        functools.partial(unfold_hidden_kernel, piece),
        out_shape=[jax.ShapeDtypeStruct((rows, total), F32), jax.ShapeDtypeStruct((rows, 1), F32)],
        in_specs=in_smem(1) + in_vmem(n_fsdp + 2),
        out_specs=in_vmem(2),
        compiler_params=params(),
        cost_estimate=LIGHT,
        name="unfold_hidden",
    )(jnp.stack([core, line]).astype(jnp.int32), *pieces, weight, gain)


def place_kernel(at_ref, *refs):
    *p_refs, out_ref = refs
    for i, ref in enumerate(p_refs):
        out_ref[at_ref[i]] = ref[...]


def place(pieces, index, room=None):
    n = len(pieces)
    moved = 2 * n * pieces[0].size * pieces[0].dtype.itemsize
    return pl.pallas_call(
        place_kernel,
        out_shape=jax.ShapeDtypeStruct((room or n,) + pieces[0].shape, pieces[0].dtype),
        in_specs=in_smem(1) + in_vmem(n),
        out_specs=pl.BlockSpec(memory_space=pltpu.VMEM),
        compiler_params=params(VMEM_LIMIT),
        cost_estimate=LIGHT,
        name="place",
    )(jnp.stack(index).astype(jnp.int32), *pieces)


def gather(value, axes, axis=0):
    return lax.all_gather(value, axes, axis=axis, tiled=True)


def scatter(value, axes):
    return lax.psum_scatter(value, axes, scatter_dimension=0, tiled=True)


def exchange(value, axes):
    return lax.all_to_all(value, axes, split_axis=0, concat_axis=0, tiled=True)


def together(values):
    return lax.optimization_barrier(values)


def core_swap(value):
    n = lax.axis_size("plane") * 2
    return lax.ppermute(value, CTX, [(i, i ^ 1) for i in range(n)])


def plane_step(value, step):
    steps, _ = relative(lax.axis_size("plane"))
    n = lax.axis_size("plane") * 2
    return lax.ppermute(value, CTX, [(i, i ^ (2 * steps[i % 2][step])) for i in range(n)])


def line_swap(value, mask):
    n = lax.axis_size("fsdp")
    return lax.ppermute(value, "fsdp", [(i, i ^ mask) for i in range(n)])


def plane_gather_more(pieces):
    step = len(pieces).bit_length() - 1
    return pieces + [plane_step(piece, step) for piece in pieces]


def plane_gather(value):
    pieces = [value]
    while len(pieces) < lax.axis_size("plane"):
        pieces = plane_gather_more(pieces)
    return pieces


def plane_send(chunks):
    n = len(chunks) // 2
    return [plane_step(chunk, n.bit_length() - 1) for chunk in chunks[n:]]


def plane_add(chunks, came):
    return [(mine.astype(F32) + chunk.astype(F32)).astype(BF) for mine, chunk in zip(chunks, came)]


def plane_scatter(chunks):
    while len(chunks) > 1:
        chunks = plane_add(chunks, plane_send(chunks))
    return chunks[0]


def plane_index():
    _, order = relative(lax.axis_size("plane"))
    core = lax.axis_index("core")
    plane = lax.axis_index("plane")
    return [plane ^ jnp.where(core == 0, a, b) for a, b in zip(*order)]


def part(value, at, size, axis):
    return lax.dynamic_slice_in_dim(value, at * size, size, axis)


def ctx_gather(value):
    mine = plane_gather(value)
    return mine + [core_swap(piece) for piece in mine]


def ctx_scatter(theirs, mine, n_plane):
    total = (mine.astype(F32) + core_swap(theirs).astype(F32)).astype(BF)
    rows = total.shape[0] // n_plane
    return plane_scatter([total[i * rows : (i + 1) * rows] for i in range(n_plane)])


def cores_pair(value):
    core = lax.axis_index("core")
    kept = lax.dynamic_index_in_dim(value, core, 0, keepdims=False)
    return kept, core_swap(lax.dynamic_index_in_dim(value, 1 - core, 0, keepdims=False))


def lines_parts(pair):
    line = lax.axis_index("fsdp")
    return [
        jnp.stack([lax.dynamic_index_in_dim(v, line ^ mask, 0, keepdims=False) for v in pair])
        for mask in range(lax.axis_size("fsdp"))
    ]


def lines_swap(parts):
    return parts[:1] + [line_swap(parts[mask], mask) for mask in range(1, len(parts))]


def lines_pair(pair):
    return lines_swap(lines_parts(pair))


def line_rows_kernel(at_ref, *refs):
    *p_refs, out_ref = refs
    n_fsdp = len(p_refs)
    for mask, ref in enumerate(p_refs):
        line = jnp.bitwise_xor(at_ref[1], mask)
        for other in range(2):
            core = jnp.bitwise_xor(at_ref[0], other)
            out_ref[core * n_fsdp + line] = ref[other]


def line_rows(pieces):
    n = 2 * len(pieces)
    at = jnp.stack([lax.axis_index("core"), lax.axis_index("fsdp")]).astype(jnp.int32)
    return pl.pallas_call(
        line_rows_kernel,
        out_shape=jax.ShapeDtypeStruct((n,) + pieces[0].shape[1:], pieces[0].dtype),
        in_specs=in_smem(1) + in_vmem(len(pieces)),
        out_specs=pl.BlockSpec(memory_space=pltpu.VMEM),
        compiler_params=params(VMEM_LIMIT),
        cost_estimate=LIGHT,
        name="line_rows",
    )(at, *pieces)


def on_device(
    layer_input, pairing, query_weight, key_weight, value_weight, merge_weight,
    gate_weight, up_weight, down_weight, norm_first, norm_second, output_cotangent,
):
    n_plane = lax.axis_size("plane")
    n_core = lax.axis_size("core")
    n_fsdp = lax.axis_size("fsdp")
    n_ctx = n_plane * n_core
    n_tok = n_core * n_fsdp
    me = jnp.stack([lax.axis_index("plane"), lax.axis_index("core")]).astype(jnp.int32)
    index = plane_index()
    _, rows, width = layer_input.shape
    length = rows * n_ctx
    half = length // 2
    cols = width // n_ctx
    dev_rows = gate_weight.shape[0]
    piece = gate_weight.shape[1] // (n_ctx * n_fsdp)
    hid = piece * n_plane
    d_rows = n_tok * dev_rows
    tokens = layer_input.reshape(rows, width)
    cotangent = output_cotangent.reshape(rows, width)
    gain_first = norm_first.astype(F32)[:, None]
    gain_second = norm_second.astype(F32)[:, None]
    projections = (query_weight, key_weight, value_weight)

    merge_rows = gather(merge_weight, "fsdp")
    gate_moved = lines_pair(cores_pair(fold_hidden(gate_weight, gain_second, n_plane, n_core, n_fsdp)))
    own = exchange(fold_heads(projections, gain_first, n_ctx), CTX)
    x_pieces = ctx_gather(tokens)
    up_pair = cores_pair(fold_hidden(up_weight, gain_second, n_plane, n_core, n_fsdp))
    turn = jnp.stack(rope_tables(length, cols))
    own, gate_moved[3:], x_pieces, up_pair, merge_rows = together(
        (own, gate_moved[3:], x_pieces, up_pair, merge_rows)
    )
    qkv_weight = gather(own[:, None], "fsdp", axis=1).reshape(width, 3 * cols)
    gate_pieces = plane_gather(line_rows(gate_moved).reshape(d_rows, hid))
    down_pieces = plane_gather_more([down_weight])
    x_all = jnp.concatenate(x_pieces, axis=0)
    x_all, gate_pieces[:3] = together((x_all, gate_pieces[:3]))
    up_moved = lines_pair(up_pair)
    cot_all = gather(cotangent, TOK)

    kept, scale_all, attended, lse = attention_forward(pairing, me, x_all, qkv_weight, turn)
    while len(down_pieces) < n_plane:
        down_pieces = plane_gather_more(down_pieces)
    attended, down_pieces, gate_pieces = together((attended, down_pieces, gate_pieces))
    down_rows = place(down_pieces, index).reshape(hid, width)
    own_f = tokens.astype(F32)
    theirs = together(mm(attended[half:], merge_rows).astype(BF))
    mine = together(mm(attended[:half], merge_rows).astype(BF))
    mixed = own_f + ctx_scatter(theirs, mine, n_plane)
    lse_rows = lse[:, :8].T
    gate_rows = place(gate_pieces, index).reshape(width, hid)
    mixed, up_moved, lse_rows = together((mixed, up_moved, lse_rows))
    up_pieces = plane_gather_more([line_rows(up_moved).reshape(d_rows, hid)])
    gate_rows, down_rows, up_pieces = together((gate_rows, down_rows, up_pieces))
    while len(up_pieces) < n_plane:
        up_pieces = plane_gather_more(up_pieces)
    up_rows = place(up_pieces[:-1], index[:-1], n_plane)
    up_rows = lax.dynamic_update_slice(up_rows, up_pieces[-1][None], (index[-1], 0, 0)).reshape(width, hid)

    scale_second = lax.rsqrt(jnp.mean(mixed * mixed, axis=-1, keepdims=True) + EPS)
    unit_second = mixed * scale_second
    normed_all = gather(unit_second.astype(BF), TOK)
    hidden, grad_gate, grad_up, theirs, mine = feed_forward(
        normed_all, cot_all, gate_rows, up_rows, down_rows
    )
    theirs = core_swap(theirs)
    gate_late = weight_rows(normed_all, grad_gate, index[n_plane // 2 :], d_rows)
    theirs, gate_late = together((theirs, gate_late))
    e_two = (mine.astype(F32) + theirs.astype(F32)).astype(BF)

    hidden, grad_gate, grad_up, e_two = together((hidden, grad_gate, grad_up, e_two))
    gate_chunks = list(weight_rows(normed_all, grad_gate, index[: n_plane // 2], d_rows)) + list(gate_late)
    gate_came = plane_send(gate_chunks)
    up_chunks = [together(t_mm(part(normed_all, at, d_rows, 1), grad_up).astype(BF)) for at in index]
    theirs, mine = branch_rows(hidden, down_rows)
    gate_chunks, gate_came, up_chunks, theirs, mine = together(
        (gate_chunks, gate_came, up_chunks, theirs, mine)
    )
    gate_chunks = plane_add(gate_chunks, gate_came)
    branch = (mine.astype(F32) + core_swap(theirs).astype(F32)).astype(BF)
    e_two = scatter(e_two, "fsdp")
    gate_sum = plane_scatter(gate_chunks)
    e_two, gate_sum, up_chunks, branch = together((e_two, gate_sum, up_chunks, branch))
    branch_sum = scatter(branch, "fsdp")
    e_two_f = e_two.astype(F32)
    grad_mixed = cotangent.astype(F32) + scale_second * (
        e_two_f - unit_second * jnp.mean(e_two_f * unit_second, axis=-1, keepdims=True)
    )
    branch_pieces = plane_gather_more([grad_mixed.astype(BF)])
    x_t = x_all.reshape(length, n_ctx, n_fsdp, dev_rows).transpose(2, 1, 3, 0).reshape(width, length)
    branch_pieces, gate_sum, x_t = together((branch_pieces, gate_sum, x_t))
    gate_parts = lines_parts(cores_pair(gate_sum.reshape(n_core, n_fsdp, dev_rows, hid)))
    while len(branch_pieces) < n_plane:
        branch_pieces = plane_gather_more(branch_pieces)
    branch_pieces = branch_pieces + [core_swap(value) for value in branch_pieces]
    gate_back = lines_swap(gate_parts)

    branch_pieces, up_chunks = together((branch_pieces, up_chunks))
    up_came = plane_send(up_chunks)
    grad_attended, merge_grad = merge_terms(attended, merge_rows, branch_pieces)
    merge_grad, grad_attended = together((merge_grad, grad_attended))
    merge_grad = scatter(merge_grad, "fsdp")
    grad_qkv, grad_scaled = attention_backward(
        pairing, me, n_ctx, grad_attended, kept, scale_all, lse_rows, turn
    )
    grad_scaled, branch_sum = together((grad_scaled, branch_sum))
    sums = heads_term(x_t, grad_scaled)
    grad_qkv, up_chunks, up_came, gate_back, sums, merge_grad, branch_sum = together(
        (grad_qkv, up_chunks, up_came, gate_back, sums, merge_grad, branch_sum)
    )
    sums = scatter(sums, "fsdp")
    up_sum = plane_scatter(plane_add(up_chunks, up_came))
    layer_output = (mixed + branch_sum.astype(F32)).astype(BF)
    theirs = back_rows(grad_qkv, qkv_weight, 1)
    mine = back_rows(grad_qkv, qkv_weight, 0)
    e_one = ctx_scatter(theirs, mine, n_plane)
    up_parts = lines_parts(cores_pair(up_sum.reshape(n_core, n_fsdp, dev_rows, hid)))
    hidden, mine = together((hidden, mine))
    down_chunks = [together(t_mm(part(hidden, at, piece, 1), cot_all).astype(BF)) for at in index]
    e_one, down_chunks = together((e_one, down_chunks))
    down_came = plane_send(down_chunks)
    sums, up_parts, merge_grad = together((sums, up_parts, merge_grad.astype(F32)))
    up_back = lines_swap(up_parts)
    sums = exchange(sums.reshape(n_ctx, dev_rows, 3 * cols), CTX)
    query_grad, key_grad, value_grad, first_grad = unfold_heads(sums, projections, gain_first)
    query_grad, key_grad, value_grad, first_grad, up_back = together(
        (query_grad, key_grad, value_grad, first_grad, up_back)
    )
    scale_first = lax.rsqrt(jnp.mean(own_f * own_f, axis=-1, keepdims=True) + EPS)
    unit_first = own_f * scale_first
    input_grad = (
        grad_mixed
        + scale_first * (e_one - unit_first * jnp.mean(e_one * unit_first, axis=-1, keepdims=True))
    ).astype(BF)
    down_grad = plane_scatter(plane_add(down_chunks, down_came)).astype(F32)
    gate_grad, second_gate = unfold_hidden(gate_back, gate_weight, gain_second, n_plane)
    up_grad, second_up = unfold_hidden(up_back, up_weight, gain_second, n_plane)
    second_grad = (second_gate + second_up)[:, 0]
    return (
        layer_output.reshape(1, rows, width),
        input_grad.reshape(1, rows, width),
        query_grad,
        key_grad,
        value_grad,
        merge_grad,
        gate_grad,
        up_grad,
        down_grad,
        first_grad[:, 0],
        second_grad,
    )


def solution(mesh):
    n_ctx, n_fsdp = mesh.shape["ctx"], mesh.shape["fsdp"]
    inner = Mesh(mesh.devices.reshape(n_ctx // 2, 2, n_fsdp), ("plane", "core", "fsdp"))
    token = P("fsdp", CTX, None)
    weight = P(("plane", "core", "fsdp"), None)
    gain = P(("plane", "core", "fsdp"))
    return jax.shard_map(
        on_device,
        mesh=inner,
        in_specs=(token, P("fsdp", None)) + (weight,) * 7 + (gain, gain, token),
        out_specs=(token, token) + (weight,) * 7 + (gain, gain),
        check_vma=False,
    )
```
